256 devices in a mesh: section: 4 (over z_hi), mp: 8 (over z_lo, y), seq: 8 (over x, core).
Axes of the slice: x: 4, y: 4, z: 8 (z_hi: 4, z_lo: 2; z = z_hi * 2 + z_lo), core: 2. Of those that a mesh axis runs over, the one named last changes fastest.
Arguments:
- prompt_queries: bfloat16 [4, 2, 1024, 8192], P('section', None, 'seq', 'mp'), may hold values from -8 to 8
- prompt_pairs: bfloat16 [4, 2, 1024, 2, 1024], P('section', None, 'seq', None, 'mp'), may hold values from -10 to 10
- decode_queries: bfloat16 [4, 128, 4, 8192], P('section', None, None, 'mp'), may hold values from -8 to 8
- decode_pairs: bfloat16 [4, 128, 4, 2, 1024], P('section', None, None, None, 'mp'), may hold values from -10 to 10
- cache_pool: bfloat16 [4, 384, 128, 2, 1024], P('section', 'seq', None, None, 'mp'), may hold values from -10 to 10
- out_weight: bfloat16 [4, 8192, 8192], P('section', 'mp', 'seq'), may hold values from -0.0625 to 0.0625
- slot_pages: int32 [384], P('seq'), may hold values from -1 to 131071, as said below
- placement: int32 [16], replicated, may hold values from 0 to 383, as said below
- context_len: int32 [128], replicated, may hold values from 2 to 2048, as said below
Outputs:
- prefill_out: bfloat16 [4, 2, 1024, 8192], P('section', None, 'seq', 'mp')
- decode_mix: bfloat16 [4, 128, 4, 8192], P('section', 'mp', None, 'seq')
The draws below stay inside these ranges and needn't reach their ends.
Inputs may be any that keep to these rules, and one draw needn't show every extreme that they name: placement[p] = owner * 48 + slot; all entries differ and name slots that slot_pages marks free. The 2 pages whose positions lie in one index of seq's part of the prompt blocks both go to one owner; several indices of seq may send to the same owner. `slot_pages`: -1 marks a free slot; any other entry is r * 1024 + k with 1 <= r < 128: the slot holds page k of decode row r. Every row r >= 1 has its pages 0 to n_r - 1 each in one slot, n_r >= 1. Row 0 is the prefilled request: context_len[0] = 2048 and its pages are those of placement. For r >= 1, (n_r - 1) * 128 + 2 <= context_len[r] <= n_r * 128.
All inputs are finite; a program needn't handle non-finite values.
Results may differ from the reference program's by a relative error of at most 0.024.
Values may be sent and summed in bfloat16 or wider, within the bound.
A program may use at most 128 MiB of HBM per device.

```python
import math
import jax
import jax.numpy as jnp
from jax import lax

D = 8192
QUERY_HEADS = 64
KEY_HEADS = 8
HEAD_SIZE = 128
PAGE_TOKENS = 128
MAXP = 1024
DECODE_STEPS = 4
PROMPT_BLOCKS = 2
BTOK_DEV = 128
DECODE_ROWS = 128
POOL_DEV = 48
LAYER_COUNT = 4
BLOCK_TOKENS = 1024
GROUP_SLOTS = 384
PROMPT_PAGES = 16
CAP = 2


def page_layout(key):
    seq_count = GROUP_SLOTS // POOL_DEV
    block_pages = BTOK_DEV // PAGE_TOKENS
    device_pages = PROMPT_BLOCKS * block_pages
    subkeys = jax.random.split(jax.random.fold_in(key, 4242), 7)
    offsets = jax.random.randint(subkeys[0], (seq_count,), 0, seq_count)
    offsets = offsets.at[0].set(seq_count - 1)
    orders = jax.vmap(lambda subkey: jax.random.permutation(subkey, device_pages))(jax.random.split(subkeys[1], seq_count))
    owner_source = (offsets[:, None] + orders // CAP) % seq_count
    owner_fresh = jnp.transpose(owner_source.reshape(seq_count, PROMPT_BLOCKS, block_pages), (1, 0, 2)).reshape(PROMPT_PAGES)
    fresh_ids = jnp.arange(PROMPT_PAGES, dtype=jnp.int32)
    arrival = jnp.sum((fresh_ids[None, :] < fresh_ids[:, None]) & (owner_fresh[None, :] == owner_fresh[:, None]), axis=1)
    lower_orders = jax.vmap(lambda subkey: jax.random.permutation(subkey, POOL_DEV - 1))(jax.random.split(subkeys[2], seq_count))
    slot_orders = jnp.concatenate([jnp.full((seq_count, 1), POOL_DEV - 1, jnp.int32), lower_orders.astype(jnp.int32)], axis=1)
    placement_list = owner_fresh * POOL_DEV + slot_orders[owner_fresh, arrival]
    taken_mask = jnp.zeros((GROUP_SLOTS,), jnp.int32).at[placement_list].set(1)
    ranking = jax.random.permutation(subkeys[3], GROUP_SLOTS) + GROUP_SLOTS * taken_mask
    order_slots = jnp.argsort(ranking)
    index_line = jnp.arange(GROUP_SLOTS, dtype=jnp.int32)
    position_of = jnp.zeros((GROUP_SLOTS,), jnp.int32).at[order_slots].set(index_line)
    spare_slots = (GROUP_SLOTS - PROMPT_PAGES) // 16
    used_slots = GROUP_SLOTS - PROMPT_PAGES - spare_slots
    skewed = 1 + jnp.minimum(jax.random.randint(subkeys[4], (GROUP_SLOTS,), 0, DECODE_ROWS - 1), jax.random.randint(subkeys[5], (GROUP_SLOTS,), 0, DECODE_ROWS - 1))
    row_at = jnp.where(index_line < DECODE_ROWS - 1, index_line + 1, skewed)
    first_live = index_line < used_slots
    page_at = jnp.sum((index_line[None, :] < index_line[:, None]) & (row_at[None, :] == row_at[:, None]) & first_live[None, :], axis=1)
    live_at = first_live & (page_at < PROMPT_PAGES - 1)
    row_ids = jnp.arange(DECODE_ROWS, dtype=jnp.int32)
    page_counts = jnp.sum((row_at[None, :] == row_ids[:, None]) & live_at[None, :], axis=1)
    tail_fill = jax.random.randint(subkeys[6], (DECODE_ROWS,), 2, PAGE_TOKENS + 1)
    lengths = jnp.where(row_ids == 0, PROMPT_BLOCKS * BLOCK_TOKENS, (page_counts - 1) * PAGE_TOKENS + tail_fill)
    entry_at = jnp.where(live_at, row_at * MAXP + page_at, -1)
    slot_list = entry_at[position_of]
    return (placement_list.astype(jnp.int32), slot_list.astype(jnp.int32), lengths.astype(jnp.int32))


def draw_placement(key, part):
    placement_list, slot_list, lengths = page_layout(key)
    return placement_list


def draw_slot_pages(key, part):
    placement_list, slot_list, lengths = page_layout(key)
    return slot_list


def draw_context_len(key, part):
    placement_list, slot_list, lengths = page_layout(key)
    return lengths


def draw_prompt_queries(key, part):
    key = jax.random.fold_in(key, 1)
    subkeys = jax.random.split(key, 1)
    full_shape = (LAYER_COUNT, PROMPT_BLOCKS, BLOCK_TOKENS, QUERY_HEADS * HEAD_SIZE)
    values = jnp.clip(1.2 * jax.random.normal(subkeys[0], full_shape, jnp.float32), -8.0, 8.0)
    return values.astype(jnp.bfloat16)


def draw_prompt_pairs(key, part):
    key = jax.random.fold_in(key, 2)
    subkeys = jax.random.split(key, 2)
    half_layout = (LAYER_COUNT, PROMPT_BLOCKS, BLOCK_TOKENS, KEY_HEADS * HEAD_SIZE)
    key_part = jnp.clip(1.2 * jax.random.normal(subkeys[0], half_layout, jnp.float32), -8.0, 8.0)
    value_part = jnp.clip(3.0 * jax.random.normal(subkeys[1], half_layout, jnp.float32), -10.0, 10.0)
    return jnp.stack([key_part, value_part], axis=3).astype(jnp.bfloat16)


def draw_decode_queries(key, part):
    key = jax.random.fold_in(key, 3)
    subkeys = jax.random.split(key, 1)
    full_shape = (LAYER_COUNT, DECODE_ROWS, DECODE_STEPS, QUERY_HEADS * HEAD_SIZE)
    values = jnp.clip(1.2 * jax.random.normal(subkeys[0], full_shape, jnp.float32), -8.0, 8.0)
    return values.astype(jnp.bfloat16)


def draw_decode_pairs(key, part):
    key = jax.random.fold_in(key, 4)
    subkeys = jax.random.split(key, 2)
    half_layout = (LAYER_COUNT, DECODE_ROWS, DECODE_STEPS, KEY_HEADS * HEAD_SIZE)
    key_part = jnp.clip(1.2 * jax.random.normal(subkeys[0], half_layout, jnp.float32), -8.0, 8.0)
    value_part = jnp.clip(3.0 * jax.random.normal(subkeys[1], half_layout, jnp.float32), -10.0, 10.0)
    return jnp.stack([key_part, value_part], axis=3).astype(jnp.bfloat16)


def draw_cache_pool(key, part):
    key = jax.random.fold_in(key, 5)
    subkeys = jax.random.split(key, 2)
    half_layout = (LAYER_COUNT, GROUP_SLOTS, PAGE_TOKENS, KEY_HEADS * HEAD_SIZE)
    key_part = jnp.clip(1.2 * jax.random.normal(subkeys[0], half_layout, jnp.float32), -8.0, 8.0)
    value_part = jnp.clip(3.0 * jax.random.normal(subkeys[1], half_layout, jnp.float32), -10.0, 10.0)
    return jnp.stack([key_part, value_part], axis=3).astype(jnp.bfloat16)


def block_levels(key, extent, pieces, least, largest):
    def one(position, blocks):
        steps = jax.random.uniform(jax.random.fold_in(jax.random.fold_in(key, 6), position), (blocks,), jnp.float32, least / len(pieces), largest / len(pieces))
        return jnp.repeat(jnp.exp(steps), extent[position] // blocks).reshape((-1,) + (1,) * (len(extent) - position - 1))

    level = one(*pieces[0])
    for cut in pieces[1:]:
        level = level * one(*cut)
    return level


def bell_draw(own_key, dims, spread, bound, pieces=(), kind=jnp.bfloat16):
    values = spread * jax.random.normal(own_key, dims, jnp.float32)
    if pieces:
        values = values * block_levels(own_key, dims, pieces, -0.22, 0.18)
    return jnp.clip(values, -bound, bound).astype(kind)


def setup_inputs(seed: int = 0) -> dict:
    key_list = jax.random.split(jax.random.key(seed), 10)
    return {
        "prompt_queries": draw_prompt_queries(jax.random.fold_in(key_list[9], 71), 0),
        "prompt_pairs": draw_prompt_pairs(jax.random.fold_in(key_list[9], 71), 0),
        "decode_queries": draw_decode_queries(jax.random.fold_in(key_list[9], 71), 0),
        "decode_pairs": draw_decode_pairs(jax.random.fold_in(key_list[9], 71), 0),
        "cache_pool": draw_cache_pool(jax.random.fold_in(key_list[9], 71), 0),
        "out_weight": bell_draw(key_list[5], (LAYER_COUNT, QUERY_HEADS * HEAD_SIZE, D), (QUERY_HEADS * HEAD_SIZE) ** -0.5, 0.0625, ((0, 4), (1, 8), (2, 8))),
        "slot_pages": draw_slot_pages(jax.random.fold_in(key_list[9], 71), 0),
        "placement": draw_placement(jax.random.fold_in(key_list[9], 71), 0),
        "context_len": draw_context_len(jax.random.fold_in(key_list[9], 71), 0),
    }


MASKED_SCORE = -1e+30

def prefill_layer(layer_inputs):
    query_matrix, key_value_pairs = layer_inputs
    row_total_count = PROMPT_BLOCKS * BLOCK_TOKENS
    query_group_width = QUERY_HEADS // KEY_HEADS
    score_scale = 1.0 / math.sqrt(HEAD_SIZE)
    query_lines = query_matrix.reshape(row_total_count, KEY_HEADS, query_group_width, HEAD_SIZE)
    key_matrix = key_value_pairs[:, :, 0].reshape(row_total_count, KEY_HEADS, HEAD_SIZE)
    value_matrix = key_value_pairs[:, :, 1].reshape(row_total_count, KEY_HEADS, HEAD_SIZE)
    results = []
    for block_number in range(row_total_count // BTOK_DEV):
        block_start = block_number * BTOK_DEV
        block_end = block_start + BTOK_DEV
        query_pos = block_start + jnp.arange(BTOK_DEV, dtype=jnp.int32)
        key_pos = jnp.arange(block_end, dtype=jnp.int32)
        allowed = (key_pos[None, :] <= query_pos[:, None])[:, None, :]

        def one_head(head_inputs, allowed=allowed):
            head_queries, head_keys, head_values = head_inputs
            scores = jnp.einsum('iqd,jd->iqj', head_queries.astype(jnp.float32), head_keys.astype(jnp.float32)) * score_scale
            scores = jnp.where(allowed, scores, MASKED_SCORE)
            row_max = lax.optimization_barrier(jnp.max(scores, axis=-1, keepdims=True))
            attention_weight = jnp.where(allowed, jnp.exp(scores - row_max), 0.0)
            rounded = lax.optimization_barrier(attention_weight.astype(jnp.bfloat16)).astype(jnp.float32)
            weighted_total = jnp.einsum('iqj,jd->iqd', rounded, head_values.astype(jnp.float32))
            return (weighted_total / lax.optimization_barrier(jnp.sum(attention_weight, axis=-1))[..., None]).astype(jnp.bfloat16)
        heads_out = lax.map(one_head, (jnp.transpose(query_lines[block_start:block_end], (1, 0, 2, 3)), jnp.transpose(key_matrix[:block_end], (1, 0, 2)), jnp.transpose(value_matrix[:block_end], (1, 0, 2))))
        results.append(jnp.transpose(heads_out, (1, 0, 2, 3)).reshape(BTOK_DEV, QUERY_HEADS * HEAD_SIZE))
    return jnp.concatenate(results, axis=0).reshape(PROMPT_BLOCKS, BLOCK_TOKENS, QUERY_HEADS * HEAD_SIZE)

def decode_layer(query_matrix, incoming_pairs, pool_pages, weight_matrix, prompt_cache_pairs, slot_pages, placement, context_len):
    query_group_width = QUERY_HEADS // KEY_HEADS
    score_scale = 1.0 / math.sqrt(HEAD_SIZE)
    prompt_page_list = prompt_cache_pairs.reshape(PROMPT_PAGES, PAGE_TOKENS, 2, KEY_HEADS * HEAD_SIZE)
    complete_pool = pool_pages.at[placement].set(prompt_page_list)
    entries = slot_pages.at[placement].set(jnp.arange(PROMPT_PAGES, dtype=jnp.int32))
    live_slot = entries >= 0
    owning_row = jnp.where(live_slot, entries // MAXP, 0).astype(jnp.int32)
    page_number = jnp.where(live_slot, entries % MAXP, 0).astype(jnp.int32)
    valid_rows = jnp.where(live_slot, jnp.clip(context_len[owning_row] - page_number * PAGE_TOKENS, 0, PAGE_TOKENS), 0)
    slotted_queries = query_matrix[owning_row].reshape(GROUP_SLOTS, DECODE_STEPS, KEY_HEADS, query_group_width, HEAD_SIZE).astype(jnp.float32)
    slotted_keys = complete_pool[:, :, 0].reshape(GROUP_SLOTS, PAGE_TOKENS, KEY_HEADS, HEAD_SIZE).astype(jnp.float32)
    slotted_values = complete_pool[:, :, 1].reshape(GROUP_SLOTS, PAGE_TOKENS, KEY_HEADS, HEAD_SIZE).astype(jnp.float32)
    scores = jnp.einsum('stgqd,sjgd->stgqj', slotted_queries, slotted_keys) * score_scale
    allowed = (jnp.arange(PAGE_TOKENS, dtype=jnp.int32)[None, :] < valid_rows[:, None])[:, None, None, None, :]
    scores = jnp.where(allowed, scores, MASKED_SCORE)
    slot_max = lax.optimization_barrier(jnp.max(scores, axis=-1))
    member = (owning_row[None, :] == jnp.arange(DECODE_ROWS, dtype=jnp.int32)[:, None]) & live_slot[None, :]
    pool_max = lax.optimization_barrier(jnp.max(jnp.where(member[:, :, None, None, None], slot_max[None], MASKED_SCORE), axis=1))
    reshaped_input = query_matrix.reshape(DECODE_ROWS, DECODE_STEPS, KEY_HEADS, query_group_width, HEAD_SIZE).astype(jnp.float32)
    incoming_keys = incoming_pairs[:, :, 0].reshape(DECODE_ROWS, DECODE_STEPS, KEY_HEADS, HEAD_SIZE).astype(jnp.float32)
    incoming_values = incoming_pairs[:, :, 1].reshape(DECODE_ROWS, DECODE_STEPS, KEY_HEADS, HEAD_SIZE).astype(jnp.float32)
    recent = jnp.einsum('rtgqd,rugd->rtgqu', reshaped_input, incoming_keys) * score_scale
    step_ids = jnp.arange(DECODE_STEPS, dtype=jnp.int32)
    causal = (step_ids[None, :] <= step_ids[:, None])[None, :, None, None, :]
    recent = jnp.where(causal, recent, MASKED_SCORE)
    row_max = jnp.maximum(pool_max, lax.optimization_barrier(jnp.max(recent, axis=-1)))
    attention_weight = jnp.where(allowed, jnp.exp(scores - row_max[owning_row][..., None]), 0.0)
    rounded = lax.optimization_barrier(attention_weight.astype(jnp.bfloat16)).astype(jnp.float32)
    slotted_weighted_total = jnp.einsum('stgqj,sjgd->stgqd', rounded, slotted_values)
    indicator_matrix = member.astype(jnp.float32)
    weighted_total = jnp.dot(indicator_matrix, slotted_weighted_total.reshape(GROUP_SLOTS, -1), precision=lax.Precision.HIGHEST).reshape(DECODE_ROWS, DECODE_STEPS, KEY_HEADS, query_group_width, HEAD_SIZE)
    softmax_divisor = jnp.dot(indicator_matrix, lax.optimization_barrier(jnp.sum(attention_weight, axis=-1)).reshape(GROUP_SLOTS, -1), precision=lax.Precision.HIGHEST).reshape(DECODE_ROWS, DECODE_STEPS, KEY_HEADS, query_group_width)
    recent_weights = jnp.where(causal, jnp.exp(recent - row_max[..., None]), 0.0)
    recent_rounded = lax.optimization_barrier(recent_weights.astype(jnp.bfloat16)).astype(jnp.float32)
    weighted_total = weighted_total + jnp.einsum('rtgqu,rugd->rtgqd', recent_rounded, incoming_values)
    softmax_divisor = softmax_divisor + lax.optimization_barrier(jnp.sum(recent_weights, axis=-1))
    attended = (weighted_total / softmax_divisor[..., None]).astype(jnp.bfloat16).reshape(DECODE_ROWS * DECODE_STEPS, QUERY_HEADS * HEAD_SIZE)
    mixed = jnp.dot(attended, weight_matrix, preferred_element_type=jnp.float32)
    return mixed.reshape(DECODE_ROWS, DECODE_STEPS, D).astype(jnp.bfloat16)

def reference(prompt_queries, prompt_pairs, decode_queries, decode_pairs, cache_pool, out_weight, slot_pages, placement, context_len):
    prefill_out = lax.map(prefill_layer, (prompt_queries, prompt_pairs))
    mixes = []
    for group_index in range(LAYER_COUNT):
        layer_index = (group_index + LAYER_COUNT // 2) % LAYER_COUNT
        mixes.append(decode_layer(decode_queries[group_index], decode_pairs[group_index], cache_pool[group_index], out_weight[group_index], prompt_pairs[layer_index], slot_pages, placement, context_len))
    return (prefill_out, jnp.stack(mixes))
```

```python
import functools
import math

import jax
import jax.numpy as jnp
from jax import lax
from jax.experimental import pallas as pl
from jax.experimental.pallas import tpu as pltpu
from jax.sharding import PartitionSpec as P

HEAD = 128
PAGE = 128
MAXP = 1024
BLOCKS = 2
NEG = -1e30
F32 = jnp.float32
BF16 = jnp.bfloat16
MESH = pl.DeviceIdType.MESH
SCALE = 1.0 / (math.sqrt(HEAD) * math.log(2.0))


def dot_nt(a, b):
    return lax.dot_general(a, b, (((1,), (1,)), ((), ())), preferred_element_type=F32)


def dot_nn(a, b, precision=None):
    return lax.dot_general(
        a, b, (((1,), (0,)), ((), ())), preferred_element_type=F32, precision=precision
    )


def iota(shape, dim):
    return lax.broadcasted_iota(jnp.int32, shape, dim)


def kernel(
    nsec, nseq, nmp, slots, rows, heads, steps,
    pq_h, pp_h, dq_h, dp_h, pool_h, w_h, slot_s, ctx_s,
    pre_h, mix_o,
    pq_v, pp_v, dq_v, dp_v, pool_v, w_v, kv, q0, r0_out, r0_in, lse, accs,
    part, part_in, att, prod, prod_in, pre_v,
    in_sem, out_sem, kv_s, kv_r, z_s, z_r, lse_s, lse_r, rs_s, rs_r, ag_s, ag_r, mp_s, mp_r,
):
    hs = heads * steps
    own = rows // nseq
    me = lax.axis_index("seq")
    mp = lax.axis_index("mp")
    sec = lax.axis_index("section")
    partner = {"section": lax.rem(sec + nsec // 2, nsec)}

    def seq_dev(k):
        return {"seq": lax.rem(me + k, nseq)}

    def mp_dev(k):
        return {"mp": lax.rem(mp + k, nmp)}

    def remote(src, dst, send, recv, device):
        return pltpu.make_async_remote_copy(
            src_ref=src, dst_ref=dst, send_sem=send, recv_sem=recv,
            device_id=device, device_id_type=MESH,
        )

    chunk = slots // 4 * 2 * PAGE
    loads = [
        pltpu.make_async_copy(pp_h, pp_v, in_sem.at[0]),
        pltpu.make_async_copy(dq_h, dq_v, in_sem.at[1]),
        pltpu.make_async_copy(dp_h.at[pl.ds(me * own * 2 * steps, own * 2 * steps)], dp_v, in_sem.at[2]),
        pltpu.make_async_copy(pool_h, pool_v, in_sem.at[3]),
        pltpu.make_async_copy(pq_h, pq_v, in_sem.at[4]),
        pltpu.make_async_copy(w_h, w_v, in_sem.at[5]),
    ]
    for c in loads:
        c.start()

    barrier = pltpu.get_barrier_semaphore()
    for k in range(1, nseq):
        pl.semaphore_signal(barrier, inc=1, device_id=seq_dev(k), device_id_type=MESH)
    for k in range(1, nmp):
        pl.semaphore_signal(barrier, inc=1, device_id=mp_dev(k), device_id_type=MESH)
    pl.semaphore_signal(barrier, inc=1, device_id=partner, device_id_type=MESH)

    loads[0].wait()
    ri = iota((2 * PAGE, 2 * PAGE), 0)
    ci = iota((2 * PAGE, 2 * PAGE), 1)
    pick = jnp.where(ci == jnp.where(ri < PAGE, 2 * ri, 2 * (ri - PAGE) + 1), 1.0, 0.0).astype(BF16)
    for b in range(BLOCKS):
        both = dot_nn(pick, pp_v[b * 2 * PAGE:(b + 1) * 2 * PAGE, :]).astype(BF16)
        kv[me, b * PAGE:(b + 1) * PAGE, :] = both[:PAGE]
        kv[me, (BLOCKS + b) * PAGE:(BLOCKS + b + 1) * PAGE, :] = both[PAGE:]
    loads[1].wait()

    pl.semaphore_wait(barrier, nseq + nmp - 1)

    q_out = remote(dq_v.at[0], q0, z_s.at[0], z_r.at[0], partner)
    q_out.start()
    kv_copies = [
        remote(kv.at[me], kv.at[me], kv_s.at[k - 1], kv_r.at[k - 1], seq_dev(k))
        for k in range(1, nseq)
    ]
    for c in kv_copies:
        c.start()

    lane = iota((hs, 128), 1)
    lane1 = iota((8, 128), 1)
    key_lane = iota((hs, 2 * PAGE), 1)
    key_id = jnp.where(key_lane % 2 == 0, key_lane // 2, PAGE)

    def merge(state, index, row, m, l):
        top, total, slot_top, slot_row = state
        hit = lane == row
        fresh = jnp.where(hit, jnp.maximum(top, m), top)
        total = total * jnp.exp2((top - fresh) * SCALE) + jnp.where(
            hit, l * jnp.exp2((m - fresh) * SCALE), 0.0
        )
        slot_top = jnp.where(lane == index, m, slot_top)
        slot_row = jnp.where(lane1 == index, row, slot_row)
        return fresh, total, slot_top, slot_row

    def slot_group(g, state, width):
        done = []
        for i in range(width):
            j = g * width + i
            entry = slot_s[j]
            live = entry >= 0
            row = jnp.where(live, entry // MAXP, 0)
            count = jnp.where(live, jnp.clip(ctx_s[row] - (entry % MAXP) * PAGE, 0, PAGE), 0)
            page = pool_v[pl.ds(pl.multiple_of(j * 2 * PAGE, 2 * PAGE), 2 * PAGE), :]
            done.append((j, jnp.where(live, row, -1), count, page, dot_nt(dq_v[row], page)))
        for j, row, count, page, scores in done:
            allowed = key_id < count
            scores = jnp.where(allowed, scores, NEG)
            m = jnp.max(scores, axis=1, keepdims=True)
            p = jnp.where(allowed, jnp.exp2((scores - m) * SCALE), 0.0)
            l = jnp.sum(p, axis=1, keepdims=True)
            acc = dot_nn(pltpu.roll(p, 1, 1).astype(BF16), page)
            accs[pl.ds(pl.multiple_of(j * hs, hs), hs), :] = acc
            state = merge(state, j, row, m, l)
        return state

    state = (
        jnp.full((hs, 128), NEG, F32), jnp.zeros((hs, 128), F32),
        jnp.full((hs, 128), NEG, F32), jnp.full((8, 128), -1, jnp.int32),
    )
    width = 4
    loads[3].wait()
    first = slots // width // 2
    state = lax.fori_loop(0, first, lambda g, s: slot_group(g, s, width), state)

    q_out.wait()
    k_mine = kv[me, 0:BLOCKS * PAGE, :]
    v_mine = kv[me, BLOCKS * PAGE:2 * BLOCKS * PAGE, :]
    scores = dot_nt(q0[...], k_mine)
    place = iota((hs, BLOCKS * PAGE), 1)
    position = jnp.where(place < PAGE, place, place - PAGE + nseq * PAGE) + me * PAGE
    allowed = position < ctx_s[0]
    scores = jnp.where(allowed, scores, NEG)
    m = jnp.max(scores, axis=1, keepdims=True)
    p = jnp.where(allowed, jnp.exp2((scores - m) * SCALE), 0.0)
    l = jnp.sum(p, axis=1, keepdims=True)
    r0_out[0:hs, :] = dot_nn(p.astype(BF16), v_mine)
    r0_out[hs:2 * hs, :] = jnp.where(lane == 0, m, l)
    r0_copy = remote(r0_out, r0_in, z_s.at[1], z_r.at[1], partner)
    r0_copy.start()

    state = lax.fori_loop(first, slots // width, lambda g, s: slot_group(g, s, width), state)

    loads[2].wait()
    recent = dp_v[...]
    rq = dq_v[pl.ds(me * own, own)].reshape(own * hs, HEAD)
    scores = dot_nt(rq, recent)
    ri = iota(scores.shape, 0)
    ci = iota(scores.shape, 1)
    allowed = (
        (ci % 2 == 0) & (ci // (2 * steps) == ri // hs) & ((ci % (2 * steps)) // 2 <= ri % steps)
    )
    scores = jnp.where(allowed, scores, NEG)
    m = jnp.max(scores, axis=1, keepdims=True)
    p = jnp.where(allowed, jnp.exp2((scores - m) * SCALE), 0.0)
    l = jnp.sum(p, axis=1, keepdims=True)
    accs[slots * hs:(slots + own) * hs, :] = dot_nn(pltpu.roll(p, 1, 1).astype(BF16), recent)
    for r in range(own):
        state = merge(
            state, slots + r, me * own + r, m[r * hs:(r + 1) * hs], l[r * hs:(r + 1) * hs]
        )

    r0_copy.wait()
    stats = r0_in[hs:2 * hs, :]
    row0 = slots + own
    accs[row0 * hs:(row0 + 1) * hs, :] = r0_in[0:hs, :]
    state = merge(state, row0, 0, stats[:, 0:1], stats[:, 1:2])
    pad_rows = accs.shape[0] - (row0 + 1) * hs
    accs[(row0 + 1) * hs:, :] = jnp.zeros((pad_rows, HEAD), F32)

    top, total, slot_top, slot_row = state
    lse[me] = jnp.where(
        total > 0.0, top * SCALE + jnp.log2(jnp.maximum(total, 1e-30)), NEG
    )
    lse_copies = [
        remote(lse.at[me], lse.at[me], lse_s.at[k - 1], lse_r.at[k - 1], seq_dev(k))
        for k in range(1, nseq)
    ]
    for c in lse_copies:
        c.start()

    loads[4].wait()
    kv_ready = []

    def prompt_piece(b, pair):
        two = pq_v[b, :, pl.ds(pl.multiple_of(pair * 2 * HEAD, 2 * HEAD), 2 * HEAD)]
        q = jnp.concatenate([two[:, :HEAD], two[:, HEAD:]], axis=0)
        n = nseq * PAGE
        k_own = kv[:, b * PAGE:(b + 1) * PAGE, :].reshape(n, HEAD)
        v_own = kv[:, (BLOCKS + b) * PAGE:(BLOCKS + b + 1) * PAGE, :].reshape(n, HEAD)
        s_own = dot_nt(q, k_own)
        limit = me * PAGE + iota((2 * PAGE, n), 0) % PAGE
        s_own = jnp.where(iota((2 * PAGE, n), 1) <= limit, s_own, NEG)
        m = jnp.max(s_own, axis=1, keepdims=True)
        if b:
            k_old = kv[:, 0:PAGE, :].reshape(n, HEAD)
            v_old = kv[:, BLOCKS * PAGE:(BLOCKS + 1) * PAGE, :].reshape(n, HEAD)
            s_old = dot_nt(q, k_old)
            m = jnp.maximum(m, jnp.max(s_old, axis=1, keepdims=True))
        p = jnp.exp2((s_own - m) * SCALE)
        l = jnp.sum(p, axis=1, keepdims=True)
        o = dot_nn(p.astype(BF16), v_own)
        if b:
            p = jnp.exp2((s_old - m) * SCALE)
            l = l + jnp.sum(p, axis=1, keepdims=True)
            o = o + dot_nn(p.astype(BF16), v_old)
        o = (o / l).astype(BF16)
        pre_v[b, :, pl.ds(pl.multiple_of(pair * 2 * HEAD, 2 * HEAD), 2 * HEAD)] = jnp.concatenate(
            [o[:PAGE], o[PAGE:]], axis=1
        )

    def prompt_pieces(b, lo, hi):
        def step(i, carry):
            prompt_piece(b, i)
            return carry

        lax.fori_loop(lo, hi, step, 0)

    for c in kv_copies:
        c.wait()
    pairs = heads // 2
    prompt_pieces(0, 0, pairs)

    for c in lse_copies:
        c.wait()
    every = [lse[k] for k in range(nseq)]
    peak = functools.reduce(jnp.maximum, every)
    whole = peak + jnp.log2(sum(jnp.exp2(e - peak) for e in every))
    row_pick = jnp.where(
        iota((128, 128), 0) == jnp.broadcast_to(slot_row[0:1], (128, 128)), 1.0, 0.0
    )
    whole_slot = dot_nn(whole, row_pick, lax.Precision.HIGHEST)
    factor = jnp.exp2(slot_top * SCALE - whole_slot)
    count = accs.shape[0] // hs
    for i in range(hs):
        weights = (row_pick * jnp.broadcast_to(factor[i:i + 1], (128, 128)))[:rows, :count]
        sums = dot_nn(
            weights.astype(BF16), accs[pl.ds(i, count, stride=hs), :].astype(BF16)
        ).astype(BF16)
        for s in range(nseq):
            part[s, i] = sums[s * own:(s + 1) * own]

    rs_copies = [
        remote(
            part.at[lax.rem(me + k, nseq)], part_in.at[k - 1],
            rs_s.at[k - 1], rs_r.at[k - 1], seq_dev(k),
        )
        for k in range(1, nseq)
    ]
    for c in rs_copies:
        c.start()

    prompt_pieces(1, 0, pairs // 2)

    for c in rs_copies:
        c.wait()
    for i in range(heads):
        sl = slice(i * steps, (i + 1) * steps)
        tot = part[me, sl].astype(F32)
        for k in range(nseq - 1):
            tot = tot + part_in[k, sl].astype(F32)
        att[me, sl] = tot.astype(BF16)

    ag_copies = [
        remote(att.at[me], att.at[me], ag_s.at[k - 1], ag_r.at[k - 1], seq_dev(k))
        for k in range(1, nseq)
    ]
    for c in ag_copies:
        c.start()

    prompt_pieces(1, pairs // 2, pairs)
    pre_copy = pltpu.make_async_copy(pre_v, pre_h, out_sem)
    pre_copy.start()

    for c in ag_copies:
        c.wait()
    loads[5].wait()

    def slab_product(s):
        left = jnp.concatenate(
            [att[s, h * steps:(h + 1) * steps].reshape(steps * own, HEAD) for h in range(heads)],
            axis=1,
        )
        return dot_nn(left, w_v[...])

    mp_copies = []
    for k in range(1, nmp):
        prod[k] = slab_product(lax.rem(mp + k, nmp)).astype(BF16)
        c = remote(prod.at[k], prod_in.at[k - 1], mp_s.at[k - 1], mp_r.at[k - 1], mp_dev(k))
        c.start()
        mp_copies.append(c)
    mix = slab_product(mp)
    for k, c in enumerate(mp_copies):
        c.wait()
        mix = mix + prod_in[k].astype(F32)
    mix_o[...] = mix.astype(BF16)
    pre_copy.wait()


def body(
    prompt_queries, prompt_pairs, decode_queries, decode_pairs, cache_pool, out_weight,
    slot_pages, placement, context_len,
):
    nsec, nseq, nmp = (lax.axis_size(a) for a in ("section", "seq", "mp"))
    _, blocks, btok, qwidth = prompt_queries.shape
    _, rows, steps, _ = decode_queries.shape
    slots = cache_pool.shape[1]
    width = out_weight.shape[2]
    heads = qwidth // HEAD
    hs = heads * steps
    own = rows // nseq
    pq = prompt_queries[0]
    pp = prompt_pairs.reshape(blocks * btok * 2, HEAD)
    dq = decode_queries.reshape(rows, steps, heads, HEAD).transpose(0, 2, 1, 3).reshape(rows, hs, HEAD)
    dp = decode_pairs.reshape(rows * steps * 2, HEAD)
    pool = cache_pool.reshape(slots * PAGE * 2, HEAD)
    w = out_weight[0]
    count = -(-(slots + own + 1) // 16) * 16
    any_spec = pl.BlockSpec(memory_space=pl.ANY)
    smem_spec = pl.BlockSpec(memory_space=pltpu.SMEM)
    dma = pltpu.SemaphoreType.DMA
    prefill, mixed = pl.pallas_call(
        functools.partial(kernel, nsec, nseq, nmp, slots, rows, heads, steps),
        out_shape=(
            jax.ShapeDtypeStruct(pq.shape, BF16),
            jax.ShapeDtypeStruct((steps * own, width), BF16),
        ),
        in_specs=[any_spec] * 6 + [smem_spec] * 2,
        out_specs=(any_spec, pl.BlockSpec(memory_space=pltpu.VMEM)),
        scratch_shapes=[
            pltpu.VMEM(pq.shape, BF16),
            pltpu.VMEM(pp.shape, BF16),
            pltpu.VMEM(dq.shape, BF16),
            pltpu.VMEM((own * 2 * steps, HEAD), BF16),
            pltpu.VMEM(pool.shape, BF16),
            pltpu.VMEM(w.shape, BF16),
            pltpu.VMEM((nseq,) + pp.shape, BF16),
            pltpu.VMEM((hs, HEAD), BF16),
            pltpu.VMEM((2 * hs, HEAD), F32),
            pltpu.VMEM((2 * hs, HEAD), F32),
            pltpu.VMEM((nseq, hs, 128), F32),
            pltpu.VMEM((count * hs, HEAD), F32),
            pltpu.VMEM((nseq, hs, own, HEAD), BF16),
            pltpu.VMEM((nseq, hs, own, HEAD), BF16),
            pltpu.VMEM((nseq, hs, own, HEAD), BF16),
            pltpu.VMEM((nmp, steps * own, width), BF16),
            pltpu.VMEM((nmp, steps * own, width), BF16),
            pltpu.VMEM(pq.shape, BF16),
            dma((6,)),
            dma,
            dma((nseq,)), dma((nseq,)),
            dma((2,)), dma((2,)),
            dma((nseq,)), dma((nseq,)),
            dma((nseq,)), dma((nseq,)),
            dma((nseq,)), dma((nseq,)),
            dma((nmp,)), dma((nmp,)),
        ],
        compiler_params=pltpu.CompilerParams(
            collective_id=0, has_side_effects=True, vmem_limit_bytes=56 * 1024 * 1024
        ),
    )(pq, pp, dq, dp, pool, w, slot_pages, context_len)
    mixed = mixed.reshape(steps, own, width).transpose(1, 0, 2)
    return prefill[None], mixed[None]


def solution(mesh):
    return jax.shard_map(
        body,
        mesh=mesh,
        in_specs=(
            P("section", None, "seq", "mp"),
            P("section", None, "seq", None, "mp"),
            P("section", None, None, "mp"),
            P("section", None, None, None, "mp"),
            P("section", "seq", None, None, "mp"),
            P("section", "mp", "seq"),
            P("seq"),
            P(),
            P(),
        ),
        out_specs=(P("section", None, "seq", "mp"), P("section", "mp", None, "seq")),
        check_vma=False,
    )
```

```python
import functools
import math

import jax
import jax.numpy as jnp
from jax import lax
from jax.experimental import pallas as pl
from jax.experimental.pallas import tpu as pltpu
from jax.sharding import PartitionSpec as P

HEAD = 128
PAGE = 128
MAXP = 1024
BLOCKS = 2
NEG = -1e30
F32 = jnp.float32
BF16 = jnp.bfloat16
MESH = pl.DeviceIdType.MESH
SCALE = 1.0 / (math.sqrt(HEAD) * math.log(2.0))


def dot_nt(a, b):
    return lax.dot_general(a, b, (((1,), (1,)), ((), ())), preferred_element_type=F32)


def dot_nn(a, b, precision=None):
    return lax.dot_general(
        a, b, (((1,), (0,)), ((), ())), preferred_element_type=F32, precision=precision
    )


def iota(shape, dim):
    return lax.broadcasted_iota(jnp.int32, shape, dim)


def kernel(
    nsec, nseq, nmp, slots, rows, heads, steps,
    pq_h, pp_h, dq_h, dp_h, pool_h, w_h, slot_s, ctx_s,
    pre_h, mix_o,
    pq_v, pp_v, dq_v, dp_v, pool_v, w_v, kv, q0, r0_out, r0_in, lse_out, lse_in, lse_t, lse_t_in,
    accs, part, sib_in, part_in, att_f, att, prod, prod_in, mix_v, pre_v,
    in_sem, out_sem, kv_s, kv_r, z_s, z_r, sib_s, sib_r, rs_s, rs_r, st_s, st_r, ag_s, ag_r, mp_s, mp_r,
):
    hs = heads * steps
    half = hs // 2
    own = rows // nseq
    chips = nseq // 2
    me = lax.axis_index("seq")
    mp = lax.axis_index("mp")
    sec = lax.axis_index("section")
    chip, core = me // 2, me % 2
    partner = {"section": lax.rem(sec + nsec // 2, nsec)}
    sibling = {"seq": 2 * chip + 1 - core}
    away = (1, 3, 2)
    far_chip = [lax.rem(chip + k, 4) for k in away]
    far = [{"seq": 2 * c + core} for c in far_chip]
    from_chip = [lax.rem(chip + 4 - k, 4) for k in away]

    def mp_dev(k):
        return {"mp": lax.rem(mp + k, nmp)}

    def remote(src, dst, send, recv, device):
        return pltpu.make_async_remote_copy(
            src_ref=src, dst_ref=dst, send_sem=send, recv_sem=recv,
            device_id=device, device_id_type=MESH,
        )

    barrier = pltpu.get_barrier_semaphore()
    greeted = [partner, *far, *(mp_dev(k) for k in range(1, nmp)), sibling]
    for device in greeted:
        pl.semaphore_signal(barrier, inc=1, device_id=device, device_id_type=MESH)

    half_pool = slots * PAGE
    loads = [
        pltpu.make_async_copy(dq_h, dq_v, in_sem.at[0]),
        pltpu.make_async_copy(pool_h.at[0:half_pool], pool_v.at[0:half_pool], in_sem.at[1]),
        pltpu.make_async_copy(pp_h, pp_v, in_sem.at[2]),
        pltpu.make_async_copy(pool_h.at[half_pool:], pool_v.at[half_pool:], in_sem.at[3]),
        pltpu.make_async_copy(dp_h, dp_v, in_sem.at[4]),
        pltpu.make_async_copy(pq_h, pq_v, in_sem.at[5]),
        pltpu.make_async_copy(w_h, w_v, in_sem.at[6]),
    ]
    for c in loads:
        c.start()

    lane = iota((hs, 128), 1)
    lane1 = iota((8, 128), 1)
    key_lane = iota((hs, 2 * PAGE), 1)
    key_id = jnp.where(key_lane % 2 == 0, key_lane // 2, PAGE)

    def place_of(row):
        return (row % 16) // 2 * 16 + row % 2 * 8 + row // 16

    def merge(state, index, place, m, l):
        top, total, slot_top, slot_place = state
        hit = lane == place
        fresh = jnp.where(hit, jnp.maximum(top, m), top)
        total = total * jnp.exp2((top - fresh) * SCALE) + jnp.where(
            hit, l * jnp.exp2((m - fresh) * SCALE), 0.0
        )
        slot_top = jnp.where(lane == index, m, slot_top)
        slot_place = jnp.where(lane1 == index, place, slot_place)
        return fresh, total, slot_top, slot_place

    def slot_group(g, state, width):
        done = []
        for i in range(width):
            j = g * width + i
            entry = slot_s[j]
            live = entry >= 0
            row = jnp.where(live, entry // MAXP, 0)
            count = jnp.where(live, jnp.clip(ctx_s[row] - (entry % MAXP) * PAGE, 0, PAGE), 0)
            page = pool_v[pl.ds(pl.multiple_of(j * 2 * PAGE, 2 * PAGE), 2 * PAGE), :]
            place = jnp.where(live, place_of(row), -1)
            done.append((j, place, count, page, dot_nt(dq_v[row], page)))
        for j, place, count, page, scores in done:
            allowed = key_id < count
            scores = jnp.where(allowed, scores, NEG)
            m = jnp.max(scores, axis=1, keepdims=True)
            p = jnp.where(allowed, jnp.exp2((scores - m) * SCALE), 0.0)
            l = jnp.sum(p, axis=1, keepdims=True)
            acc = dot_nn(pltpu.roll(p, 1, 1).astype(BF16), page)
            accs[pl.ds(pl.multiple_of(j * hs, hs), hs), :] = acc
            state = merge(state, j, place, m, l)
        return state

    state = (
        jnp.full((hs, 128), NEG, F32), jnp.zeros((hs, 128), F32),
        jnp.full((hs, 128), NEG, F32), jnp.full((8, 128), -1, jnp.int32),
    )
    width = 4
    loads[0].wait()
    loads[1].wait()
    first = slots // width // 2
    state = lax.fori_loop(0, first, lambda g, s: slot_group(g, s, width), state)

    loads[2].wait()
    ri = iota((2 * PAGE, 2 * PAGE), 0)
    ci = iota((2 * PAGE, 2 * PAGE), 1)
    pick = jnp.where(ci == jnp.where(ri < PAGE, 2 * ri, 2 * (ri - PAGE) + 1), 1.0, 0.0).astype(BF16)
    for b in range(BLOCKS):
        both = dot_nn(pick, pp_v[b * 2 * PAGE:(b + 1) * 2 * PAGE, :]).astype(BF16)
        kv[me, b * PAGE:(b + 1) * PAGE, :] = both[:PAGE]
        kv[me, (BLOCKS + b) * PAGE:(BLOCKS + b + 1) * PAGE, :] = both[PAGE:]

    pl.semaphore_wait(barrier, len(greeted))
    q_out = remote(dq_v.at[0], q0, z_s.at[0], z_r.at[0], partner)
    q_out.start()
    kv_far = [remote(kv.at[me], kv.at[me], kv_s.at[i], kv_r.at[i], far[i]) for i in range(3)]
    for c in kv_far:
        c.start()
    kv_near = [remote(kv.at[me], kv.at[me], kv_s.at[3], kv_r.at[3], sibling)] + [
        remote(kv.at[2 * f + core], kv.at[2 * f + core], kv_s.at[4 + i], kv_r.at[4 + i], sibling)
        for i, f in enumerate(from_chip)
    ]
    kv_near[0].start()

    loads[3].wait()
    state = lax.fori_loop(first, slots // width, lambda g, s: slot_group(g, s, width), state)

    loads[4].wait()
    mine = [16 * m + 2 * me for m in range(nmp)]
    line = 2 * steps
    recent = jnp.concatenate(
        [dp_v[pl.ds(pl.multiple_of(r * line, 2 * line), 2 * line), :] for r in mine], axis=0
    )
    rq = jnp.concatenate([dq_v[pl.ds(r, 2)].reshape(2 * hs, HEAD) for r in mine], axis=0)
    scores = dot_nt(rq, recent)
    ri = iota(scores.shape, 0)
    ci = iota(scores.shape, 1)
    allowed = (
        (ci % 2 == 0) & (ci // line == ri // hs) & ((ci % line) // 2 <= ri % steps)
    )
    scores = jnp.where(allowed, scores, NEG)
    m = jnp.max(scores, axis=1, keepdims=True)
    p = jnp.where(allowed, jnp.exp2((scores - m) * SCALE), 0.0)
    l = jnp.sum(p, axis=1, keepdims=True)
    accs[slots * hs:(slots + own) * hs, :] = dot_nn(pltpu.roll(p, 1, 1).astype(BF16), recent)
    for r in range(own):
        state = merge(
            state, slots + r, me * own + r % 2 * 8 + r // 2,
            m[r * hs:(r + 1) * hs], l[r * hs:(r + 1) * hs],
        )
    top, total, slot_top, slot_place = state
    lse_mine = jnp.where(
        total > 0.0, top * SCALE + jnp.log2(jnp.maximum(total, 1e-30)), NEG
    )
    lse_out[...] = lse_mine
    lse_copy = remote(lse_out, lse_in, z_s.at[2], z_r.at[2], sibling)
    lse_copy.start()
    place_pick = jnp.where(
        iota((128, 128), 0) == jnp.broadcast_to(slot_place[0:1], (128, 128)), 1.0, 0.0
    )
    lse_copy.wait()
    peak = jnp.maximum(lse_mine, lse_in[...])
    lse_chip = peak + jnp.log2(jnp.exp2(lse_mine - peak) + jnp.exp2(lse_in[...] - peak))
    whole_slot = dot_nn(lse_chip, place_pick, lax.Precision.HIGHEST)
    factor = jnp.exp2(slot_top * SCALE - whole_slot)
    lse_t[...] = jnp.concatenate([lse_chip, jnp.zeros((128 - hs, 128), F32)], axis=0).T

    count = accs.shape[0] // hs
    sib_copies = []
    for h in range(2):
        for i in range(half):
            j = h * half + i
            weights = (place_pick * jnp.broadcast_to(factor[j:j + 1], (128, 128)))[:rows, :count]
            sums = dot_nn(
                weights.astype(BF16), accs[pl.ds(j, count, stride=hs), :].astype(BF16)
            ).astype(BF16)
            for s in range(nseq):
                part[h, s % 2, s // 2, i] = sums[s * own:(s + 1) * own]
        c = remote(part.at[h, 1 - core], sib_in.at[h], sib_s.at[h], sib_r.at[h], sibling)
        c.start()
        sib_copies.append(c)

    st_copies = [
        remote(
            lse_t.at[pl.ds(pl.multiple_of((2 * f + core) * own, own), own)], lse_t_in.at[i],
            st_s.at[i], st_r.at[i], far[i],
        )
        for i, f in enumerate(far_chip)
    ]
    for c in st_copies:
        c.start()
    rs_copies = []
    for h in range(2):
        sib_copies[h].wait()
        for f in far_chip + [chip]:
            for i in range(0, half, 4):
                sl = slice(i, i + 4)
                part[h, core, f, sl] = (
                    part[h, core, f, sl].astype(F32) + sib_in[h, f, sl].astype(F32)
                ).astype(BF16)
        for i, f in enumerate(far_chip):
            c = remote(
                part.at[h, core, f], part_in.at[h, i], rs_s.at[h, i], rs_r.at[h, i], far[i]
            )
            c.start()
            rs_copies.append(c)

    for i in range(3):
        kv_far[i].wait()
        kv_near[i + 1].start()
    for c in kv_near:
        c.wait()
    loads[5].wait()
    n = nseq * PAGE

    def prompt_keys(b):
        return kv[:, b * PAGE:(b + 1) * PAGE, :].reshape(n, HEAD)

    def prompt_values(b):
        return kv[:, (BLOCKS + b) * PAGE:(BLOCKS + b + 1) * PAGE, :].reshape(n, HEAD)

    q_out.wait()
    s0 = []
    for b in range(BLOCKS):
        scores = dot_nt(q0[...], prompt_keys(b))
        s0.append(jnp.where(iota(scores.shape, 1) + b * n < ctx_s[0], scores, NEG))
    m = functools.reduce(jnp.maximum, [jnp.max(x, axis=1, keepdims=True) for x in s0])
    p0 = [jnp.exp2((x - m) * SCALE) for x in s0]
    l = sum(jnp.sum(p, axis=1, keepdims=True) for p in p0)
    acc = sum(dot_nn(p.astype(BF16), prompt_values(b)) for b, p in enumerate(p0))
    r0_out[0:hs, :] = acc / l
    lse_prompt = jnp.broadcast_to(m * SCALE + jnp.log2(l), (hs, 128))
    r0_out[hs:hs + 8, :] = jnp.concatenate(
        [lse_prompt, jnp.zeros((128 - hs, 128), F32)], axis=0
    ).T[0:8]
    r0_copy = remote(r0_out, r0_in, z_s.at[1], z_r.at[1], partner)
    r0_copy.start()

    def prompt_piece(b, pair):
        two = pq_v[b, :, pl.ds(pl.multiple_of(pair * 2 * HEAD, 2 * HEAD), 2 * HEAD)]
        q = jnp.concatenate([two[:, :HEAD], two[:, HEAD:]], axis=0)
        s_own = dot_nt(q, prompt_keys(b))
        limit = me * PAGE + iota((2 * PAGE, n), 0) % PAGE
        s_own = jnp.where(iota((2 * PAGE, n), 1) <= limit, s_own, NEG)
        m = jnp.max(s_own, axis=1, keepdims=True)
        if b:
            s_old = dot_nt(q, prompt_keys(0))
            m = jnp.maximum(m, jnp.max(s_old, axis=1, keepdims=True))
        p = jnp.exp2((s_own - m) * SCALE)
        l = jnp.sum(p, axis=1, keepdims=True)
        o = dot_nn(p.astype(BF16), prompt_values(b))
        if b:
            p = jnp.exp2((s_old - m) * SCALE)
            l = l + jnp.sum(p, axis=1, keepdims=True)
            o = o + dot_nn(p.astype(BF16), prompt_values(0))
        o = (o / l).astype(BF16)
        pre_v[b, :, pl.ds(pl.multiple_of(pair * 2 * HEAD, 2 * HEAD), 2 * HEAD)] = jnp.concatenate(
            [o[:PAGE], o[PAGE:]], axis=1
        )

    def prompt_pieces(b, lo, hi):
        def step(i, carry):
            prompt_piece(b, i)
            return carry

        lax.fori_loop(lo, hi, step, 0)

    pairs = heads // 2
    prompt_pieces(0, 0, pairs)

    for c in st_copies:
        c.wait()
    r0_copy.wait()
    first_row = (iota((own, 128), 0) == 0) & (me == 0)
    terms = [lse_t[pl.ds(pl.multiple_of(me * own, own), own), :]] + [lse_t_in[i] for i in range(3)] + [
        jnp.where(first_row, jnp.broadcast_to(r0_in[hs:hs + 1, :], (own, 128)), NEG)
    ]
    peak = functools.reduce(jnp.maximum, terms)
    whole = peak + jnp.log2(sum(jnp.exp2(t - peak) for t in terms))
    shares = [jnp.exp2(t - whole) for t in terms]
    ag_far = []
    ag_near = []
    lines = own * steps
    for h in range(2):
        for c in rs_copies[3 * h:3 * h + 3]:
            c.wait()
        for i in range(half):
            j = h * half + i
            blocks = [part[h, core, chip, i]] + [part_in[h, k, i] for k in range(3)]
            tot = jnp.broadcast_to(r0_in[j:j + 1, :], (own, HEAD)) * shares[4][:, j:j + 1]
            for share, block in zip(shares, blocks):
                tot = tot + block.astype(F32) * share[:, j:j + 1]
            for t in range(2):
                at = j // steps * lines + t * steps + j % steps
                att_f[pl.ds(at, 8, stride=8), :] = tot[8 * t:8 * t + 8]
        sl = slice(h * half * own, (h + 1) * half * own)
        att[me, sl] = att_f[sl, :].astype(BF16)
        for i in range(3):
            c = remote(att.at[me, sl], att.at[me, sl], ag_s.at[h, i], ag_r.at[h, i], far[i])
            c.start()
            ag_far.append(c)
        c = remote(att.at[me, sl], att.at[me, sl], ag_s.at[h, 3], ag_r.at[h, 3], sibling)
        c.start()
        ag_near.append(c)

    def products(chunk, sources):
        left = jnp.concatenate(
            [
                jnp.concatenate(
                    [att[2 * f + c, h * lines:(h + 1) * lines] for h in range(heads)], axis=1
                )
                for f in sources for c in range(2)
            ],
            axis=0,
        )
        out = dot_nn(left, w_v[...])
        for m in range(nmp):
            for i in range(len(sources)):
                at = 2 * i * lines + 8 * m
                prod[m, chunk + i] = jnp.concatenate(
                    [out[at:at + 8], out[at + lines:at + lines + 8]], axis=0
                ).astype(BF16)

    mp_copies = []

    def send_products(stage, chunk, width):
        sl = pl.ds(chunk, width)
        for k in range(1, nmp):
            c = remote(
                prod.at[lax.rem(mp + k, nmp), sl], prod_in.at[k - 1, sl],
                mp_s.at[stage, k - 1], mp_r.at[stage, k - 1], mp_dev(k),
            )
            c.start()
            mp_copies.append(c)

    loads[6].wait()
    for c in ag_near:
        c.wait()
    products(0, [chip])
    send_products(0, 0, 1)
    prompt_pieces(1, 0, pairs // 2)
    forward = [
        remote(
            att.at[2 * f + core], att.at[2 * f + core], ag_s.at[2, i], ag_r.at[2, i], sibling
        )
        for i, f in enumerate(from_chip)
    ]
    for i in range(3):
        ag_far[i].wait()
        ag_far[3 + i].wait()
        forward[i].start()
    prompt_pieces(1, pairs // 2, pairs)
    pre_copy = pltpu.make_async_copy(pre_v, pre_h, out_sem)
    pre_copy.start()
    forward[0].wait()
    forward[1].wait()
    products(1, from_chip[:2])
    send_products(1, 1, 2)
    forward[2].wait()
    products(3, from_chip[2:])
    send_products(2, 3, 1)

    for stage, chunks in enumerate(((0,), (1, 2), (3,))):
        for c in mp_copies[stage * (nmp - 1):(stage + 1) * (nmp - 1)]:
            c.wait()
        for chunk in chunks:
            source = ([chip] + from_chip)[chunk]
            value = prod[mp, chunk].astype(F32)
            for k in range(nmp - 1):
                value = value + prod_in[k, chunk].astype(F32)
            for r in range(4):
                for t in range(heads):
                    mix_v[source, r * hs + t * steps:r * hs + (t + 1) * steps] = value[
                        r * steps:(r + 1) * steps, t * 128:(t + 1) * 128
                    ]
    mix_o[...] = mix_v[...].reshape(mix_o.shape).astype(BF16)
    pre_copy.wait()


def hand_over(pre_i, mix_i, pre_o, mix_o, sems):
    copies = [
        pltpu.make_async_copy(pre_i, pre_o, sems.at[0]),
        pltpu.make_async_copy(mix_i, mix_o, sems.at[1]),
    ]
    for c in copies:
        c.start()
    for c in copies:
        c.wait()


def body(
    prompt_queries, prompt_pairs, decode_queries, decode_pairs, cache_pool, out_weight,
    slot_pages, placement, context_len,
):
    nsec, nseq, nmp = (lax.axis_size(a) for a in ("section", "seq", "mp"))
    _, blocks, btok, qwidth = prompt_queries.shape
    _, rows, steps, _ = decode_queries.shape
    slots = cache_pool.shape[1]
    width = out_weight.shape[2]
    heads = qwidth // HEAD
    hs = heads * steps
    own = rows // nseq
    pq = prompt_queries[0]
    pp = prompt_pairs.reshape(blocks * btok * 2, HEAD)
    dq = decode_queries.reshape(rows, steps, heads, HEAD).transpose(0, 2, 1, 3).reshape(rows, hs, HEAD)
    dp = decode_pairs.reshape(rows * steps * 2, HEAD)
    pool = cache_pool.reshape(slots * PAGE * 2, HEAD)
    w = out_weight[0]
    count = slots + own
    any_spec = pl.BlockSpec(memory_space=pl.ANY)
    smem_spec = pl.BlockSpec(memory_space=pltpu.SMEM)
    dma = pltpu.SemaphoreType.DMA
    prefill, mixed = pl.pallas_call(
        functools.partial(kernel, nsec, nseq, nmp, slots, rows, heads, steps),
        out_shape=(
            jax.ShapeDtypeStruct(pq.shape, BF16),
            jax.ShapeDtypeStruct((own * hs, HEAD), BF16),
        ),
        in_specs=[any_spec] * 6 + [smem_spec] * 2,
        out_specs=(any_spec, pl.BlockSpec(memory_space=pltpu.VMEM)),
        scratch_shapes=[
            pltpu.VMEM(pq.shape, BF16),
            pltpu.VMEM(pp.shape, BF16),
            pltpu.VMEM(dq.shape, BF16),
            pltpu.VMEM(dp.shape, BF16),
            pltpu.VMEM(pool.shape, BF16),
            pltpu.VMEM(w.shape, BF16),
            pltpu.VMEM((nseq,) + pp.shape, BF16),
            pltpu.VMEM((hs, HEAD), BF16),
            pltpu.VMEM((hs + 8, HEAD), F32),
            pltpu.VMEM((hs + 8, HEAD), F32),
            pltpu.VMEM((hs, 128), F32),
            pltpu.VMEM((hs, 128), F32),
            pltpu.VMEM((128, 128), F32),
            pltpu.VMEM((3, own, 128), F32),
            pltpu.VMEM((count * hs, HEAD), F32),
            pltpu.VMEM((2, 2, nseq // 2, hs // 2, own, HEAD), BF16),
            pltpu.VMEM((2, nseq // 2, hs // 2, own, HEAD), BF16),
            pltpu.VMEM((2, 3, hs // 2, own, HEAD), BF16),
            pltpu.VMEM((own * hs, HEAD), F32),
            pltpu.VMEM((nseq, own * hs, HEAD), BF16),
            pltpu.VMEM((nmp, 4, 4 * steps, width), BF16),
            pltpu.VMEM((nmp - 1, 4, 4 * steps, width), BF16),
            pltpu.VMEM((4, 4 * hs, HEAD), F32),
            pltpu.VMEM(pq.shape, BF16),
            dma((7,)),
            dma,
            dma((7,)), dma((7,)),
            dma((3,)), dma((3,)),
            dma((2,)), dma((2,)),
            dma((2, 3)), dma((2, 3)),
            dma((3,)), dma((3,)),
            dma((3, 4)), dma((3, 4)),
            dma((3, nmp - 1)), dma((3, nmp - 1)),
        ],
        compiler_params=pltpu.CompilerParams(
            collective_id=0, has_side_effects=True, vmem_limit_bytes=56 * 1024 * 1024
        ),
    )(pq, pp, dq, dp, pool, w, slot_pages, context_len)
    prefill, mixed = pl.pallas_call(
        hand_over,
        out_shape=(
            jax.ShapeDtypeStruct(prefill.shape, BF16), jax.ShapeDtypeStruct(mixed.shape, BF16)
        ),
        in_specs=[any_spec] * 2,
        out_specs=(any_spec,) * 2,
        scratch_shapes=[dma((2,))],
        compiler_params=pltpu.CompilerParams(vmem_limit_bytes=56 * 1024 * 1024),
    )(prefill, mixed)
    mixed = mixed.reshape(own, width // HEAD, steps, HEAD).transpose(0, 2, 1, 3)
    mixed = mixed.reshape(own, steps, width)
    return prefill[None], mixed[None]


def solution(mesh):
    return jax.shard_map(
        body,
        mesh=mesh,
        in_specs=(
            P("section", None, "seq", "mp"),
            P("section", None, "seq", None, "mp"),
            P("section", None, None, "mp"),
            P("section", None, None, None, "mp"),
            P("section", "seq", None, None, "mp"),
            P("section", "mp", "seq"),
            P("seq"),
            P(),
            P(),
        ),
        out_specs=(P("section", None, "seq", "mp"), P("section", "mp", None, "seq")),
        check_vma=False,
    )
```

```python
import functools
import math

import jax
import jax.numpy as jnp
from jax import lax
from jax.experimental import pallas as pl
from jax.experimental.pallas import tpu as pltpu
from jax.sharding import PartitionSpec as P

HEAD = 128
PAGE = 128
MAXP = 1024
BLOCKS = 2
NEG = -1e30
F32 = jnp.float32
BF16 = jnp.bfloat16
MESH = pl.DeviceIdType.MESH
SCALE = 1.0 / (math.sqrt(HEAD) * math.log(2.0))


def dot_nt(a, b):
    return lax.dot_general(a, b, (((1,), (1,)), ((), ())), preferred_element_type=F32)


def dot_nn(a, b, precision=None):
    return lax.dot_general(
        a, b, (((1,), (0,)), ((), ())), preferred_element_type=F32, precision=precision
    )


def iota(shape, dim):
    return lax.broadcasted_iota(jnp.int32, shape, dim)


def kernel(
    nsec, nseq, nmp, slots, rows, heads, steps,
    pq_h, pp_h, dq_h, dp_h, pool_h, w_h, slot_s, ctx_s,
    pre_h, mix_o,
    pq_v, pp_v, dq_v, dp_v, pool_v, w_v, kv, q0, r0_out, r0_in, lse_out, lse_in, lse_t, lse_t_in,
    accs, part, sib_in, part_in, att, prod_f, prod, prod_in, mix_v, pre_v,
    in_sem, out_sem, kv_s, kv_r, z_s, z_r, sib_s, sib_r, rs_s, rs_r, st_s, st_r, ag_s, ag_r, fw_s, fw_r, mp_s, mp_r,
):
    hs = heads * steps
    half = hs // 2
    own = rows // nseq
    chips = nseq // 2
    me = lax.axis_index("seq")
    mp = lax.axis_index("mp")
    sec = lax.axis_index("section")
    chip, core = me // 2, me % 2
    partner = {"section": lax.rem(sec + nsec // 2, nsec)}
    sibling = {"seq": 2 * chip + 1 - core}
    away = (1, 3, 2)
    far_chip = [lax.rem(chip + k, 4) for k in away]
    far = [{"seq": 2 * c + core} for c in far_chip]
    from_chip = [lax.rem(chip + 4 - k, 4) for k in away]

    def mp_dev(k):
        return {"mp": lax.rem(mp + k, nmp)}

    def remote(src, dst, send, recv, device):
        return pltpu.make_async_remote_copy(
            src_ref=src, dst_ref=dst, send_sem=send, recv_sem=recv,
            device_id=device, device_id_type=MESH,
        )

    barrier = pltpu.get_barrier_semaphore()
    greeted = [partner, *far, *(mp_dev(k) for k in range(1, nmp)), sibling]
    for device in greeted:
        pl.semaphore_signal(barrier, inc=1, device_id=device, device_id_type=MESH)

    half_pool = slots * PAGE * 4 // 3
    loads = [
        pltpu.make_async_copy(dq_h, dq_v, in_sem.at[0]),
        pltpu.make_async_copy(pool_h.at[0:half_pool], pool_v.at[0:half_pool], in_sem.at[1]),
        pltpu.make_async_copy(pp_h, pp_v, in_sem.at[2]),
        pltpu.make_async_copy(pool_h.at[half_pool:], pool_v.at[half_pool:], in_sem.at[3]),
        pltpu.make_async_copy(dp_h, dp_v, in_sem.at[4]),
        pltpu.make_async_copy(pq_h, pq_v, in_sem.at[5]),
        pltpu.make_async_copy(w_h, w_v, in_sem.at[6]),
    ]
    for c in loads:
        c.start()

    lane = iota((hs, 128), 1)
    lane1 = iota((8, 128), 1)
    key_lane = iota((hs, 2 * PAGE), 1)
    key_id = jnp.where(key_lane % 2 == 0, key_lane // 2, PAGE)

    def place_of(row):
        return (row % 16) // 2 * 16 + row % 2 * 8 + row // 16

    def merge(state, index, place, m, l):
        top, total, slot_top, slot_place = state
        hit = lane == place
        fresh = jnp.where(hit, jnp.maximum(top, m), top)
        total = total * jnp.exp2((top - fresh) * SCALE) + jnp.where(
            hit, l * jnp.exp2((m - fresh) * SCALE), 0.0
        )
        slot_top = jnp.where(lane == index, m, slot_top)
        slot_place = jnp.where(lane1 == index, place, slot_place)
        return fresh, total, slot_top, slot_place

    def slot_group(g, state, width):
        done = []
        for i in range(width):
            j = g * width + i
            entry = slot_s[j]
            live = entry >= 0
            row = jnp.where(live, entry // MAXP, 0)
            count = jnp.where(live, jnp.clip(ctx_s[row] - (entry % MAXP) * PAGE, 0, PAGE), 0)
            page = pool_v[pl.ds(pl.multiple_of(j * 2 * PAGE, 2 * PAGE), 2 * PAGE), :]
            place = jnp.where(live, place_of(row), -1)
            done.append((j, place, count, page, dot_nt(dq_v[row], page)))
        for j, place, count, page, scores in done:
            allowed = key_id < count
            scores = jnp.where(allowed, scores, NEG)
            m = jnp.max(scores, axis=1, keepdims=True)
            p = jnp.where(allowed, jnp.exp2((scores - m) * SCALE), 0.0)
            l = jnp.sum(p, axis=1, keepdims=True)
            acc = dot_nn(pltpu.roll(p, 1, 1).astype(BF16), page)
            accs[pl.ds(pl.multiple_of(j * hs, hs), hs), :] = acc
            state = merge(state, j, place, m, l)
        return state

    state = (
        jnp.full((hs, 128), NEG, F32), jnp.zeros((hs, 128), F32),
        jnp.full((hs, 128), NEG, F32), jnp.full((8, 128), -1, jnp.int32),
    )
    width = 4
    loads[0].wait()
    loads[1].wait()
    first = slots // width * 2 // 3
    state = lax.fori_loop(0, first, lambda g, s: slot_group(g, s, width), state)

    loads[2].wait()
    ri = iota((2 * PAGE, 2 * PAGE), 0)
    ci = iota((2 * PAGE, 2 * PAGE), 1)
    pick = jnp.where(ci == jnp.where(ri < PAGE, 2 * ri, 2 * (ri - PAGE) + 1), 1.0, 0.0).astype(BF16)
    for b in range(BLOCKS):
        both = dot_nn(pick, pp_v[b * 2 * PAGE:(b + 1) * 2 * PAGE, :]).astype(BF16)
        kv[me, b * PAGE:(b + 1) * PAGE, :] = both[:PAGE]
        kv[me, (BLOCKS + b) * PAGE:(BLOCKS + b + 1) * PAGE, :] = both[PAGE:]

    pl.semaphore_wait(barrier, len(greeted))
    q_out = remote(dq_v.at[0], q0, z_s.at[0], z_r.at[0], partner)
    q_out.start()
    kv_far = [remote(kv.at[me], kv.at[me], kv_s.at[i], kv_r.at[i], far[i]) for i in range(3)]
    for c in kv_far:
        c.start()
    kv_near = [remote(kv.at[me], kv.at[me], kv_s.at[3], kv_r.at[3], sibling)] + [
        remote(kv.at[2 * f + core], kv.at[2 * f + core], kv_s.at[4 + i], kv_r.at[4 + i], sibling)
        for i, f in enumerate(from_chip)
    ]
    kv_near[0].start()

    loads[3].wait()
    state = lax.fori_loop(first, slots // width, lambda g, s: slot_group(g, s, width), state)

    loads[4].wait()
    mine = [16 * m + 2 * me for m in range(nmp)]
    line = 2 * steps
    recent = jnp.concatenate(
        [dp_v[pl.ds(pl.multiple_of(r * line, 2 * line), 2 * line), :] for r in mine], axis=0
    )
    rq = jnp.concatenate([dq_v[pl.ds(r, 2)].reshape(2 * hs, HEAD) for r in mine], axis=0)
    scores = dot_nt(rq, recent)
    ri = iota(scores.shape, 0)
    ci = iota(scores.shape, 1)
    allowed = (
        (ci % 2 == 0) & (ci // line == ri // hs) & ((ci % line) // 2 <= ri % steps)
    )
    scores = jnp.where(allowed, scores, NEG)
    m = jnp.max(scores, axis=1, keepdims=True)
    p = jnp.where(allowed, jnp.exp2((scores - m) * SCALE), 0.0)
    l = jnp.sum(p, axis=1, keepdims=True)
    accs[slots * hs:(slots + own) * hs, :] = dot_nn(pltpu.roll(p, 1, 1).astype(BF16), recent)
    for r in range(own):
        state = merge(
            state, slots + r, me * own + r % 2 * 8 + r // 2,
            m[r * hs:(r + 1) * hs], l[r * hs:(r + 1) * hs],
        )
    top, total, slot_top, slot_place = state
    lse_mine = jnp.where(
        total > 0.0, top * SCALE + jnp.log2(jnp.maximum(total, 1e-30)), NEG
    )
    lse_out[...] = lse_mine
    lse_copy = remote(lse_out, lse_in, z_s.at[2], z_r.at[2], sibling)
    lse_copy.start()
    place_pick = jnp.where(
        iota((128, 128), 0) == jnp.broadcast_to(slot_place[0:1], (128, 128)), 1.0, 0.0
    )
    lse_copy.wait()
    peak = jnp.maximum(lse_mine, lse_in[...])
    lse_chip = peak + jnp.log2(jnp.exp2(lse_mine - peak) + jnp.exp2(lse_in[...] - peak))
    whole_slot = dot_nn(lse_chip, place_pick, lax.Precision.HIGHEST)
    factor = jnp.exp2(slot_top * SCALE - whole_slot)
    lse_t[...] = jnp.concatenate([lse_chip, jnp.zeros((128 - hs, 128), F32)], axis=0).T

    count = accs.shape[0] // hs

    def row_sums(j):
        weights = (place_pick * jnp.broadcast_to(factor[j:j + 1], (128, 128)))[:rows, :count]
        return dot_nn(weights.astype(BF16), accs[pl.ds(j, count, stride=hs), :].astype(BF16))

    for i in range(half):
        even, odd = row_sums(2 * i), row_sums(2 * i + 1)
        for s in range(nseq):
            for t in range(2):
                sl = slice(s * own + 8 * t, s * own + 8 * t + 8)
                part[t, s % 2, s // 2, i] = jnp.concatenate([even[sl], odd[sl]], axis=0).astype(BF16)
    order = (1, 0)
    sib_copies = [
        remote(part.at[t, 1 - core], sib_in.at[t], sib_s.at[t], sib_r.at[t], sibling)
        for t in range(2)
    ]
    for t in order:
        sib_copies[t].start()

    st_copies = [
        remote(
            lse_t.at[pl.ds(pl.multiple_of((2 * f + core) * own, own), own)], lse_t_in.at[i],
            st_s.at[i], st_r.at[i], far[i],
        )
        for i, f in enumerate(far_chip)
    ]
    rs_copies = [
        [
            remote(part.at[t, core, f], part_in.at[t, i], rs_s.at[t, i], rs_r.at[t, i], far[i])
            for i, f in enumerate(far_chip)
        ]
        for t in range(2)
    ]
    for t in order:
        sib_copies[t].wait()
        for i, f in enumerate(far_chip + [chip]):
            for at in range(0, half, 4):
                sl = slice(at, at + 4)
                part[t, core, f, sl] = (
                    part[t, core, f, sl].astype(F32) + sib_in[t, f, sl].astype(F32)
                ).astype(BF16)
            if i < 3:
                rs_copies[t][i].start()
        if t == order[0]:
            for c in st_copies:
                c.start()

    for i in range(3):
        kv_far[i].wait()
        kv_near[i + 1].start()
    for c in kv_near:
        c.wait()
    loads[5].wait()
    n = nseq * PAGE

    def prompt_keys(b):
        return kv[:, b * PAGE:(b + 1) * PAGE, :].reshape(n, HEAD)

    def prompt_values(b):
        return kv[:, (BLOCKS + b) * PAGE:(BLOCKS + b + 1) * PAGE, :].reshape(n, HEAD)

    q_out.wait()
    s0 = []
    for b in range(BLOCKS):
        scores = dot_nt(q0[...], prompt_keys(b))
        s0.append(jnp.where(iota(scores.shape, 1) + b * n < ctx_s[0], scores, NEG))
    m = functools.reduce(jnp.maximum, [jnp.max(x, axis=1, keepdims=True) for x in s0])
    p0 = [jnp.exp2((x - m) * SCALE) for x in s0]
    l = sum(jnp.sum(p, axis=1, keepdims=True) for p in p0)
    acc = sum(dot_nn(p.astype(BF16), prompt_values(b)) for b, p in enumerate(p0))
    r0_out[0:hs, :] = acc / l
    lse_prompt = jnp.broadcast_to(m * SCALE + jnp.log2(l), (hs, 128))
    r0_out[hs:hs + 8, :] = jnp.concatenate(
        [lse_prompt, jnp.zeros((128 - hs, 128), F32)], axis=0
    ).T[0:8]
    r0_copy = remote(r0_out, r0_in, z_s.at[1], z_r.at[1], partner)
    r0_copy.start()

    def prompt_piece(b, pair):
        two = pq_v[b, :, pl.ds(pl.multiple_of(pair * 2 * HEAD, 2 * HEAD), 2 * HEAD)]
        q = jnp.concatenate([two[:, :HEAD], two[:, HEAD:]], axis=0)
        s_own = dot_nt(q, prompt_keys(b))
        limit = me * PAGE + iota((2 * PAGE, n), 0) % PAGE
        s_own = jnp.where(iota((2 * PAGE, n), 1) <= limit, s_own, NEG)
        m = jnp.max(s_own, axis=1, keepdims=True)
        if b:
            s_old = dot_nt(q, prompt_keys(0))
            m = jnp.maximum(m, jnp.max(s_old, axis=1, keepdims=True))
        p = jnp.exp2((s_own - m) * SCALE)
        l = jnp.sum(p, axis=1, keepdims=True)
        o = dot_nn(p.astype(BF16), prompt_values(b))
        if b:
            p = jnp.exp2((s_old - m) * SCALE)
            l = l + jnp.sum(p, axis=1, keepdims=True)
            o = o + dot_nn(p.astype(BF16), prompt_values(0))
        o = (o / l).astype(BF16)
        pre_v[b, :, pl.ds(pl.multiple_of(pair * 2 * HEAD, 2 * HEAD), 2 * HEAD)] = jnp.concatenate(
            [o[:PAGE], o[PAGE:]], axis=1
        )

    def prompt_pieces(b, lo, hi):
        def step(i, carry):
            prompt_piece(b, i)
            return carry

        lax.fori_loop(lo, hi, step, 0)

    pairs = heads // 2
    prompt_pieces(0, 0, pairs // 2)

    for c in st_copies:
        c.wait()
    ag_far = []
    ag_near = []
    lines = 8 * steps

    def shares_of(terms):
        peak = functools.reduce(jnp.maximum, terms)
        whole = peak + jnp.log2(sum(jnp.exp2(t - peak) for t in terms))
        return [jnp.exp2(t - whole) for t in terms]

    def finish(t):
        sl = slice(8 * t, 8 * t + 8)
        mine_t = lse_t[pl.ds(pl.multiple_of(me * own + 8 * t, 8), 8), :]
        terms = [mine_t] + [lse_t_in[i, sl] for i in range(3)]
        if t == 0:
            r0_copy.wait()
            first_row = (iota((8, 128), 0) == 0) & (me == 0)
            terms.append(jnp.where(first_row, jnp.broadcast_to(r0_in[hs:hs + 1, :], (8, 128)), NEG))
        shares = shares_of(terms)
        for c in rs_copies[t]:
            c.wait()
        for i in range(half):
            blocks = [part[t, core, chip, i]] + [part_in[t, k, i] for k in range(3)]
            blocks = [b.astype(F32) for b in blocks]
            two = []
            for j in range(2):
                at = 2 * i + j
                tot = sum(
                    b[8 * j:8 * j + 8] * share[:, at:at + 1] for b, share in zip(blocks, shares)
                )
                if t == 0:
                    tot = tot + jnp.broadcast_to(r0_in[at:at + 1, :], (8, HEAD)) * shares[4][:, at:at + 1]
                two.append(tot)
            att[t, me, 16 * i:16 * i + 16] = jnp.concatenate(two, axis=0).astype(BF16)
        block = att.at[t, me]
        c = remote(block, block, ag_s.at[t, 3], ag_r.at[t, 3], sibling)
        c.start()
        ag_near.append(c)
        group = [remote(block, block, ag_s.at[t, i], ag_r.at[t, i], far[i]) for i in range(3)]
        for c in group:
            c.start()
        ag_far.append(group)

    finish(order[0])
    prompt_pieces(0, pairs // 2, pairs)
    finish(order[1])

    half_cols = w_v.shape[1] // 2

    def products(first_unit, sources):
        left = jnp.concatenate(
            [
                jnp.concatenate(
                    [att[t, 2 * f + c, h * lines:(h + 1) * lines] for h in range(heads)], axis=1
                )
                for t, f in sources for c in range(2)
            ],
            axis=0,
        )
        out = dot_nn(left, w_v[...])
        for k in range(heads):
            prod_f[k, 0:2 * lines * len(sources), :] = out[:, 128 * k:128 * (k + 1)]
        for i in range(len(sources)):
            for m in range(nmp):
                value = jnp.concatenate(
                    [
                        prod_f[k, pl.ds(2 * lines * i + m, 8, stride=8), :]
                        for k in range(heads)
                    ],
                    axis=1,
                )
                prod[m, first_unit + i] = jnp.concatenate(
                    [value[:, :half_cols], value[:, half_cols:]], axis=0
                ).astype(BF16)

    mp_copies = []

    def send_products(stage, first_unit, units):
        sl = pl.ds(first_unit, units)
        for k in range(1, nmp):
            c = remote(
                prod.at[lax.rem(mp + k, nmp), sl], prod_in.at[k - 1, sl],
                mp_s.at[stage, k - 1], mp_r.at[stage, k - 1], mp_dev(k),
            )
            c.start()
            mp_copies.append(c)

    loads[6].wait()
    for c in ag_near:
        c.wait()
    products(0, [(t, chip) for t in order])
    send_products(0, 0, 2)
    for turn, t in enumerate(order):
        forward = []
        for i, f in enumerate(from_chip):
            ag_far[turn][i].wait()
            block = att.at[t, 2 * f + core]
            c = remote(block, block, fw_s.at[t, i], fw_r.at[t, i], sibling)
            c.start()
            forward.append(c)
        for c in forward:
            c.wait()
        products(2 + 3 * turn, [(t, f) for f in from_chip])
        send_products(1 + turn, 2 + 3 * turn, 3)
        prompt_pieces(1, turn * pairs // 2, (turn + 1) * pairs // 2)
    pre_copy = pltpu.make_async_copy(pre_v, pre_h, out_sem)
    pre_copy.start()

    units = [(t, chip) for t in order] + [(t, f) for t in order for f in from_chip]
    for stage, (lo, hi) in enumerate(((0, 2), (2, 5), (5, 8))):
        for c in mp_copies[stage * (nmp - 1):(stage + 1) * (nmp - 1)]:
            c.wait()
        for unit in range(lo, hi):
            t, source = units[unit]
            value = prod[mp, unit].astype(F32)
            for k in range(nmp - 1):
                value = value + prod_in[k, unit].astype(F32)
            for c in range(2):
                for k in range(heads):
                    at = (2 * c + t) * hs + k * steps
                    row = k // (heads // 2) * 8 + c * steps
                    col = k % (heads // 2) * 128
                    mix_v[source, at:at + steps] = value[row:row + steps, col:col + 128]
    mix_o[...] = mix_v[...].reshape(mix_o.shape).astype(BF16)
    pre_copy.wait()


def hand_over(pre_i, mix_i, pre_o, mix_o, sems):
    copies = [
        pltpu.make_async_copy(pre_i, pre_o, sems.at[0]),
        pltpu.make_async_copy(mix_i, mix_o, sems.at[1]),
    ]
    for c in copies:
        c.start()
    for c in copies:
        c.wait()


def body(
    prompt_queries, prompt_pairs, decode_queries, decode_pairs, cache_pool, out_weight,
    slot_pages, placement, context_len,
):
    nsec, nseq, nmp = (lax.axis_size(a) for a in ("section", "seq", "mp"))
    _, blocks, btok, qwidth = prompt_queries.shape
    _, rows, steps, _ = decode_queries.shape
    slots = cache_pool.shape[1]
    width = out_weight.shape[2]
    heads = qwidth // HEAD
    hs = heads * steps
    own = rows // nseq
    pq = prompt_queries[0]
    pp = prompt_pairs.reshape(blocks * btok * 2, HEAD)
    dq = decode_queries.reshape(rows, steps, heads, HEAD).transpose(0, 2, 1, 3).reshape(rows, hs, HEAD)
    dp = decode_pairs.reshape(rows * steps * 2, HEAD)
    pool = cache_pool.reshape(slots * PAGE * 2, HEAD)
    w = out_weight[0]
    count = slots + own
    any_spec = pl.BlockSpec(memory_space=pl.ANY)
    smem_spec = pl.BlockSpec(memory_space=pltpu.SMEM)
    dma = pltpu.SemaphoreType.DMA
    prefill, mixed = pl.pallas_call(
        functools.partial(kernel, nsec, nseq, nmp, slots, rows, heads, steps),
        out_shape=(
            jax.ShapeDtypeStruct(pq.shape, BF16),
            jax.ShapeDtypeStruct((own * hs, HEAD), BF16),
        ),
        in_specs=[any_spec] * 6 + [smem_spec] * 2,
        out_specs=(any_spec, pl.BlockSpec(memory_space=pltpu.VMEM)),
        scratch_shapes=[
            pltpu.VMEM(pq.shape, BF16),
            pltpu.VMEM(pp.shape, BF16),
            pltpu.VMEM(dq.shape, BF16),
            pltpu.VMEM(dp.shape, BF16),
            pltpu.VMEM(pool.shape, BF16),
            pltpu.VMEM(w.shape, BF16),
            pltpu.VMEM((nseq,) + pp.shape, BF16),
            pltpu.VMEM((hs, HEAD), BF16),
            pltpu.VMEM((hs + 8, HEAD), F32),
            pltpu.VMEM((hs + 8, HEAD), F32),
            pltpu.VMEM((hs, 128), F32),
            pltpu.VMEM((hs, 128), F32),
            pltpu.VMEM((128, 128), F32),
            pltpu.VMEM((3, own, 128), F32),
            pltpu.VMEM((count * hs, HEAD), F32),
            pltpu.VMEM((2, 2, nseq // 2, hs // 2, own, HEAD), BF16),
            pltpu.VMEM((2, nseq // 2, hs // 2, own, HEAD), BF16),
            pltpu.VMEM((2, 3, hs // 2, own, HEAD), BF16),
            pltpu.VMEM((2, nseq, own * hs // 2, HEAD), BF16),
            pltpu.VMEM((width // 128, 48 * steps, 128), F32),
            pltpu.VMEM((nmp, 8, 16, width // 2), BF16),
            pltpu.VMEM((nmp - 1, 8, 16, width // 2), BF16),
            pltpu.VMEM((4, 4 * hs, HEAD), F32),
            pltpu.VMEM(pq.shape, BF16),
            dma((7,)),
            dma,
            dma((7,)), dma((7,)),
            dma((3,)), dma((3,)),
            dma((2,)), dma((2,)),
            dma((2, 3)), dma((2, 3)),
            dma((3,)), dma((3,)),
            dma((2, 4)), dma((2, 4)),
            dma((2, 3)), dma((2, 3)),
            dma((3, nmp - 1)), dma((3, nmp - 1)),
        ],
        compiler_params=pltpu.CompilerParams(
            collective_id=0, has_side_effects=True, vmem_limit_bytes=56 * 1024 * 1024
        ),
    )(pq, pp, dq, dp, pool, w, slot_pages, context_len)
    prefill, mixed = pl.pallas_call(
        hand_over,
        out_shape=(
            jax.ShapeDtypeStruct(prefill.shape, BF16), jax.ShapeDtypeStruct(mixed.shape, BF16)
        ),
        in_specs=[pl.BlockSpec(memory_space=pltpu.VMEM)] * 2,
        out_specs=(any_spec,) * 2,
        scratch_shapes=[dma((2,))],
    )(prefill, mixed)
    mixed = mixed.reshape(own, width // HEAD, steps, HEAD).transpose(0, 2, 1, 3)
    mixed = mixed.reshape(own, steps, width)
    return prefill[None], mixed[None]


def solution(mesh):
    return jax.shard_map(
        body,
        mesh=mesh,
        in_specs=(
            P("section", None, "seq", "mp"),
            P("section", None, "seq", None, "mp"),
            P("section", None, None, "mp"),
            P("section", None, None, None, "mp"),
            P("section", "seq", None, None, "mp"),
            P("section", "mp", "seq"),
            P("seq"),
            P(),
            P(),
        ),
        out_specs=(P("section", None, "seq", "mp"), P("section", "mp", None, "seq")),
        check_vma=False,
    )
```

```python
import functools
import math

import jax
import jax.numpy as jnp
from jax import lax
from jax.experimental import pallas as pl
from jax.experimental.pallas import tpu as pltpu
from jax.sharding import PartitionSpec as P

HEAD = 128
PAGE = 128
MAXP = 1024
BLOCKS = 2
NEG = -1e30
F32 = jnp.float32
BF16 = jnp.bfloat16
MESH = pl.DeviceIdType.MESH
SCALE = 1.0 / (math.sqrt(HEAD) * math.log(2.0))


def dot_nt(a, b):
    return lax.dot_general(a, b, (((1,), (1,)), ((), ())), preferred_element_type=F32)


def dot_nn(a, b, precision=None):
    return lax.dot_general(
        a, b, (((1,), (0,)), ((), ())), preferred_element_type=F32, precision=precision
    )


def iota(shape, dim):
    return lax.broadcasted_iota(jnp.int32, shape, dim)


def kernel(
    nsec, nseq, nmp, slots, rows, heads, steps,
    pq_h, pp_h, dq_h, dp_h, pool_h, w_h, slot_s, ctx_s,
    pre_h, mix_o,
    pq_v, pp_v, dq_v, dp_v, pool_v, w_v, kv, q0, r0_out, r0_in, r0_mix, r0_mix_in,
    lse_out, lse_in, lse_t, lse_t_in,
    accs, part, sib_in, part_in, att, prod_f, prod, prod_in, mix_v, pre_v,
    in_sem, out_sem, kv_s, kv_r, z_s, z_r, r0_s, r0_r, sib_s, sib_r, rs_s, rs_r, st_s, st_r, ag_s, ag_r, fw_s, fw_r, mp_s, mp_r,
):
    hs = heads * steps
    half = hs // 2
    own = rows // nseq
    chips = nseq // 2
    me = lax.axis_index("seq")
    mp = lax.axis_index("mp")
    sec = lax.axis_index("section")
    chip, core = me // 2, me % 2
    next_sec = {"section": lax.rem(sec + 1, nsec)}
    last_sec = {"section": lax.rem(sec + nsec - 1, nsec)}
    sibling = {"seq": 2 * chip + 1 - core}
    away = (1, 3, 2)
    far_chip = [lax.rem(chip + k, 4) for k in away]
    far = [{"seq": 2 * c + core} for c in far_chip]
    from_chip = [lax.rem(chip + 4 - k, 4) for k in away]

    def mp_dev(k):
        return {"mp": lax.rem(mp + k, nmp)}

    def remote(src, dst, send, recv, device):
        return pltpu.make_async_remote_copy(
            src_ref=src, dst_ref=dst, send_sem=send, recv_sem=recv,
            device_id=device, device_id_type=MESH,
        )

    barrier = pltpu.get_barrier_semaphore()
    greeted = [*(mp_dev(k) for k in range(1, nmp)), next_sec, last_sec, *far, sibling]
    for device in greeted:
        pl.semaphore_signal(barrier, inc=1, device_id=device, device_id_type=MESH)

    width = 12
    groups = slots // width
    group_lines = width * 2 * PAGE

    def pool_load(g):
        sl = slice(g * group_lines, (g + 1) * group_lines)
        return pltpu.make_async_copy(pool_h.at[sl], pool_v.at[sl], in_sem.at[5 + g])

    load_dq = pltpu.make_async_copy(dq_h, dq_v, in_sem.at[0])
    load_dp = pltpu.make_async_copy(dp_h, dp_v, in_sem.at[1])
    load_pp = pltpu.make_async_copy(pp_h, pp_v, in_sem.at[2])
    load_pq = pltpu.make_async_copy(pq_h, pq_v, in_sem.at[3])
    load_w = pltpu.make_async_copy(w_h, w_v, in_sem.at[4])
    load_pool = [pool_load(g) for g in range(groups)]
    for c in [load_dq, *load_pool, load_dp, load_pp, load_pq, load_w]:
        c.start()

    lane = iota((hs, 128), 1)
    lane1 = iota((8, 128), 1)
    key_lane = iota((hs, 2 * PAGE), 1)
    key_id = jnp.where(key_lane % 2 == 0, key_lane // 2, PAGE)

    def place_of(row):
        return (row % 16) // 2 * 16 + row % 2 * 8 + row // 16

    def merge(state, index, place, m, l):
        top, total, slot_top, slot_place = state
        hit = lane == place
        fresh = jnp.where(hit, jnp.maximum(top, m), top)
        total = total * jnp.exp2((top - fresh) * SCALE) + jnp.where(
            hit, l * jnp.exp2((m - fresh) * SCALE), 0.0
        )
        slot_top = jnp.where(lane == index, m, slot_top)
        slot_place = jnp.where(lane1 == index, place, slot_place)
        return fresh, total, slot_top, slot_place

    def slot_group(g, state, width):
        done = []
        for i in range(width):
            j = g * width + i
            entry = slot_s[j]
            live = entry >= 0
            row = jnp.where(live, entry // MAXP, 0)
            count = jnp.where(live, jnp.clip(ctx_s[row] - (entry % MAXP) * PAGE, 0, PAGE), 0)
            page = pool_v[pl.ds(pl.multiple_of(j * 2 * PAGE, 2 * PAGE), 2 * PAGE), :]
            place = jnp.where(live, place_of(row), -1)
            done.append((j, place, count, page, dot_nt(dq_v[row], page)))
        for j, place, count, page, scores in done:
            allowed = key_id < count
            scores = jnp.where(allowed, scores, NEG)
            m = jnp.max(scores, axis=1, keepdims=True)
            p = jnp.where(allowed, jnp.exp2((scores - m) * SCALE), 0.0)
            l = jnp.sum(p, axis=1, keepdims=True)
            acc = dot_nn(pltpu.roll(p, 1, 1).astype(BF16), page)
            accs[pl.ds(pl.multiple_of(j * hs, hs), hs), :] = acc
            state = merge(state, j, place, m, l)
        return state

    state = (
        jnp.full((hs, 128), NEG, F32), jnp.zeros((hs, 128), F32),
        jnp.full((hs, 128), NEG, F32), jnp.full((8, 128), -1, jnp.int32),
    )
    load_dq.wait()
    for g in range(groups):
        load_pool[g].wait()
        state = slot_group(g, state, width)

    load_pp.wait()
    ri = iota((2 * PAGE, 2 * PAGE), 0)
    ci = iota((2 * PAGE, 2 * PAGE), 1)
    pick = jnp.where(ci == jnp.where(ri < PAGE, 2 * ri, 2 * (ri - PAGE) + 1), 1.0, 0.0).astype(BF16)
    for b in range(BLOCKS):
        both = dot_nn(pick, pp_v[b * 2 * PAGE:(b + 1) * 2 * PAGE, :]).astype(BF16)
        kv[me, b * PAGE:(b + 1) * PAGE, :] = both[:PAGE]
        kv[me, (BLOCKS + b) * PAGE:(BLOCKS + b + 1) * PAGE, :] = both[PAGE:]

    load_dp.wait()
    mine = [16 * m + 2 * me for m in range(nmp)]
    line = 2 * steps
    recent = jnp.concatenate(
        [dp_v[pl.ds(pl.multiple_of(r * line, 2 * line), 2 * line), :] for r in mine], axis=0
    )
    rq = jnp.concatenate([dq_v[pl.ds(r, 2)].reshape(2 * hs, HEAD) for r in mine], axis=0)
    scores = dot_nt(rq, recent)
    ri = iota(scores.shape, 0)
    ci = iota(scores.shape, 1)
    allowed = (
        (ci % 2 == 0) & (ci // line == ri // hs) & ((ci % line) // 2 <= ri % steps)
    )
    scores = jnp.where(allowed, scores, NEG)
    m = jnp.max(scores, axis=1, keepdims=True)
    p = jnp.where(allowed, jnp.exp2((scores - m) * SCALE), 0.0)
    l = jnp.sum(p, axis=1, keepdims=True)
    accs[slots * hs:(slots + own) * hs, :] = dot_nn(pltpu.roll(p, 1, 1).astype(BF16), recent)
    for r in range(own):
        state = merge(
            state, slots + r, me * own + r % 2 * 8 + r // 2,
            m[r * hs:(r + 1) * hs], l[r * hs:(r + 1) * hs],
        )
    top, total, slot_top, slot_place = state
    lse_mine = jnp.where(
        total > 0.0, top * SCALE + jnp.log2(jnp.maximum(total, 1e-30)), NEG
    )
    lse_out[...] = lse_mine
    scores = dot_nt(dq_v[0], dp_v[0:2 * line, :])
    ci = iota(scores.shape, 1)
    allowed = (ci % 2 == 0) & (ci < line) & (ci // 2 <= iota(scores.shape, 0) % steps)
    scores = jnp.where(allowed, scores, NEG)
    row0_m = jnp.max(scores, axis=1, keepdims=True)
    p = jnp.where(allowed, jnp.exp2((scores - row0_m) * SCALE), 0.0)
    row0_l = jnp.sum(p, axis=1, keepdims=True)
    p = jnp.concatenate([jnp.zeros((hs, 1), F32), p[:, :2 * line - 1]], axis=1)
    row0_acc = dot_nn(p.astype(BF16), dp_v[0:2 * line, :])

    pl.semaphore_wait(barrier, len(greeted))
    lse_copy = remote(lse_out, lse_in, z_s.at[0], z_r.at[0], sibling)
    lse_copy.start()
    q_first = remote(dq_v.at[0], q0.at[0], z_s.at[1], z_r.at[1], next_sec)
    q_second = remote(q0.at[0], q0.at[1], z_s.at[2], z_r.at[2], next_sec)
    q_first.start()
    kv_far = [remote(kv.at[me], kv.at[me], kv_s.at[i], kv_r.at[i], far[i]) for i in range(3)]
    for c in kv_far:
        c.start()
    kv_near = [remote(kv.at[me], kv.at[me], kv_s.at[3], kv_r.at[3], sibling)] + [
        remote(kv.at[2 * f + core], kv.at[2 * f + core], kv_s.at[4 + i], kv_r.at[4 + i], sibling)
        for i, f in enumerate(from_chip)
    ]
    kv_near[0].start()
    place_pick = jnp.where(
        iota((128, 128), 0) == jnp.broadcast_to(slot_place[0:1], (128, 128)), 1.0, 0.0
    )
    lse_copy.wait()
    peak = jnp.maximum(lse_mine, lse_in[...])
    lse_chip = peak + jnp.log2(jnp.exp2(lse_mine - peak) + jnp.exp2(lse_in[...] - peak))
    whole_slot = dot_nn(lse_chip, place_pick, lax.Precision.HIGHEST)
    factor = jnp.exp2(slot_top * SCALE - whole_slot)
    lse_t[...] = jnp.concatenate([lse_chip, jnp.zeros((128 - hs, 128), F32)], axis=0).T

    count = accs.shape[0] // hs

    def row_sums(j):
        weights = (place_pick * jnp.broadcast_to(factor[j:j + 1], (128, 128)))[:rows, :count]
        return dot_nn(weights.astype(BF16), accs[pl.ds(j, count, stride=hs), :].astype(BF16))

    for i in range(half):
        even, odd = row_sums(2 * i), row_sums(2 * i + 1)
        for s in range(nseq):
            for t in range(2):
                sl = slice(s * own + 8 * t, s * own + 8 * t + 8)
                part[t, s % 2, s // 2, i] = jnp.concatenate([even[sl], odd[sl]], axis=0).astype(BF16)
    order = (1, 0)
    sib_copies = [
        remote(part.at[t, 1 - core], sib_in.at[t], sib_s.at[t], sib_r.at[t], sibling)
        for t in range(2)
    ]
    for t in order:
        sib_copies[t].start()

    st_copies = [
        remote(
            lse_t.at[pl.ds(pl.multiple_of((2 * f + core) * own, own), own)], lse_t_in.at[i],
            st_s.at[i], st_r.at[i], far[i],
        )
        for i, f in enumerate(far_chip)
    ]
    rs_copies = [
        [
            remote(part.at[t, core, f], part_in.at[t, i], rs_s.at[t, i], rs_r.at[t, i], far[i])
            for i, f in enumerate(far_chip)
        ]
        for t in range(2)
    ]
    for t in order:
        sib_copies[t].wait()
        for i, f in enumerate(far_chip + [chip]):
            for at in range(0, half, 4):
                sl = slice(at, at + 4)
                part[t, core, f, sl] = (
                    part[t, core, f, sl].astype(F32) + sib_in[t, f, sl].astype(F32)
                ).astype(BF16)
            if i < 3:
                rs_copies[t][i].start()
        if t == order[0]:
            for c in st_copies:
                c.start()

    q_first.wait()
    q_second.start()

    for i in range(3):
        kv_far[i].wait()
        kv_near[i + 1].start()
    for c in kv_near:
        c.wait()
    load_pq.wait()
    n = nseq * PAGE

    def prompt_keys(b):
        return kv[:, b * PAGE:(b + 1) * PAGE, :].reshape(n, HEAD)

    def prompt_values(b):
        return kv[:, (BLOCKS + b) * PAGE:(BLOCKS + b + 1) * PAGE, :].reshape(n, HEAD)

    q_second.wait()
    s0 = []
    for b in range(BLOCKS):
        scores = dot_nt(q0[1], prompt_keys(b))
        s0.append(jnp.where(iota(scores.shape, 1) + b * n < ctx_s[0], scores, NEG))
    m = functools.reduce(jnp.maximum, [jnp.max(x, axis=1, keepdims=True) for x in s0])
    p0 = [jnp.exp2((x - m) * SCALE) for x in s0]
    l = sum(jnp.sum(p, axis=1, keepdims=True) for p in p0)
    r0_out[0:hs, :] = sum(dot_nn(p.astype(BF16), prompt_values(b)) for b, p in enumerate(p0))
    r0_out[hs:2 * hs, :] = jnp.where(lane == 0, m, l)
    r0_first = remote(r0_out, r0_in.at[0], z_s.at[3], z_r.at[3], next_sec)
    r0_second = remote(r0_in.at[0], r0_in.at[1], z_s.at[4], z_r.at[4], next_sec)
    r0_first.start()

    def prompt_piece(b, pair):
        two = pq_v[b, :, pl.ds(pl.multiple_of(pair * 2 * HEAD, 2 * HEAD), 2 * HEAD)]
        q = jnp.concatenate([two[:, :HEAD], two[:, HEAD:]], axis=0)
        s_own = dot_nt(q, prompt_keys(b))
        limit = me * PAGE + iota((2 * PAGE, n), 0) % PAGE
        s_own = jnp.where(iota((2 * PAGE, n), 1) <= limit, s_own, NEG)
        m = jnp.max(s_own, axis=1, keepdims=True)
        if b:
            s_old = dot_nt(q, prompt_keys(0))
            m = jnp.maximum(m, jnp.max(s_old, axis=1, keepdims=True))
        p = jnp.exp2((s_own - m) * SCALE)
        l = jnp.sum(p, axis=1, keepdims=True)
        o = dot_nn(p.astype(BF16), prompt_values(b))
        if b:
            p = jnp.exp2((s_old - m) * SCALE)
            l = l + jnp.sum(p, axis=1, keepdims=True)
            o = o + dot_nn(p.astype(BF16), prompt_values(0))
        o = (o / l).astype(BF16)
        pre_v[b, :, pl.ds(pl.multiple_of(pair * 2 * HEAD, 2 * HEAD), 2 * HEAD)] = jnp.concatenate(
            [o[:PAGE], o[PAGE:]], axis=1
        )

    def prompt_pieces(b, lo, hi):
        def step(i, carry):
            prompt_piece(b, i)
            return carry

        lax.fori_loop(lo, hi, step, 0)

    pairs = heads // 2
    prompt_pieces(0, 0, 1)

    for c in st_copies:
        c.wait()
    ag_far = []
    ag_near = []
    lines = 8 * steps

    def shares_of(terms):
        peak = functools.reduce(jnp.maximum, terms)
        whole = peak + jnp.log2(sum(jnp.exp2(t - peak) for t in terms))
        return [jnp.exp2(t - whole) for t in terms]

    def finish(t):
        sl = slice(8 * t, 8 * t + 8)
        mine_t = lse_t[pl.ds(pl.multiple_of(me * own + 8 * t, 8), 8), :]
        terms = [mine_t] + [lse_t_in[i, sl] for i in range(3)]
        shares = shares_of(terms)
        for c in rs_copies[t]:
            c.wait()
        for i in range(half):
            blocks = [part[t, core, chip, i]] + [part_in[t, k, i] for k in range(3)]
            blocks = [b.astype(F32) for b in blocks]
            two = []
            for j in range(2):
                at = 2 * i + j
                tot = sum(
                    b[8 * j:8 * j + 8] * share[:, at:at + 1] for b, share in zip(blocks, shares)
                )
                two.append(tot)
            att[t, me, 16 * i:16 * i + 16] = jnp.concatenate(two, axis=0).astype(BF16)
        block = att.at[t, me]
        c = remote(block, block, ag_s.at[t, 3], ag_r.at[t, 3], sibling)
        c.start()
        ag_near.append(c)
        group = [remote(block, block, ag_s.at[t, i], ag_r.at[t, i], far[i]) for i in range(3)]
        for c in group:
            c.start()
        ag_far.append(group)

    half_cols = w_v.shape[1] // 2

    def products(first_unit, sources):
        left = jnp.concatenate(
            [
                jnp.concatenate(
                    [att[t, 2 * f + c, h * lines:(h + 1) * lines] for h in range(heads)], axis=1
                )
                for t, f in sources for c in range(2)
            ],
            axis=0,
        )
        out = dot_nn(left, w_v[...])
        for k in range(heads):
            prod_f[k, 0:2 * lines * len(sources), :] = out[:, 128 * k:128 * (k + 1)]
        for i in range(len(sources)):
            for m in range(nmp):
                value = jnp.concatenate(
                    [
                        prod_f[k, pl.ds(2 * lines * i + m, 8, stride=8), :]
                        for k in range(heads)
                    ],
                    axis=1,
                )
                prod[m, first_unit + i] = jnp.concatenate(
                    [value[:, :half_cols], value[:, half_cols:]], axis=0
                ).astype(BF16)

    mp_copies = []

    def send_products(stage, first_unit, units):
        sl = pl.ds(first_unit, units)
        for k in range(1, nmp):
            c = remote(
                prod.at[lax.rem(mp + k, nmp), sl], prod_in.at[k - 1, sl],
                mp_s.at[stage, k - 1], mp_r.at[stage, k - 1], mp_dev(k),
            )
            c.start()
            mp_copies.append(c)

    def forward_rows(turn):
        copies = []
        for i, f in enumerate(from_chip):
            ag_far[turn][i].wait()
            block = att.at[order[turn], 2 * f + core]
            c = remote(block, block, fw_s.at[turn, i], fw_r.at[turn, i], sibling)
            c.start()
            copies.append(c)
        return copies

    finish(order[0])
    load_w.wait()
    ag_near[0].wait()
    products(0, [(order[0], chip)])
    send_products(0, 0, 1)
    r0_first.wait()
    r0_second.start()
    finish(order[1])
    prompt_pieces(0, 1, 2)
    ag_near[1].wait()
    products(1, [(order[1], chip)])
    send_products(1, 1, 1)
    prompt_pieces(0, 2, 3)
    forward = forward_rows(0)
    prompt_pieces(0, 3, pairs)
    for c in forward:
        c.wait()
    products(2, [(order[0], f) for f in from_chip])
    send_products(2, 2, 3)
    forward = forward_rows(1)

    r0_second.wait()
    prompt_m, prompt_l = r0_in[1, hs:2 * hs, 0:1], r0_in[1, hs:2 * hs, 1:2]
    peak = jnp.maximum(row0_m, prompt_m)
    keep = jnp.exp2((row0_m - peak) * SCALE)
    more = jnp.exp2((prompt_m - peak) * SCALE)
    row0 = (row0_acc * keep + r0_in[1, 0:hs, :] * more) / (row0_l * keep + prompt_l * more)
    row0 = jnp.concatenate([row0[h * steps:(h + 1) * steps] for h in range(heads)], axis=1)
    row0 = jnp.concatenate([row0, jnp.zeros((16 - steps, row0.shape[1]), F32)], axis=0)
    row0 = dot_nn(row0.astype(BF16), w_v[...])[0:8]
    row0 = jnp.concatenate([row0[:, :half_cols], row0[:, half_cols:]], axis=0)
    r0_mix[...] = row0.astype(BF16)

    def row0_copy(k):
        return remote(r0_mix, r0_mix_in.at[k - 1], r0_s.at[k - 1], r0_r.at[k - 1], {"mp": 0})

    for k in range(1, nmp):
        @pl.when(mp == k)
        def _(k=k):
            row0_copy(k).start()

    for c in forward:
        c.wait()
    products(5, [(order[1], f) for f in from_chip])
    send_products(3, 5, 3)
    prompt_pieces(1, 0, pairs)
    pre_copy = pltpu.make_async_copy(pre_v, pre_h, out_sem)
    pre_copy.start()

    for k in range(1, nmp):
        @pl.when(mp == k)
        def _(k=k):
            row0_copy(k).wait_send()
            r0_mix_in[...] = jnp.zeros(r0_mix_in.shape, BF16)

    @pl.when(mp == 0)
    def _():
        for k in range(1, nmp):
            row0_copy(k).wait_recv()

    for k in range(nmp - 1):
        row0 = row0 + r0_mix_in[k].astype(F32)

    units = [(t, chip) for t in order]
    units = units + [(t, f) for t in order for f in from_chip]
    for stage, (lo, hi) in enumerate(((0, 1), (1, 2), (2, 5), (5, 8))):
        for c in mp_copies[stage * (nmp - 1):(stage + 1) * (nmp - 1)]:
            c.wait()
        for unit in range(lo, hi):
            t, source = units[unit]
            value = prod[mp, unit].astype(F32)
            for k in range(nmp - 1):
                value = value + prod_in[k, unit].astype(F32)
            if t == 0:
                here = (mp == 0) & (source == 0) & (iota(value.shape, 0) % 8 < steps)
                value = jnp.where(here, row0, value)
            for c in range(2):
                for k in range(heads):
                    at = (2 * c + t) * hs + k * steps
                    row = k // (heads // 2) * 8 + c * steps
                    col = k % (heads // 2) * 128
                    mix_v[source, at:at + steps] = value[row:row + steps, col:col + 128]
    mix_o[...] = mix_v[...].reshape(mix_o.shape).astype(BF16)
    pre_copy.wait()


def hand_over(pre_i, mix_i, pre_o, mix_o, sems):
    copies = [
        pltpu.make_async_copy(pre_i, pre_o, sems.at[0]),
        pltpu.make_async_copy(mix_i, mix_o, sems.at[1]),
    ]
    for c in copies:
        c.start()
    for c in copies:
        c.wait()


def body(
    prompt_queries, prompt_pairs, decode_queries, decode_pairs, cache_pool, out_weight,
    slot_pages, placement, context_len,
):
    nsec, nseq, nmp = (lax.axis_size(a) for a in ("section", "seq", "mp"))
    _, blocks, btok, qwidth = prompt_queries.shape
    _, rows, steps, _ = decode_queries.shape
    slots = cache_pool.shape[1]
    width = out_weight.shape[2]
    heads = qwidth // HEAD
    hs = heads * steps
    own = rows // nseq
    pq = prompt_queries[0]
    pp = prompt_pairs.reshape(blocks * btok * 2, HEAD)
    dq = decode_queries.reshape(rows, steps, heads, HEAD).transpose(0, 2, 1, 3).reshape(rows, hs, HEAD)
    dp = decode_pairs.reshape(rows * steps * 2, HEAD)
    pool = cache_pool.reshape(slots * PAGE * 2, HEAD)
    w = out_weight[0]
    count = slots + own
    any_spec = pl.BlockSpec(memory_space=pl.ANY)
    smem_spec = pl.BlockSpec(memory_space=pltpu.SMEM)
    dma = pltpu.SemaphoreType.DMA
    prefill, mixed = pl.pallas_call(
        functools.partial(kernel, nsec, nseq, nmp, slots, rows, heads, steps),
        out_shape=(
            jax.ShapeDtypeStruct(pq.shape, BF16),
            jax.ShapeDtypeStruct((own * hs, HEAD), BF16),
        ),
        in_specs=[any_spec] * 6 + [smem_spec] * 2,
        out_specs=(any_spec, pl.BlockSpec(memory_space=pltpu.VMEM)),
        scratch_shapes=[
            pltpu.VMEM(pq.shape, BF16),
            pltpu.VMEM(pp.shape, BF16),
            pltpu.VMEM(dq.shape, BF16),
            pltpu.VMEM(dp.shape, BF16),
            pltpu.VMEM(pool.shape, BF16),
            pltpu.VMEM(w.shape, BF16),
            pltpu.VMEM((nseq,) + pp.shape, BF16),
            pltpu.VMEM((2, hs, HEAD), BF16),
            pltpu.VMEM((2 * hs, HEAD), F32),
            pltpu.VMEM((2, 2 * hs, HEAD), F32),
            pltpu.VMEM((16, width // 2), BF16),
            pltpu.VMEM((nmp - 1, 16, width // 2), BF16),
            pltpu.VMEM((hs, 128), F32),
            pltpu.VMEM((hs, 128), F32),
            pltpu.VMEM((128, 128), F32),
            pltpu.VMEM((3, own, 128), F32),
            pltpu.VMEM((count * hs, HEAD), F32),
            pltpu.VMEM((2, 2, nseq // 2, hs // 2, own, HEAD), BF16),
            pltpu.VMEM((2, nseq // 2, hs // 2, own, HEAD), BF16),
            pltpu.VMEM((2, 3, hs // 2, own, HEAD), BF16),
            pltpu.VMEM((2, nseq, own * hs // 2, HEAD), BF16),
            pltpu.VMEM((width // 128, 48 * steps, 128), F32),
            pltpu.VMEM((nmp, 8, 16, width // 2), BF16),
            pltpu.VMEM((nmp - 1, 8, 16, width // 2), BF16),
            pltpu.VMEM((4, 4 * hs, HEAD), F32),
            pltpu.VMEM(pq.shape, BF16),
            dma((16,)),
            dma,
            dma((7,)), dma((7,)),
            dma((5,)), dma((5,)),
            dma((nmp - 1,)), dma((nmp - 1,)),
            dma((2,)), dma((2,)),
            dma((2, 3)), dma((2, 3)),
            dma((3,)), dma((3,)),
            dma((2, 4)), dma((2, 4)),
            dma((2, 3)), dma((2, 3)),
            dma((4, nmp - 1)), dma((4, nmp - 1)),
        ],
        compiler_params=pltpu.CompilerParams(
            collective_id=0, has_side_effects=True, vmem_limit_bytes=56 * 1024 * 1024
        ),
    )(pq, pp, dq, dp, pool, w, slot_pages, context_len)
    prefill, mixed = pl.pallas_call(
        hand_over,
        out_shape=(
            jax.ShapeDtypeStruct(prefill.shape, BF16), jax.ShapeDtypeStruct(mixed.shape, BF16)
        ),
        in_specs=[pl.BlockSpec(memory_space=pltpu.VMEM)] * 2,
        out_specs=(any_spec,) * 2,
        scratch_shapes=[dma((2,))],
    )(prefill, mixed)
    mixed = mixed.reshape(own, width // HEAD, steps, HEAD).transpose(0, 2, 1, 3)
    mixed = mixed.reshape(own, steps, width)
    return prefill[None], mixed[None]


def solution(mesh):
    return jax.shard_map(
        body,
        mesh=mesh,
        in_specs=(
            P("section", None, "seq", "mp"),
            P("section", None, "seq", None, "mp"),
            P("section", None, None, "mp"),
            P("section", None, None, None, "mp"),
            P("section", "seq", None, None, "mp"),
            P("section", "mp", "seq"),
            P("seq"),
            P(),
            P(),
        ),
        out_specs=(P("section", None, "seq", "mp"), P("section", "mp", None, "seq")),
        check_vma=False,
    )
```

```python
import functools
import math

import jax
import jax.numpy as jnp
from jax import lax
from jax.experimental import pallas as pl
from jax.experimental.pallas import tpu as pltpu
from jax.sharding import PartitionSpec as P

HEAD = 128
PAGE = 128
MAXP = 1024
BLOCKS = 2
NEG = -1e30
F32 = jnp.float32
BF16 = jnp.bfloat16
MESH = pl.DeviceIdType.MESH
SCALE = 1.0 / (math.sqrt(HEAD) * math.log(2.0))


def dot_nt(a, b):
    return lax.dot_general(a, b, (((1,), (1,)), ((), ())), preferred_element_type=F32)


def dot_nn(a, b, precision=None):
    return lax.dot_general(
        a, b, (((1,), (0,)), ((), ())), preferred_element_type=F32, precision=precision
    )


def iota(shape, dim):
    return lax.broadcasted_iota(jnp.int32, shape, dim)


def kernel(
    nsec, nseq, nmp, slots, rows, heads, steps,
    pq_h, pp_h, dq_h, dp_h, pool_h, w_h, slot_s, ctx_s,
    pre_h, mix_o,
    pq_v, pp_v, dq_v, dp_v, pool_v, w_v, kv, q0, r0_out, r0_in, r0_mix, r0_mix_in,
    lse_out, lse_in, lse_t, lse_t_in,
    accs, part, sib_in, part_in, att, prod_f, prod, prod_in, mix_v, pre_v,
    in_sem, out_sem, kv_s, kv_r, z_s, z_r, r0_s, r0_r, sib_s, sib_r, rs_s, rs_r, st_s, st_r, ag_s, ag_r, fw_s, fw_r, mp_s, mp_r,
):
    hs = heads * steps
    half = hs // 2
    own = rows // nseq
    chips = nseq // 2
    me = lax.axis_index("seq")
    mp = lax.axis_index("mp")
    sec = lax.axis_index("section")
    chip, core = me // 2, me % 2
    next_sec = {"section": lax.rem(sec + 1, nsec)}
    last_sec = {"section": lax.rem(sec + nsec - 1, nsec)}
    sibling = {"seq": 2 * chip + 1 - core}
    away = (1, 3, 2)
    far_chip = [lax.rem(chip + k, 4) for k in away]
    far = [{"seq": 2 * c + core} for c in far_chip]
    from_chip = [lax.rem(chip + 4 - k, 4) for k in away]

    def mp_dev(k):
        return {"mp": lax.rem(mp + k, nmp)}

    def remote(src, dst, send, recv, device):
        return pltpu.make_async_remote_copy(
            src_ref=src, dst_ref=dst, send_sem=send, recv_sem=recv,
            device_id=device, device_id_type=MESH,
        )

    barrier = pltpu.get_barrier_semaphore()
    greeted = [*(mp_dev(k) for k in range(1, nmp)), next_sec, last_sec, *far, sibling]
    for device in greeted:
        pl.semaphore_signal(barrier, inc=1, device_id=device, device_id_type=MESH)

    width = 12
    groups = slots // width
    group_lines = width * 2 * PAGE

    def pool_load(g):
        sl = slice(g * group_lines, (g + 1) * group_lines)
        return pltpu.make_async_copy(pool_h.at[sl], pool_v.at[sl], in_sem.at[5 + g])

    load_dq = pltpu.make_async_copy(dq_h, dq_v, in_sem.at[0])
    load_dp = pltpu.make_async_copy(dp_h, dp_v, in_sem.at[1])
    load_pp = pltpu.make_async_copy(pp_h, pp_v, in_sem.at[2])
    load_pq = pltpu.make_async_copy(pq_h, pq_v, in_sem.at[3])
    load_w = pltpu.make_async_copy(w_h, w_v, in_sem.at[4])
    load_pool = [pool_load(g) for g in range(groups)]
    for c in [load_dq, *load_pool, load_dp, load_pp, load_pq, load_w]:
        c.start()

    lane = iota((hs, 128), 1)
    lane1 = iota((8, 128), 1)
    key_lane = iota((hs, 2 * PAGE), 1)
    key_id = jnp.where(key_lane % 2 == 0, key_lane // 2, PAGE)

    def place_of(row):
        return (row % 16) // 2 * 16 + row % 2 * 8 + row // 16

    def merge(state, index, place, m, l):
        top, total, slot_top, slot_place = state
        hit = lane == place
        fresh = jnp.where(hit, jnp.maximum(top, m), top)
        total = total * jnp.exp2((top - fresh) * SCALE) + jnp.where(
            hit, l * jnp.exp2((m - fresh) * SCALE), 0.0
        )
        slot_top = jnp.where(lane == index, m, slot_top)
        slot_place = jnp.where(lane1 == index, place, slot_place)
        return fresh, total, slot_top, slot_place

    def slot_group(g, state, width):
        done = []
        for i in range(width):
            j = g * width + i
            entry = slot_s[j]
            live = entry >= 0
            row = jnp.where(live, entry // MAXP, 0)
            count = jnp.where(live, jnp.clip(ctx_s[row] - (entry % MAXP) * PAGE, 0, PAGE), 0)
            page = pool_v[pl.ds(pl.multiple_of(j * 2 * PAGE, 2 * PAGE), 2 * PAGE), :]
            place = jnp.where(live, place_of(row), -1)
            done.append((j, place, count, page, dot_nt(dq_v[row], page)))
        for j, place, count, page, scores in done:
            allowed = key_id < count
            scores = jnp.where(allowed, scores, NEG)
            m = jnp.max(scores, axis=1, keepdims=True)
            p = jnp.where(allowed, jnp.exp2((scores - m) * SCALE), 0.0)
            l = jnp.sum(p, axis=1, keepdims=True)
            acc = dot_nn(pltpu.roll(p, 1, 1).astype(BF16), page)
            accs[pl.ds(pl.multiple_of(j * hs, hs), hs), :] = acc
            state = merge(state, j, place, m, l)
        return state

    state = (
        jnp.full((hs, 128), NEG, F32), jnp.zeros((hs, 128), F32),
        jnp.full((hs, 128), NEG, F32), jnp.full((8, 128), -1, jnp.int32),
    )
    load_dq.wait()
    for g in range(groups):
        load_pool[g].wait()
        state = slot_group(g, state, width)

    load_pp.wait()
    ri = iota((2 * PAGE, 2 * PAGE), 0)
    ci = iota((2 * PAGE, 2 * PAGE), 1)
    pick = jnp.where(ci == jnp.where(ri < PAGE, 2 * ri, 2 * (ri - PAGE) + 1), 1.0, 0.0).astype(BF16)
    for b in range(BLOCKS):
        both = dot_nn(pick, pp_v[b * 2 * PAGE:(b + 1) * 2 * PAGE, :]).astype(BF16)
        kv[me, b * PAGE:(b + 1) * PAGE, :] = both[:PAGE]
        kv[me, (BLOCKS + b) * PAGE:(BLOCKS + b + 1) * PAGE, :] = both[PAGE:]

    load_dp.wait()
    mine = [16 * m + 2 * me for m in range(nmp)]
    line = 2 * steps
    recent = jnp.concatenate(
        [dp_v[pl.ds(pl.multiple_of(r * line, 2 * line), 2 * line), :] for r in mine], axis=0
    )
    rq = jnp.concatenate([dq_v[pl.ds(r, 2)].reshape(2 * hs, HEAD) for r in mine], axis=0)
    scores = dot_nt(rq, recent)
    ri = iota(scores.shape, 0)
    ci = iota(scores.shape, 1)
    allowed = (
        (ci % 2 == 0) & (ci // line == ri // hs) & ((ci % line) // 2 <= ri % steps)
    )
    scores = jnp.where(allowed, scores, NEG)
    m = jnp.max(scores, axis=1, keepdims=True)
    p = jnp.where(allowed, jnp.exp2((scores - m) * SCALE), 0.0)
    l = jnp.sum(p, axis=1, keepdims=True)
    accs[slots * hs:(slots + own) * hs, :] = dot_nn(pltpu.roll(p, 1, 1).astype(BF16), recent)
    for r in range(own):
        state = merge(
            state, slots + r, me * own + r % 2 * 8 + r // 2,
            m[r * hs:(r + 1) * hs], l[r * hs:(r + 1) * hs],
        )
    top, total, slot_top, slot_place = state
    lse_mine = jnp.where(
        total > 0.0, top * SCALE + jnp.log2(jnp.maximum(total, 1e-30)), NEG
    )
    lse_out[...] = lse_mine
    scores = dot_nt(dq_v[0], dp_v[0:2 * line, :])
    ci = iota(scores.shape, 1)
    allowed = (ci % 2 == 0) & (ci < line) & (ci // 2 <= iota(scores.shape, 0) % steps)
    scores = jnp.where(allowed, scores, NEG)
    row0_m = jnp.max(scores, axis=1, keepdims=True)
    p = jnp.where(allowed, jnp.exp2((scores - row0_m) * SCALE), 0.0)
    row0_l = jnp.sum(p, axis=1, keepdims=True)
    p = jnp.concatenate([jnp.zeros((hs, 1), F32), p[:, :2 * line - 1]], axis=1)
    row0_acc = dot_nn(p.astype(BF16), dp_v[0:2 * line, :])

    pl.semaphore_wait(barrier, len(greeted))
    lse_copy = remote(lse_out, lse_in, z_s.at[0], z_r.at[0], sibling)
    lse_copy.start()
    q_first = remote(dq_v.at[0], q0.at[0], z_s.at[1], z_r.at[1], next_sec)
    q_second = remote(q0.at[0], q0.at[1], z_s.at[2], z_r.at[2], next_sec)
    q_first.start()
    kv_far = [remote(kv.at[me], kv.at[me], kv_s.at[i], kv_r.at[i], far[i]) for i in range(3)]
    for c in kv_far[:2]:
        c.start()
    kv_near = [remote(kv.at[me], kv.at[me], kv_s.at[3], kv_r.at[3], sibling)] + [
        remote(kv.at[2 * f + core], kv.at[2 * f + core], kv_s.at[4 + i], kv_r.at[4 + i], sibling)
        for i, f in enumerate(from_chip)
    ]
    kv_near[0].start()
    place_pick = jnp.where(
        iota((128, 128), 0) == jnp.broadcast_to(slot_place[0:1], (128, 128)), 1.0, 0.0
    )
    lse_copy.wait()
    peak = jnp.maximum(lse_mine, lse_in[...])
    lse_chip = peak + jnp.log2(jnp.exp2(lse_mine - peak) + jnp.exp2(lse_in[...] - peak))
    whole_slot = dot_nn(lse_chip, place_pick, lax.Precision.HIGHEST)
    factor = jnp.exp2(slot_top * SCALE - whole_slot)
    lse_t[...] = jnp.concatenate([lse_chip, jnp.zeros((128 - hs, 128), F32)], axis=0).T

    count = accs.shape[0] // hs

    def row_sums(j):
        weights = (place_pick * jnp.broadcast_to(factor[j:j + 1], (128, 128)))[:rows, :count]
        return dot_nn(weights.astype(BF16), accs[pl.ds(j, count, stride=hs), :].astype(BF16))

    for i in range(half):
        even, odd = row_sums(2 * i), row_sums(2 * i + 1)
        for s in range(nseq):
            for t in range(2):
                sl = slice(s * own + 8 * t, s * own + 8 * t + 8)
                part[t, s % 2, s // 2, i] = jnp.concatenate([even[sl], odd[sl]], axis=0).astype(BF16)
    order = (1, 0)
    sib_copies = [
        remote(part.at[t, 1 - core], sib_in.at[t], sib_s.at[t], sib_r.at[t], sibling)
        for t in range(2)
    ]
    for t in order:
        sib_copies[t].start()

    st_copies = [
        remote(
            lse_t.at[pl.ds(pl.multiple_of((2 * f + core) * own, own), own)], lse_t_in.at[i],
            st_s.at[i], st_r.at[i], far[i],
        )
        for i, f in enumerate(far_chip)
    ]
    rs_copies = [
        [
            remote(part.at[t, core, f], part_in.at[t, i], rs_s.at[t, i], rs_r.at[t, i], far[i])
            for i, f in enumerate(far_chip)
        ]
        for t in range(2)
    ]
    for t in order:
        sib_copies[t].wait()
        for i, f in enumerate(far_chip + [chip]):
            for at in range(0, half, 4):
                sl = slice(at, at + 4)
                part[t, core, f, sl] = (
                    part[t, core, f, sl].astype(F32) + sib_in[t, f, sl].astype(F32)
                ).astype(BF16)
            if i < 3:
                rs_copies[t][i].start()
        if t == order[0]:
            for c in st_copies:
                c.start()

    kv_far[2].start()
    q_first.wait()
    q_second.start()

    n = nseq * PAGE

    def prompt_keys(b):
        return kv[:, b * PAGE:(b + 1) * PAGE, :].reshape(n, HEAD)

    def prompt_values(b):
        return kv[:, (BLOCKS + b) * PAGE:(BLOCKS + b + 1) * PAGE, :].reshape(n, HEAD)

    def prompt_piece(b, pair):
        two = pq_v[b, :, pl.ds(pl.multiple_of(pair * 2 * HEAD, 2 * HEAD), 2 * HEAD)]
        q = jnp.concatenate([two[:, :HEAD], two[:, HEAD:]], axis=0)
        s_own = dot_nt(q, prompt_keys(b))
        limit = me * PAGE + iota((2 * PAGE, n), 0) % PAGE
        s_own = jnp.where(iota((2 * PAGE, n), 1) <= limit, s_own, NEG)
        m = jnp.max(s_own, axis=1, keepdims=True)
        if b:
            s_old = dot_nt(q, prompt_keys(0))
            m = jnp.maximum(m, jnp.max(s_old, axis=1, keepdims=True))
        p = jnp.exp2((s_own - m) * SCALE)
        l = jnp.sum(p, axis=1, keepdims=True)
        o = dot_nn(p.astype(BF16), prompt_values(b))
        if b:
            p = jnp.exp2((s_old - m) * SCALE)
            l = l + jnp.sum(p, axis=1, keepdims=True)
            o = o + dot_nn(p.astype(BF16), prompt_values(0))
        o = (o / l).astype(BF16)
        pre_v[b, :, pl.ds(pl.multiple_of(pair * 2 * HEAD, 2 * HEAD), 2 * HEAD)] = jnp.concatenate(
            [o[:PAGE], o[PAGE:]], axis=1
        )

    def prompt_pieces(b, lo, hi):
        def step(i, carry):
            prompt_piece(b, i)
            return carry

        lax.fori_loop(lo, hi, step, 0)

    pairs = heads // 2

    for c in st_copies:
        c.wait()
    ag_far = []
    ag_near = []
    lines = 8 * steps

    def shares_of(terms):
        peak = functools.reduce(jnp.maximum, terms)
        whole = peak + jnp.log2(sum(jnp.exp2(t - peak) for t in terms))
        return [jnp.exp2(t - whole) for t in terms]

    def finish(t):
        sl = slice(8 * t, 8 * t + 8)
        mine_t = lse_t[pl.ds(pl.multiple_of(me * own + 8 * t, 8), 8), :]
        terms = [mine_t] + [lse_t_in[i, sl] for i in range(3)]
        shares = shares_of(terms)
        for c in rs_copies[t]:
            c.wait()
        for i in range(half):
            blocks = [part[t, core, chip, i]] + [part_in[t, k, i] for k in range(3)]
            blocks = [b.astype(F32) for b in blocks]
            two = []
            for j in range(2):
                at = 2 * i + j
                tot = sum(
                    b[8 * j:8 * j + 8] * share[:, at:at + 1] for b, share in zip(blocks, shares)
                )
                two.append(tot)
            att[t, me, 16 * i:16 * i + 16] = jnp.concatenate(two, axis=0).astype(BF16)
        block = att.at[t, me]
        c = remote(block, block, ag_s.at[t, 3], ag_r.at[t, 3], sibling)
        c.start()
        ag_near.append(c)
        group = [remote(block, block, ag_s.at[t, i], ag_r.at[t, i], far[i]) for i in range(3)]
        for c in group:
            c.start()
        ag_far.append(group)

    half_cols = w_v.shape[1] // 2

    def products(first_unit, sources):
        left = jnp.concatenate(
            [
                jnp.concatenate(
                    [att[t, 2 * f + c, h * lines:(h + 1) * lines] for h in range(heads)], axis=1
                )
                for t, f in sources for c in range(2)
            ],
            axis=0,
        )
        out = dot_nn(left, w_v[...])
        for k in range(heads):
            prod_f[k, 0:2 * lines * len(sources), :] = out[:, 128 * k:128 * (k + 1)]
        for i in range(len(sources)):
            for m in range(nmp):
                value = jnp.concatenate(
                    [
                        prod_f[k, pl.ds(2 * lines * i + m, 8, stride=8), :]
                        for k in range(heads)
                    ],
                    axis=1,
                )
                prod[m, first_unit + i] = jnp.concatenate(
                    [value[:, :half_cols], value[:, half_cols:]], axis=0
                ).astype(BF16)

    mp_copies = []

    def send_products(stage, first_unit, units):
        sl = pl.ds(first_unit, units)
        for k in range(1, nmp):
            c = remote(
                prod.at[lax.rem(mp + k, nmp), sl], prod_in.at[k - 1, sl],
                mp_s.at[stage, k - 1], mp_r.at[stage, k - 1], mp_dev(k),
            )
            c.start()
            mp_copies.append(c)

    def forward_rows(turn):
        copies = []
        for i, f in enumerate(from_chip):
            ag_far[turn][i].wait()
            block = att.at[order[turn], 2 * f + core]
            c = remote(block, block, fw_s.at[turn, i], fw_r.at[turn, i], sibling)
            c.start()
            copies.append(c)
        return copies

    finish(order[0])
    load_w.wait()
    ag_near[0].wait()
    products(0, [(order[0], chip)])
    send_products(0, 0, 1)
    finish(order[1])

    for i in range(3):
        kv_far[i].wait()
        kv_near[i + 1].start()

    ag_near[1].wait()
    products(1, [(order[1], chip)])
    send_products(1, 1, 1)
    for c in kv_near:
        c.wait()

    q_second.wait()
    s0 = []
    for b in range(BLOCKS):
        scores = dot_nt(q0[1], prompt_keys(b))
        s0.append(jnp.where(iota(scores.shape, 1) + b * n < ctx_s[0], scores, NEG))
    m = functools.reduce(jnp.maximum, [jnp.max(x, axis=1, keepdims=True) for x in s0])
    p0 = [jnp.exp2((x - m) * SCALE) for x in s0]
    l = sum(jnp.sum(p, axis=1, keepdims=True) for p in p0)
    r0_out[0:hs, :] = sum(dot_nn(p.astype(BF16), prompt_values(b)) for b, p in enumerate(p0))
    r0_out[hs:2 * hs, :] = jnp.where(lane == 0, m, l)
    r0_first = remote(r0_out, r0_in.at[0], z_s.at[3], z_r.at[3], next_sec)
    r0_second = remote(r0_in.at[0], r0_in.at[1], z_s.at[4], z_r.at[4], next_sec)
    r0_first.start()

    load_pq.wait()
    prompt_pieces(0, 0, 1)
    forward = forward_rows(0)
    prompt_pieces(0, 1, 2)
    for c in forward:
        c.wait()
    products(2, [(order[0], f) for f in from_chip])
    send_products(2, 2, 3)
    r0_first.wait()
    r0_second.start()
    forward = forward_rows(1)
    prompt_pieces(0, 2, 3)
    for c in forward:
        c.wait()
    products(5, [(order[1], f) for f in from_chip])
    send_products(3, 5, 3)
    prompt_pieces(0, 3, pairs)
    prompt_pieces(1, 0, 1)

    r0_second.wait()
    prompt_m, prompt_l = r0_in[1, hs:2 * hs, 0:1], r0_in[1, hs:2 * hs, 1:2]
    peak = jnp.maximum(row0_m, prompt_m)
    keep = jnp.exp2((row0_m - peak) * SCALE)
    more = jnp.exp2((prompt_m - peak) * SCALE)
    row0 = (row0_acc * keep + r0_in[1, 0:hs, :] * more) / (row0_l * keep + prompt_l * more)
    row0 = jnp.concatenate([row0[h * steps:(h + 1) * steps] for h in range(heads)], axis=1)
    row0 = jnp.concatenate([row0, jnp.zeros((16 - steps, row0.shape[1]), F32)], axis=0)
    row0 = dot_nn(row0.astype(BF16), w_v[...])[0:8]
    row0 = jnp.concatenate([row0[:, :half_cols], row0[:, half_cols:]], axis=0)
    r0_mix[...] = row0.astype(BF16)

    def row0_copy(k):
        return remote(r0_mix, r0_mix_in.at[k - 1], r0_s.at[k - 1], r0_r.at[k - 1], {"mp": 0})

    for k in range(1, nmp):
        @pl.when(mp == k)
        def _(k=k):
            row0_copy(k).start()

    prompt_pieces(1, 1, pairs)
    pre_copy = pltpu.make_async_copy(pre_v, pre_h, out_sem)
    pre_copy.start()

    for k in range(1, nmp):
        @pl.when(mp == k)
        def _(k=k):
            row0_copy(k).wait_send()
            r0_mix_in[...] = jnp.zeros(r0_mix_in.shape, BF16)

    @pl.when(mp == 0)
    def _():
        for k in range(1, nmp):
            row0_copy(k).wait_recv()

    for k in range(nmp - 1):
        row0 = row0 + r0_mix_in[k].astype(F32)

    units = [(t, chip) for t in order]
    units = units + [(t, f) for t in order for f in from_chip]
    for stage, (lo, hi) in enumerate(((0, 1), (1, 2), (2, 5), (5, 8))):
        for c in mp_copies[stage * (nmp - 1):(stage + 1) * (nmp - 1)]:
            c.wait()
        for unit in range(lo, hi):
            t, source = units[unit]
            value = prod[mp, unit].astype(F32)
            for k in range(nmp - 1):
                value = value + prod_in[k, unit].astype(F32)
            if t == 0:
                here = (mp == 0) & (source == 0) & (iota(value.shape, 0) % 8 < steps)
                value = jnp.where(here, row0, value)
            for c in range(2):
                for k in range(heads):
                    at = (2 * c + t) * hs + k * steps
                    row = k // (heads // 2) * 8 + c * steps
                    col = k % (heads // 2) * 128
                    mix_v[source, at:at + steps] = value[row:row + steps, col:col + 128]
    mix_o[...] = mix_v[...].reshape(mix_o.shape).astype(BF16)
    pre_copy.wait()


def hand_over(pre_i, mix_i, pre_o, mix_o, sems):
    copies = [
        pltpu.make_async_copy(pre_i, pre_o, sems.at[0]),
        pltpu.make_async_copy(mix_i, mix_o, sems.at[1]),
    ]
    for c in copies:
        c.start()
    for c in copies:
        c.wait()


def body(
    prompt_queries, prompt_pairs, decode_queries, decode_pairs, cache_pool, out_weight,
    slot_pages, placement, context_len,
):
    nsec, nseq, nmp = (lax.axis_size(a) for a in ("section", "seq", "mp"))
    _, blocks, btok, qwidth = prompt_queries.shape
    _, rows, steps, _ = decode_queries.shape
    slots = cache_pool.shape[1]
    width = out_weight.shape[2]
    heads = qwidth // HEAD
    hs = heads * steps
    own = rows // nseq
    pq = prompt_queries[0]
    pp = prompt_pairs.reshape(blocks * btok * 2, HEAD)
    dq = decode_queries.reshape(rows, steps, heads, HEAD).transpose(0, 2, 1, 3).reshape(rows, hs, HEAD)
    dp = decode_pairs.reshape(rows * steps * 2, HEAD)
    pool = cache_pool.reshape(slots * PAGE * 2, HEAD)
    w = out_weight[0]
    count = slots + own
    any_spec = pl.BlockSpec(memory_space=pl.ANY)
    smem_spec = pl.BlockSpec(memory_space=pltpu.SMEM)
    dma = pltpu.SemaphoreType.DMA
    prefill, mixed = pl.pallas_call(
        functools.partial(kernel, nsec, nseq, nmp, slots, rows, heads, steps),
        out_shape=(
            jax.ShapeDtypeStruct(pq.shape, BF16),
            jax.ShapeDtypeStruct((own * hs, HEAD), BF16),
        ),
        in_specs=[any_spec] * 6 + [smem_spec] * 2,
        out_specs=(any_spec, pl.BlockSpec(memory_space=pltpu.VMEM)),
        scratch_shapes=[
            pltpu.VMEM(pq.shape, BF16),
            pltpu.VMEM(pp.shape, BF16),
            pltpu.VMEM(dq.shape, BF16),
            pltpu.VMEM(dp.shape, BF16),
            pltpu.VMEM(pool.shape, BF16),
            pltpu.VMEM(w.shape, BF16),
            pltpu.VMEM((nseq,) + pp.shape, BF16),
            pltpu.VMEM((2, hs, HEAD), BF16),
            pltpu.VMEM((2 * hs, HEAD), F32),
            pltpu.VMEM((2, 2 * hs, HEAD), F32),
            pltpu.VMEM((16, width // 2), BF16),
            pltpu.VMEM((nmp - 1, 16, width // 2), BF16),
            pltpu.VMEM((hs, 128), F32),
            pltpu.VMEM((hs, 128), F32),
            pltpu.VMEM((128, 128), F32),
            pltpu.VMEM((3, own, 128), F32),
            pltpu.VMEM((count * hs, HEAD), F32),
            pltpu.VMEM((2, 2, nseq // 2, hs // 2, own, HEAD), BF16),
            pltpu.VMEM((2, nseq // 2, hs // 2, own, HEAD), BF16),
            pltpu.VMEM((2, 3, hs // 2, own, HEAD), BF16),
            pltpu.VMEM((2, nseq, own * hs // 2, HEAD), BF16),
            pltpu.VMEM((width // 128, 48 * steps, 128), F32),
            pltpu.VMEM((nmp, 8, 16, width // 2), BF16),
            pltpu.VMEM((nmp - 1, 8, 16, width // 2), BF16),
            pltpu.VMEM((4, 4 * hs, HEAD), F32),
            pltpu.VMEM(pq.shape, BF16),
            dma((16,)),
            dma,
            dma((7,)), dma((7,)),
            dma((5,)), dma((5,)),
            dma((nmp - 1,)), dma((nmp - 1,)),
            dma((2,)), dma((2,)),
            dma((2, 3)), dma((2, 3)),
            dma((3,)), dma((3,)),
            dma((2, 4)), dma((2, 4)),
            dma((2, 3)), dma((2, 3)),
            dma((4, nmp - 1)), dma((4, nmp - 1)),
        ],
        compiler_params=pltpu.CompilerParams(
            collective_id=0, has_side_effects=True, vmem_limit_bytes=56 * 1024 * 1024
        ),
    )(pq, pp, dq, dp, pool, w, slot_pages, context_len)
    prefill, mixed = pl.pallas_call(
        hand_over,
        out_shape=(
            jax.ShapeDtypeStruct(prefill.shape, BF16), jax.ShapeDtypeStruct(mixed.shape, BF16)
        ),
        in_specs=[pl.BlockSpec(memory_space=pltpu.VMEM)] * 2,
        out_specs=(any_spec,) * 2,
        scratch_shapes=[dma((2,))],
    )(prefill, mixed)
    mixed = mixed.reshape(own, width // HEAD, steps, HEAD).transpose(0, 2, 1, 3)
    mixed = mixed.reshape(own, steps, width)
    return prefill[None], mixed[None]


def solution(mesh):
    return jax.shard_map(
        body,
        mesh=mesh,
        in_specs=(
            P("section", None, "seq", "mp"),
            P("section", None, "seq", None, "mp"),
            P("section", None, None, "mp"),
            P("section", None, None, None, "mp"),
            P("section", "seq", None, None, "mp"),
            P("section", "mp", "seq"),
            P("seq"),
            P(),
            P(),
        ),
        out_specs=(P("section", None, "seq", "mp"), P("section", "mp", None, "seq")),
        check_vma=False,
    )
```

```python
import functools
import math

import jax
import jax.numpy as jnp
from jax import lax
from jax.experimental import pallas as pl
from jax.experimental.pallas import tpu as pltpu
from jax.sharding import PartitionSpec as P

HEAD = 128
PAGE = 128
MAXP = 1024
BLOCKS = 2
NEG = -1e30
F32 = jnp.float32
BF16 = jnp.bfloat16
MESH = pl.DeviceIdType.MESH
SCALE = 1.0 / (math.sqrt(HEAD) * math.log(2.0))


def dot_nt(a, b):
    return lax.dot_general(a, b, (((1,), (1,)), ((), ())), preferred_element_type=F32)


def dot_nn(a, b, precision=None):
    return lax.dot_general(
        a, b, (((1,), (0,)), ((), ())), preferred_element_type=F32, precision=precision
    )


def iota(shape, dim):
    return lax.broadcasted_iota(jnp.int32, shape, dim)


def kernel(
    nsec, nseq, nmp, slots, rows, heads, steps,
    pq_h, pp_h, dq_h, dp_h, pool_h, w_h, slot_s, ctx_s,
    pre_h, mix_o,
    pq_v, pp_v, dq_v, dp_v, pool_v, w_v, kv, q0, r0_out, r0_in, r0_mix, r0_mix_in,
    lse_out, lse_in, lse_t, lse_t_in,
    accs, part, sib_in, part_in, att, prod_f, prod, prod_in, mix_v, pre_v,
    in_sem, out_sem, kv_s, kv_r, z_s, z_r, r0_s, r0_r, sib_s, sib_r, rs_s, rs_r, st_s, st_r, ag_s, ag_r, fw_s, fw_r, mp_s, mp_r,
):
    hs = heads * steps
    half = hs // 2
    own = rows // nseq
    chips = nseq // 2
    me = lax.axis_index("seq")
    mp = lax.axis_index("mp")
    sec = lax.axis_index("section")
    chip, core = me // 2, me % 2
    partner = {"section": lax.rem(sec + nsec // 2, nsec)}
    sibling = {"seq": 2 * chip + 1 - core}
    away = (1, 3, 2)
    far_chip = [lax.rem(chip + k, 4) for k in away]
    far = [{"seq": 2 * c + core} for c in far_chip]
    from_chip = [lax.rem(chip + 4 - k, 4) for k in away]

    def mp_dev(k):
        return {"mp": lax.rem(mp + k, nmp)}

    def remote(src, dst, send, recv, device):
        return pltpu.make_async_remote_copy(
            src_ref=src, dst_ref=dst, send_sem=send, recv_sem=recv,
            device_id=device, device_id_type=MESH,
        )

    barrier = pltpu.get_barrier_semaphore()
    greeted = [partner, *(mp_dev(k) for k in range(1, nmp)), *far, sibling]
    for device in greeted:
        pl.semaphore_signal(barrier, inc=1, device_id=device, device_id_type=MESH)

    width = 12
    groups = slots // width
    group_lines = width * 2 * PAGE

    def pool_load(g):
        sl = slice(g * group_lines, (g + 1) * group_lines)
        return pltpu.make_async_copy(pool_h.at[sl], pool_v.at[sl], in_sem.at[5 + g])

    load_dq = pltpu.make_async_copy(dq_h, dq_v, in_sem.at[0])
    load_dp = pltpu.make_async_copy(dp_h, dp_v, in_sem.at[1])
    load_pp = pltpu.make_async_copy(pp_h, pp_v, in_sem.at[2])
    load_pq = pltpu.make_async_copy(pq_h, pq_v, in_sem.at[3])
    load_w = pltpu.make_async_copy(w_h, w_v, in_sem.at[4])
    load_pool = [pool_load(g) for g in range(groups)]
    for c in [load_dq, *load_pool, load_dp, load_pp, load_pq, load_w]:
        c.start()

    lane = iota((hs, 128), 1)
    lane1 = iota((8, 128), 1)
    key_lane = iota((hs, 2 * PAGE), 1)
    key_id = jnp.where(key_lane % 2 == 0, key_lane // 2, PAGE)

    def place_of(row):
        return (row % 16) // 2 * 16 + row % 2 * 8 + row // 16

    def merge(state, index, place, m, l):
        top, total, slot_top, slot_place = state
        hit = lane == place
        fresh = jnp.where(hit, jnp.maximum(top, m), top)
        total = total * jnp.exp2((top - fresh) * SCALE) + jnp.where(
            hit, l * jnp.exp2((m - fresh) * SCALE), 0.0
        )
        slot_top = jnp.where(lane == index, m, slot_top)
        slot_place = jnp.where(lane1 == index, place, slot_place)
        return fresh, total, slot_top, slot_place

    def slot_group(g, state, width):
        done = []
        for i in range(width):
            j = g * width + i
            entry = slot_s[j]
            live = entry >= 0
            row = jnp.where(live, entry // MAXP, 0)
            count = jnp.where(live, jnp.clip(ctx_s[row] - (entry % MAXP) * PAGE, 0, PAGE), 0)
            page = pool_v[pl.ds(pl.multiple_of(j * 2 * PAGE, 2 * PAGE), 2 * PAGE), :]
            place = jnp.where(live, place_of(row), -1)
            done.append((j, place, count, page, dot_nt(dq_v[row], page)))
        for j, place, count, page, scores in done:
            allowed = key_id < count
            scores = jnp.where(allowed, scores, NEG)
            m = jnp.max(scores, axis=1, keepdims=True)
            p = jnp.where(allowed, jnp.exp2((scores - m) * SCALE), 0.0)
            l = jnp.sum(p, axis=1, keepdims=True)
            acc = dot_nn(pltpu.roll(p, 1, 1).astype(BF16), page)
            accs[pl.ds(pl.multiple_of(j * hs, hs), hs), :] = acc
            state = merge(state, j, place, m, l)
        return state

    state = (
        jnp.full((hs, 128), NEG, F32), jnp.zeros((hs, 128), F32),
        jnp.full((hs, 128), NEG, F32), jnp.full((8, 128), -1, jnp.int32),
    )
    load_dq.wait()
    for g in range(groups):
        load_pool[g].wait()
        state = slot_group(g, state, width)

    load_pp.wait()
    ri = iota((2 * PAGE, 2 * PAGE), 0)
    ci = iota((2 * PAGE, 2 * PAGE), 1)
    pick = jnp.where(ci == jnp.where(ri < PAGE, 2 * ri, 2 * (ri - PAGE) + 1), 1.0, 0.0).astype(BF16)
    for b in range(BLOCKS):
        both = dot_nn(pick, pp_v[b * 2 * PAGE:(b + 1) * 2 * PAGE, :]).astype(BF16)
        kv[me, b * PAGE:(b + 1) * PAGE, :] = both[:PAGE]
        kv[me, (BLOCKS + b) * PAGE:(BLOCKS + b + 1) * PAGE, :] = both[PAGE:]

    load_dp.wait()
    mine = [16 * m + 2 * me for m in range(nmp)]
    line = 2 * steps
    recent = jnp.concatenate(
        [dp_v[pl.ds(pl.multiple_of(r * line, 2 * line), 2 * line), :] for r in mine], axis=0
    )
    rq = jnp.concatenate([dq_v[pl.ds(r, 2)].reshape(2 * hs, HEAD) for r in mine], axis=0)
    scores = dot_nt(rq, recent)
    ri = iota(scores.shape, 0)
    ci = iota(scores.shape, 1)
    allowed = (
        (ci % 2 == 0) & (ci // line == ri // hs) & ((ci % line) // 2 <= ri % steps)
    )
    scores = jnp.where(allowed, scores, NEG)
    m = jnp.max(scores, axis=1, keepdims=True)
    p = jnp.where(allowed, jnp.exp2((scores - m) * SCALE), 0.0)
    l = jnp.sum(p, axis=1, keepdims=True)
    accs[slots * hs:(slots + own) * hs, :] = dot_nn(pltpu.roll(p, 1, 1).astype(BF16), recent)
    for r in range(own):
        state = merge(
            state, slots + r, me * own + r % 2 * 8 + r // 2,
            m[r * hs:(r + 1) * hs], l[r * hs:(r + 1) * hs],
        )
    top, total, slot_top, slot_place = state
    lse_mine = jnp.where(
        total > 0.0, top * SCALE + jnp.log2(jnp.maximum(total, 1e-30)), NEG
    )
    lse_out[...] = lse_mine
    scores = dot_nt(dq_v[0], dp_v[0:2 * line, :])
    ci = iota(scores.shape, 1)
    allowed = (ci % 2 == 0) & (ci < line) & (ci // 2 <= iota(scores.shape, 0) % steps)
    scores = jnp.where(allowed, scores, NEG)
    row0_m = jnp.max(scores, axis=1, keepdims=True)
    p = jnp.where(allowed, jnp.exp2((scores - row0_m) * SCALE), 0.0)
    row0_l = jnp.sum(p, axis=1, keepdims=True)
    p = jnp.concatenate([jnp.zeros((hs, 1), F32), p[:, :2 * line - 1]], axis=1)
    row0_acc = dot_nn(p.astype(BF16), dp_v[0:2 * line, :])

    pl.semaphore_wait(barrier, len(greeted))
    lse_copy = remote(lse_out, lse_in, z_s.at[0], z_r.at[0], sibling)
    lse_copy.start()
    q_copy = remote(dq_v.at[0], q0, z_s.at[1], z_r.at[1], partner)
    q_copy.start()
    kv_far = [remote(kv.at[me], kv.at[me], kv_s.at[i], kv_r.at[i], far[i]) for i in range(3)]
    for c in kv_far[:2]:
        c.start()
    kv_near = [remote(kv.at[me], kv.at[me], kv_s.at[3], kv_r.at[3], sibling)] + [
        remote(kv.at[2 * f + core], kv.at[2 * f + core], kv_s.at[4 + i], kv_r.at[4 + i], sibling)
        for i, f in enumerate(from_chip)
    ]
    kv_near[0].start()
    place_pick = jnp.where(
        iota((128, 128), 0) == jnp.broadcast_to(slot_place[0:1], (128, 128)), 1.0, 0.0
    )
    lse_copy.wait()
    peak = jnp.maximum(lse_mine, lse_in[...])
    lse_chip = peak + jnp.log2(jnp.exp2(lse_mine - peak) + jnp.exp2(lse_in[...] - peak))
    whole_slot = dot_nn(lse_chip, place_pick, lax.Precision.HIGHEST)
    factor = jnp.exp2(slot_top * SCALE - whole_slot)
    lse_t[...] = jnp.concatenate([lse_chip, jnp.zeros((128 - hs, 128), F32)], axis=0).T

    count = accs.shape[0] // hs

    def row_sums(j):
        weights = (place_pick * jnp.broadcast_to(factor[j:j + 1], (128, 128)))[:rows, :count]
        return dot_nn(weights.astype(BF16), accs[pl.ds(j, count, stride=hs), :].astype(BF16))

    for i in range(half):
        even, odd = row_sums(2 * i), row_sums(2 * i + 1)
        for s in range(nseq):
            for t in range(2):
                sl = slice(s * own + 8 * t, s * own + 8 * t + 8)
                part[t, s % 2, s // 2, i] = jnp.concatenate([even[sl], odd[sl]], axis=0).astype(BF16)
    order = (1, 0)
    sib_copies = [
        remote(part.at[t, 1 - core], sib_in.at[t], sib_s.at[t], sib_r.at[t], sibling)
        for t in range(2)
    ]
    for t in order:
        sib_copies[t].start()

    st_copies = [
        remote(
            lse_t.at[pl.ds(pl.multiple_of((2 * f + core) * own, own), own)], lse_t_in.at[i],
            st_s.at[i], st_r.at[i], far[i],
        )
        for i, f in enumerate(far_chip)
    ]
    rs_copies = [
        [
            remote(part.at[t, core, f], part_in.at[t, i], rs_s.at[t, i], rs_r.at[t, i], far[i])
            for i, f in enumerate(far_chip)
        ]
        for t in range(2)
    ]
    for t in order:
        sib_copies[t].wait()
        for i, f in enumerate(far_chip + [chip]):
            for at in range(0, half, 4):
                sl = slice(at, at + 4)
                part[t, core, f, sl] = (
                    part[t, core, f, sl].astype(F32) + sib_in[t, f, sl].astype(F32)
                ).astype(BF16)
            if i < 3:
                rs_copies[t][i].start()
        if t == order[0]:
            for c in st_copies:
                c.start()

    kv_far[2].start()

    n = nseq * PAGE

    def prompt_keys(b):
        return kv[:, b * PAGE:(b + 1) * PAGE, :].reshape(n, HEAD)

    def prompt_values(b):
        return kv[:, (BLOCKS + b) * PAGE:(BLOCKS + b + 1) * PAGE, :].reshape(n, HEAD)

    def prompt_piece(b, pair):
        two = pq_v[b, :, pl.ds(pl.multiple_of(pair * 2 * HEAD, 2 * HEAD), 2 * HEAD)]
        q = jnp.concatenate([two[:, :HEAD], two[:, HEAD:]], axis=0)
        s_own = dot_nt(q, prompt_keys(b))
        limit = me * PAGE + iota((2 * PAGE, n), 0) % PAGE
        s_own = jnp.where(iota((2 * PAGE, n), 1) <= limit, s_own, NEG)
        m = jnp.max(s_own, axis=1, keepdims=True)
        if b:
            s_old = dot_nt(q, prompt_keys(0))
            m = jnp.maximum(m, jnp.max(s_old, axis=1, keepdims=True))
        p = jnp.exp2((s_own - m) * SCALE)
        l = jnp.sum(p, axis=1, keepdims=True)
        o = dot_nn(p.astype(BF16), prompt_values(b))
        if b:
            p = jnp.exp2((s_old - m) * SCALE)
            l = l + jnp.sum(p, axis=1, keepdims=True)
            o = o + dot_nn(p.astype(BF16), prompt_values(0))
        o = (o / l).astype(BF16)
        pre_v[b, :, pl.ds(pl.multiple_of(pair * 2 * HEAD, 2 * HEAD), 2 * HEAD)] = jnp.concatenate(
            [o[:PAGE], o[PAGE:]], axis=1
        )

    def prompt_pieces(b, lo, hi):
        def step(i, carry):
            prompt_piece(b, i)
            return carry

        lax.fori_loop(lo, hi, step, 0)

    pairs = heads // 2

    for c in st_copies:
        c.wait()
    ag_far = []
    ag_near = []
    lines = 8 * steps

    def shares_of(terms):
        peak = functools.reduce(jnp.maximum, terms)
        whole = peak + jnp.log2(sum(jnp.exp2(t - peak) for t in terms))
        return [jnp.exp2(t - whole) for t in terms]

    def finish(t):
        sl = slice(8 * t, 8 * t + 8)
        mine_t = lse_t[pl.ds(pl.multiple_of(me * own + 8 * t, 8), 8), :]
        terms = [mine_t] + [lse_t_in[i, sl] for i in range(3)]
        shares = shares_of(terms)
        for c in rs_copies[t]:
            c.wait()
        for i in range(half):
            blocks = [part[t, core, chip, i]] + [part_in[t, k, i] for k in range(3)]
            blocks = [b.astype(F32) for b in blocks]
            two = []
            for j in range(2):
                at = 2 * i + j
                tot = sum(
                    b[8 * j:8 * j + 8] * share[:, at:at + 1] for b, share in zip(blocks, shares)
                )
                two.append(tot)
            att[t, me, 16 * i:16 * i + 16] = jnp.concatenate(two, axis=0).astype(BF16)
        block = att.at[t, me]
        c = remote(block, block, ag_s.at[t, 3], ag_r.at[t, 3], sibling)
        c.start()
        ag_near.append(c)
        group = [remote(block, block, ag_s.at[t, i], ag_r.at[t, i], far[i]) for i in range(3)]
        for c in group:
            c.start()
        ag_far.append(group)

    half_cols = w_v.shape[1] // 2

    def products(first_unit, sources):
        left = jnp.concatenate(
            [
                jnp.concatenate(
                    [att[t, 2 * f + c, h * lines:(h + 1) * lines] for h in range(heads)], axis=1
                )
                for t, f in sources for c in range(2)
            ],
            axis=0,
        )
        out = dot_nn(left, w_v[...])
        for k in range(heads):
            prod_f[k, 0:2 * lines * len(sources), :] = out[:, 128 * k:128 * (k + 1)]
        for i in range(len(sources)):
            for m in range(nmp):
                value = jnp.concatenate(
                    [
                        prod_f[k, pl.ds(2 * lines * i + m, 8, stride=8), :]
                        for k in range(heads)
                    ],
                    axis=1,
                )
                prod[m, first_unit + i] = jnp.concatenate(
                    [value[:, :half_cols], value[:, half_cols:]], axis=0
                ).astype(BF16)

    mp_copies = []

    def send_products(stage, first_unit, units):
        sl = pl.ds(first_unit, units)
        for k in range(1, nmp):
            c = remote(
                prod.at[lax.rem(mp + k, nmp), sl], prod_in.at[k - 1, sl],
                mp_s.at[stage, k - 1], mp_r.at[stage, k - 1], mp_dev(k),
            )
            c.start()
            mp_copies.append(c)

    def forward_rows(turn):
        copies = []
        for i, f in enumerate(from_chip):
            ag_far[turn][i].wait()
            block = att.at[order[turn], 2 * f + core]
            c = remote(block, block, fw_s.at[turn, i], fw_r.at[turn, i], sibling)
            c.start()
            copies.append(c)
        return copies

    finish(order[0])
    load_w.wait()
    ag_near[0].wait()
    products(0, [(order[0], chip)])
    send_products(0, 0, 1)
    finish(order[1])

    for i in range(3):
        kv_far[i].wait()
        kv_near[i + 1].start()

    ag_near[1].wait()
    products(1, [(order[1], chip)])
    send_products(1, 1, 1)
    for c in kv_near:
        c.wait()

    q_copy.wait()
    s0 = []
    for b in range(BLOCKS):
        scores = dot_nt(q0[...], prompt_keys(b))
        s0.append(jnp.where(iota(scores.shape, 1) + b * n < ctx_s[0], scores, NEG))
    m = functools.reduce(jnp.maximum, [jnp.max(x, axis=1, keepdims=True) for x in s0])
    p0 = [jnp.exp2((x - m) * SCALE) for x in s0]
    l = sum(jnp.sum(p, axis=1, keepdims=True) for p in p0)
    r0_out[0:hs, :] = sum(dot_nn(p.astype(BF16), prompt_values(b)) for b, p in enumerate(p0))
    r0_out[hs:2 * hs, :] = jnp.where(lane == 0, m, l)
    r0_copy = remote(r0_out, r0_in, z_s.at[2], z_r.at[2], partner)
    r0_copy.start()

    load_pq.wait()
    prompt_pieces(0, 0, 1)
    forward = forward_rows(0)
    prompt_pieces(0, 1, 2)
    for c in forward:
        c.wait()
    products(2, [(order[0], f) for f in from_chip])
    send_products(2, 2, 3)
    forward = forward_rows(1)
    prompt_pieces(0, 2, 3)
    for c in forward:
        c.wait()
    products(5, [(order[1], f) for f in from_chip])
    send_products(3, 5, 3)
    prompt_pieces(0, 3, pairs)
    prompt_pieces(1, 0, 1)

    r0_copy.wait()
    prompt_m, prompt_l = r0_in[hs:2 * hs, 0:1], r0_in[hs:2 * hs, 1:2]
    peak = jnp.maximum(row0_m, prompt_m)
    keep = jnp.exp2((row0_m - peak) * SCALE)
    more = jnp.exp2((prompt_m - peak) * SCALE)
    row0 = (row0_acc * keep + r0_in[0:hs, :] * more) / (row0_l * keep + prompt_l * more)
    row0 = jnp.concatenate([row0[h * steps:(h + 1) * steps] for h in range(heads)], axis=1)
    row0 = jnp.concatenate([row0, jnp.zeros((16 - steps, row0.shape[1]), F32)], axis=0)
    row0 = dot_nn(row0.astype(BF16), w_v[...])[0:8]
    row0 = jnp.concatenate([row0[:, :half_cols], row0[:, half_cols:]], axis=0)
    r0_mix[...] = row0.astype(BF16)

    def row0_copy(k):
        return remote(r0_mix, r0_mix_in.at[k - 1], r0_s.at[k - 1], r0_r.at[k - 1], {"mp": 0})

    for k in range(1, nmp):
        @pl.when(mp == k)
        def _(k=k):
            row0_copy(k).start()

    prompt_pieces(1, 1, pairs)
    pre_copy = pltpu.make_async_copy(pre_v, pre_h, out_sem)
    pre_copy.start()

    for k in range(1, nmp):
        @pl.when(mp == k)
        def _(k=k):
            row0_copy(k).wait_send()
            r0_mix_in[...] = jnp.zeros(r0_mix_in.shape, BF16)

    @pl.when(mp == 0)
    def _():
        for k in range(1, nmp):
            row0_copy(k).wait_recv()

    for k in range(nmp - 1):
        row0 = row0 + r0_mix_in[k].astype(F32)

    units = [(t, chip) for t in order]
    units = units + [(t, f) for t in order for f in from_chip]
    for stage, (lo, hi) in enumerate(((0, 1), (1, 2), (2, 5), (5, 8))):
        for c in mp_copies[stage * (nmp - 1):(stage + 1) * (nmp - 1)]:
            c.wait()
        for unit in range(lo, hi):
            t, source = units[unit]
            value = prod[mp, unit].astype(F32)
            for k in range(nmp - 1):
                value = value + prod_in[k, unit].astype(F32)
            if t == 0:
                here = (mp == 0) & (source == 0) & (iota(value.shape, 0) % 8 < steps)
                value = jnp.where(here, row0, value)
            for c in range(2):
                for k in range(heads):
                    at = (2 * c + t) * hs + k * steps
                    row = k // (heads // 2) * 8 + c * steps
                    col = k % (heads // 2) * 128
                    mix_v[source, at:at + steps] = value[row:row + steps, col:col + 128]
    mix_o[...] = mix_v[...].reshape(mix_o.shape).astype(BF16)
    pre_copy.wait()


def hand_over(pre_i, mix_i, pre_o, mix_o, sems):
    copies = [
        pltpu.make_async_copy(pre_i, pre_o, sems.at[0]),
        pltpu.make_async_copy(mix_i, mix_o, sems.at[1]),
    ]
    for c in copies:
        c.start()
    for c in copies:
        c.wait()


def body(
    prompt_queries, prompt_pairs, decode_queries, decode_pairs, cache_pool, out_weight,
    slot_pages, placement, context_len,
):
    nsec, nseq, nmp = (lax.axis_size(a) for a in ("section", "seq", "mp"))
    _, blocks, btok, qwidth = prompt_queries.shape
    _, rows, steps, _ = decode_queries.shape
    slots = cache_pool.shape[1]
    width = out_weight.shape[2]
    heads = qwidth // HEAD
    hs = heads * steps
    own = rows // nseq
    pq = prompt_queries[0]
    pp = prompt_pairs.reshape(blocks * btok * 2, HEAD)
    dq = decode_queries.reshape(rows, steps, heads, HEAD).transpose(0, 2, 1, 3).reshape(rows, hs, HEAD)
    dp = decode_pairs.reshape(rows * steps * 2, HEAD)
    pool = cache_pool.reshape(slots * PAGE * 2, HEAD)
    w = out_weight[0]
    count = slots + own
    any_spec = pl.BlockSpec(memory_space=pl.ANY)
    smem_spec = pl.BlockSpec(memory_space=pltpu.SMEM)
    dma = pltpu.SemaphoreType.DMA
    prefill, mixed = pl.pallas_call(
        functools.partial(kernel, nsec, nseq, nmp, slots, rows, heads, steps),
        out_shape=(
            jax.ShapeDtypeStruct(pq.shape, BF16),
            jax.ShapeDtypeStruct((own * hs, HEAD), BF16),
        ),
        in_specs=[any_spec] * 6 + [smem_spec] * 2,
        out_specs=(any_spec, pl.BlockSpec(memory_space=pltpu.VMEM)),
        scratch_shapes=[
            pltpu.VMEM(pq.shape, BF16),
            pltpu.VMEM(pp.shape, BF16),
            pltpu.VMEM(dq.shape, BF16),
            pltpu.VMEM(dp.shape, BF16),
            pltpu.VMEM(pool.shape, BF16),
            pltpu.VMEM(w.shape, BF16),
            pltpu.VMEM((nseq,) + pp.shape, BF16),
            pltpu.VMEM((hs, HEAD), BF16),
            pltpu.VMEM((2 * hs, HEAD), F32),
            pltpu.VMEM((2 * hs, HEAD), F32),
            pltpu.VMEM((16, width // 2), BF16),
            pltpu.VMEM((nmp - 1, 16, width // 2), BF16),
            pltpu.VMEM((hs, 128), F32),
            pltpu.VMEM((hs, 128), F32),
            pltpu.VMEM((128, 128), F32),
            pltpu.VMEM((3, own, 128), F32),
            pltpu.VMEM((count * hs, HEAD), F32),
            pltpu.VMEM((2, 2, nseq // 2, hs // 2, own, HEAD), BF16),
            pltpu.VMEM((2, nseq // 2, hs // 2, own, HEAD), BF16),
            pltpu.VMEM((2, 3, hs // 2, own, HEAD), BF16),
            pltpu.VMEM((2, nseq, own * hs // 2, HEAD), BF16),
            pltpu.VMEM((width // 128, 48 * steps, 128), F32),
            pltpu.VMEM((nmp, 8, 16, width // 2), BF16),
            pltpu.VMEM((nmp - 1, 8, 16, width // 2), BF16),
            pltpu.VMEM((4, 4 * hs, HEAD), F32),
            pltpu.VMEM(pq.shape, BF16),
            dma((16,)),
            dma,
            dma((7,)), dma((7,)),
            dma((3,)), dma((3,)),
            dma((nmp - 1,)), dma((nmp - 1,)),
            dma((2,)), dma((2,)),
            dma((2, 3)), dma((2, 3)),
            dma((3,)), dma((3,)),
            dma((2, 4)), dma((2, 4)),
            dma((2, 3)), dma((2, 3)),
            dma((4, nmp - 1)), dma((4, nmp - 1)),
        ],
        compiler_params=pltpu.CompilerParams(
            collective_id=0, has_side_effects=True, vmem_limit_bytes=56 * 1024 * 1024
        ),
    )(pq, pp, dq, dp, pool, w, slot_pages, context_len)
    prefill, mixed = pl.pallas_call(
        hand_over,
        out_shape=(
            jax.ShapeDtypeStruct(prefill.shape, BF16), jax.ShapeDtypeStruct(mixed.shape, BF16)
        ),
        in_specs=[pl.BlockSpec(memory_space=pltpu.VMEM)] * 2,
        out_specs=(any_spec,) * 2,
        scratch_shapes=[dma((2,))],
    )(prefill, mixed)
    mixed = mixed.reshape(own, width // HEAD, steps, HEAD).transpose(0, 2, 1, 3)
    mixed = mixed.reshape(own, steps, width)
    return prefill[None], mixed[None]


def solution(mesh):
    return jax.shard_map(
        body,
        mesh=mesh,
        in_specs=(
            P("section", None, "seq", "mp"),
            P("section", None, "seq", None, "mp"),
            P("section", None, None, "mp"),
            P("section", None, None, None, "mp"),
            P("section", "seq", None, None, "mp"),
            P("section", "mp", "seq"),
            P("seq"),
            P(),
            P(),
        ),
        out_specs=(P("section", None, "seq", "mp"), P("section", "mp", None, "seq")),
        check_vma=False,
    )
```

```python
import functools
import math

import jax
import jax.numpy as jnp
from jax import lax
from jax.experimental import pallas as pl
from jax.experimental.pallas import tpu as pltpu
from jax.sharding import PartitionSpec as P

HEAD = 128
PAGE = 128
MAXP = 1024
BLOCKS = 2
NEG = -1e30
F32 = jnp.float32
BF16 = jnp.bfloat16
MESH = pl.DeviceIdType.MESH
SCALE = 1.0 / (math.sqrt(HEAD) * math.log(2.0))


def dot_nt(a, b):
    return lax.dot_general(a, b, (((1,), (1,)), ((), ())), preferred_element_type=F32)


def dot_nn(a, b, precision=None):
    return lax.dot_general(
        a, b, (((1,), (0,)), ((), ())), preferred_element_type=F32, precision=precision
    )


def iota(shape, dim):
    return lax.broadcasted_iota(jnp.int32, shape, dim)


def kernel(
    nsec, nseq, nmp, slots, rows, heads, steps,
    pq_h, pp_h, dq_h, dp_h, pool_h, w_h, slot_s, ctx_s,
    pre_h, mix_o,
    pq_v, pp_v, dq_v, dp_v, pool_v, w_v, kv, q0, r0_out, r0_in, r0_mix, r0_mix_in,
    lse_out, lse_in, lse_t, lse_t_in,
    accs, part, sib_in, part_in, att, prod_f, prod, prod_in, mix_v, pre_v,
    in_sem, out_sem, kv_s, kv_r, z_s, z_r, r0_s, r0_r, sib_s, sib_r, rs_s, rs_r, st_s, st_r, ag_s, ag_r, fw_s, fw_r, mp_s, mp_r,
):
    hs = heads * steps
    half = hs // 2
    own = rows // nseq
    chips = nseq // 2
    me = lax.axis_index("seq")
    mp = lax.axis_index("mp")
    sec = lax.axis_index("section")
    chip, core = me // 2, me % 2
    partner = {"section": lax.rem(sec + nsec // 2, nsec)}
    sibling = {"seq": 2 * chip + 1 - core}
    away = (1, 3, 2)
    far_chip = [lax.rem(chip + k, 4) for k in away]
    far = [{"seq": 2 * c + core} for c in far_chip]
    from_chip = [lax.rem(chip + 4 - k, 4) for k in away]

    def mp_dev(k):
        return {"mp": lax.rem(mp + k, nmp)}

    def remote(src, dst, send, recv, device):
        return pltpu.make_async_remote_copy(
            src_ref=src, dst_ref=dst, send_sem=send, recv_sem=recv,
            device_id=device, device_id_type=MESH,
        )

    barrier = pltpu.get_barrier_semaphore()
    greeted = [partner, *(mp_dev(k) for k in range(1, nmp)), *far, sibling]
    for device in greeted:
        pl.semaphore_signal(barrier, inc=1, device_id=device, device_id_type=MESH)

    width = 12
    groups = slots // width
    group_lines = width * 2 * PAGE

    def pool_load(g):
        sl = slice(g * group_lines, (g + 1) * group_lines)
        return pltpu.make_async_copy(pool_h.at[sl], pool_v.at[sl], in_sem.at[5 + g])

    load_dq = pltpu.make_async_copy(dq_h, dq_v, in_sem.at[0])
    load_dp = pltpu.make_async_copy(dp_h, dp_v, in_sem.at[1])
    load_pp = pltpu.make_async_copy(pp_h, pp_v, in_sem.at[2])
    load_pq = pltpu.make_async_copy(pq_h, pq_v, in_sem.at[3])
    load_w = pltpu.make_async_copy(w_h, w_v, in_sem.at[4])
    load_pool = [pool_load(g) for g in range(groups)]
    for c in [load_dq, *load_pool, load_dp, load_pp, load_pq, load_w]:
        c.start()

    lane = iota((hs, 128), 1)
    lane1 = iota((8, 128), 1)
    key_lane = iota((hs, 2 * PAGE), 1)
    key_id = jnp.where(key_lane % 2 == 0, key_lane // 2, PAGE)

    def place_of(row):
        return (row % 16) // 2 * 16 + row % 2 * 8 + row // 16

    def merge(state, index, place, m, l):
        top, total, slot_top, slot_place = state
        hit = lane == place
        fresh = jnp.where(hit, jnp.maximum(top, m), top)
        total = total * jnp.exp2((top - fresh) * SCALE) + jnp.where(
            hit, l * jnp.exp2((m - fresh) * SCALE), 0.0
        )
        slot_top = jnp.where(lane == index, m, slot_top)
        slot_place = jnp.where(lane1 == index, place, slot_place)
        return fresh, total, slot_top, slot_place

    def slot_group(g, state, width):
        done = []
        for i in range(width):
            j = g * width + i
            entry = slot_s[j]
            live = entry >= 0
            row = jnp.where(live, entry // MAXP, 0)
            count = jnp.where(live, jnp.clip(ctx_s[row] - (entry % MAXP) * PAGE, 0, PAGE), 0)
            page = pool_v[pl.ds(pl.multiple_of(j * 2 * PAGE, 2 * PAGE), 2 * PAGE), :]
            place = jnp.where(live, place_of(row), -1)
            done.append((j, place, count, page, dot_nt(dq_v[row], page)))
        for j, place, count, page, scores in done:
            allowed = key_id < count
            scores = jnp.where(allowed, scores, NEG)
            m = jnp.max(scores, axis=1, keepdims=True)
            p = jnp.where(allowed, jnp.exp2((scores - m) * SCALE), 0.0)
            l = jnp.sum(p, axis=1, keepdims=True)
            acc = dot_nn(pltpu.roll(p, 1, 1).astype(BF16), page)
            accs[pl.ds(pl.multiple_of(j * hs, hs), hs), :] = acc
            state = merge(state, j, place, m, l)
        return state

    state = (
        jnp.full((hs, 128), NEG, F32), jnp.zeros((hs, 128), F32),
        jnp.full((hs, 128), NEG, F32), jnp.full((8, 128), -1, jnp.int32),
    )
    load_dq.wait()
    for g in range(groups):
        load_pool[g].wait()
        state = slot_group(g, state, width)

    load_pp.wait()
    ri = iota((2 * PAGE, 2 * PAGE), 0)
    ci = iota((2 * PAGE, 2 * PAGE), 1)
    pick = jnp.where(ci == jnp.where(ri < PAGE, 2 * ri, 2 * (ri - PAGE) + 1), 1.0, 0.0).astype(BF16)
    for b in range(BLOCKS):
        both = dot_nn(pick, pp_v[b * 2 * PAGE:(b + 1) * 2 * PAGE, :]).astype(BF16)
        kv[me, b * PAGE:(b + 1) * PAGE, :] = both[:PAGE]
        kv[me, (BLOCKS + b) * PAGE:(BLOCKS + b + 1) * PAGE, :] = both[PAGE:]

    load_dp.wait()
    mine = [16 * m + 2 * me for m in range(nmp)]
    line = 2 * steps
    recent = jnp.concatenate(
        [dp_v[pl.ds(pl.multiple_of(r * line, 2 * line), 2 * line), :] for r in mine], axis=0
    )
    rq = jnp.concatenate([dq_v[pl.ds(r, 2)].reshape(2 * hs, HEAD) for r in mine], axis=0)
    scores = dot_nt(rq, recent)
    ri = iota(scores.shape, 0)
    ci = iota(scores.shape, 1)
    allowed = (
        (ci % 2 == 0) & (ci // line == ri // hs) & ((ci % line) // 2 <= ri % steps)
    )
    scores = jnp.where(allowed, scores, NEG)
    m = jnp.max(scores, axis=1, keepdims=True)
    p = jnp.where(allowed, jnp.exp2((scores - m) * SCALE), 0.0)
    l = jnp.sum(p, axis=1, keepdims=True)
    accs[slots * hs:(slots + own) * hs, :] = dot_nn(pltpu.roll(p, 1, 1).astype(BF16), recent)
    for r in range(own):
        state = merge(
            state, slots + r, me * own + r % 2 * 8 + r // 2,
            m[r * hs:(r + 1) * hs], l[r * hs:(r + 1) * hs],
        )
    top, total, slot_top, slot_place = state
    lse_mine = jnp.where(
        total > 0.0, top * SCALE + jnp.log2(jnp.maximum(total, 1e-30)), NEG
    )
    lse_out[...] = lse_mine
    scores = dot_nt(dq_v[0], dp_v[0:2 * line, :])
    ci = iota(scores.shape, 1)
    allowed = (ci % 2 == 0) & (ci < line) & (ci // 2 <= iota(scores.shape, 0) % steps)
    scores = jnp.where(allowed, scores, NEG)
    row0_m = jnp.max(scores, axis=1, keepdims=True)
    p = jnp.where(allowed, jnp.exp2((scores - row0_m) * SCALE), 0.0)
    row0_l = jnp.sum(p, axis=1, keepdims=True)
    p = jnp.concatenate([jnp.zeros((hs, 1), F32), p[:, :2 * line - 1]], axis=1)
    row0_acc = dot_nn(p.astype(BF16), dp_v[0:2 * line, :])

    pl.semaphore_wait(barrier, len(greeted))
    lse_copy = remote(lse_out, lse_in, z_s.at[0], z_r.at[0], sibling)
    lse_copy.start()
    q_copy = remote(dq_v.at[0], q0, z_s.at[1], z_r.at[1], partner)
    q_copy.start()
    kv_far = [remote(kv.at[me], kv.at[me], kv_s.at[i], kv_r.at[i], far[i]) for i in range(3)]
    for c in kv_far:
        c.start()
    kv_near = [remote(kv.at[me], kv.at[me], kv_s.at[3], kv_r.at[3], sibling)] + [
        remote(kv.at[2 * f + core], kv.at[2 * f + core], kv_s.at[4 + i], kv_r.at[4 + i], sibling)
        for i, f in enumerate(from_chip)
    ]
    kv_near[0].start()
    place_pick = jnp.where(
        iota((128, 128), 0) == jnp.broadcast_to(slot_place[0:1], (128, 128)), 1.0, 0.0
    )
    lse_copy.wait()
    peak = jnp.maximum(lse_mine, lse_in[...])
    lse_chip = peak + jnp.log2(jnp.exp2(lse_mine - peak) + jnp.exp2(lse_in[...] - peak))
    whole_slot = dot_nn(lse_chip, place_pick, lax.Precision.HIGHEST)
    factor = jnp.exp2(slot_top * SCALE - whole_slot)
    lse_t[...] = jnp.concatenate([lse_chip, jnp.zeros((128 - hs, 128), F32)], axis=0).T

    count = accs.shape[0] // hs

    def row_sums(j):
        weights = (place_pick * jnp.broadcast_to(factor[j:j + 1], (128, 128)))[:rows, :count]
        return dot_nn(weights.astype(BF16), accs[pl.ds(j, count, stride=hs), :].astype(BF16))

    for i in range(half):
        even, odd = row_sums(2 * i), row_sums(2 * i + 1)
        for s in range(nseq):
            for t in range(2):
                sl = slice(s * own + 8 * t, s * own + 8 * t + 8)
                part[t, s % 2, s // 2, i] = jnp.concatenate([even[sl], odd[sl]], axis=0).astype(BF16)
    order = (1, 0)
    sib_copies = [
        remote(part.at[t, 1 - core], sib_in.at[t], sib_s.at[t], sib_r.at[t], sibling)
        for t in range(2)
    ]
    for t in order:
        sib_copies[t].start()

    st_copies = [
        remote(
            lse_t.at[pl.ds(pl.multiple_of((2 * f + core) * own, own), own)], lse_t_in.at[i],
            st_s.at[i], st_r.at[i], far[i],
        )
        for i, f in enumerate(far_chip)
    ]
    rs_copies = [
        [
            remote(part.at[t, core, f], part_in.at[t, i], rs_s.at[t, i], rs_r.at[t, i], far[i])
            for i, f in enumerate(far_chip)
        ]
        for t in range(2)
    ]
    for t in order:
        sib_copies[t].wait()
        for i, f in enumerate(far_chip + [chip]):
            for at in range(0, half, 4):
                sl = slice(at, at + 4)
                part[t, core, f, sl] = (
                    part[t, core, f, sl].astype(F32) + sib_in[t, f, sl].astype(F32)
                ).astype(BF16)
            if i < 3:
                rs_copies[t][i].start()
        if t == order[0]:
            for c in st_copies:
                c.start()


    n = nseq * PAGE

    def prompt_keys(b):
        return kv[:, b * PAGE:(b + 1) * PAGE, :].reshape(n, HEAD)

    def prompt_values(b):
        return kv[:, (BLOCKS + b) * PAGE:(BLOCKS + b + 1) * PAGE, :].reshape(n, HEAD)

    def prompt_piece(b, pair):
        two = pq_v[b, :, pl.ds(pl.multiple_of(pair * 2 * HEAD, 2 * HEAD), 2 * HEAD)]
        q = jnp.concatenate([two[:, :HEAD], two[:, HEAD:]], axis=0)
        s_own = dot_nt(q, prompt_keys(b))
        limit = me * PAGE + iota((2 * PAGE, n), 0) % PAGE
        s_own = jnp.where(iota((2 * PAGE, n), 1) <= limit, s_own, NEG)
        m = jnp.max(s_own, axis=1, keepdims=True)
        if b:
            s_old = dot_nt(q, prompt_keys(0))
            m = jnp.maximum(m, jnp.max(s_old, axis=1, keepdims=True))
        p = jnp.exp2((s_own - m) * SCALE)
        l = jnp.sum(p, axis=1, keepdims=True)
        o = dot_nn(p.astype(BF16), prompt_values(b))
        if b:
            p = jnp.exp2((s_old - m) * SCALE)
            l = l + jnp.sum(p, axis=1, keepdims=True)
            o = o + dot_nn(p.astype(BF16), prompt_values(0))
        o = (o / l).astype(BF16)
        pre_v[b, :, pl.ds(pl.multiple_of(pair * 2 * HEAD, 2 * HEAD), 2 * HEAD)] = jnp.concatenate(
            [o[:PAGE], o[PAGE:]], axis=1
        )

    def prompt_pieces(b, lo, hi):
        def step(i, carry):
            prompt_piece(b, i)
            return carry

        lax.fori_loop(lo, hi, step, 0)

    pairs = heads // 2

    for c in st_copies:
        c.wait()
    ag_far = []
    ag_near = []
    lines = 8 * steps

    def shares_of(terms):
        peak = functools.reduce(jnp.maximum, terms)
        whole = peak + jnp.log2(sum(jnp.exp2(t - peak) for t in terms))
        return [jnp.exp2(t - whole) for t in terms]

    def finish(t):
        sl = slice(8 * t, 8 * t + 8)
        mine_t = lse_t[pl.ds(pl.multiple_of(me * own + 8 * t, 8), 8), :]
        terms = [mine_t] + [lse_t_in[i, sl] for i in range(3)]
        shares = shares_of(terms)
        for c in rs_copies[t]:
            c.wait()
        for i in range(half):
            blocks = [part[t, core, chip, i]] + [part_in[t, k, i] for k in range(3)]
            blocks = [b.astype(F32) for b in blocks]
            two = []
            for j in range(2):
                at = 2 * i + j
                tot = sum(
                    b[8 * j:8 * j + 8] * share[:, at:at + 1] for b, share in zip(blocks, shares)
                )
                two.append(tot)
            att[t, me, 16 * i:16 * i + 16] = jnp.concatenate(two, axis=0).astype(BF16)
        block = att.at[t, me]
        c = remote(block, block, ag_s.at[t, 3], ag_r.at[t, 3], sibling)
        c.start()
        ag_near.append(c)
        group = [remote(block, block, ag_s.at[t, i], ag_r.at[t, i], far[i]) for i in range(3)]
        for c in group:
            c.start()
        ag_far.append(group)

    half_cols = w_v.shape[1] // 2

    def products(first_unit, sources):
        left = jnp.concatenate(
            [
                jnp.concatenate(
                    [att[t, 2 * f + c, h * lines:(h + 1) * lines] for h in range(heads)], axis=1
                )
                for t, f in sources for c in range(2)
            ],
            axis=0,
        )
        out = dot_nn(left, w_v[...])
        for k in range(heads):
            prod_f[k, 0:2 * lines * len(sources), :] = out[:, 128 * k:128 * (k + 1)]
        for i in range(len(sources)):
            for m in range(nmp):
                value = jnp.concatenate(
                    [
                        prod_f[k, pl.ds(2 * lines * i + m, 8, stride=8), :]
                        for k in range(heads)
                    ],
                    axis=1,
                )
                prod[m, first_unit + i] = jnp.concatenate(
                    [value[:, :half_cols], value[:, half_cols:]], axis=0
                ).astype(BF16)

    mp_copies = []

    def send_products(stage, first_unit, units):
        sl = pl.ds(first_unit, units)
        for k in range(1, nmp):
            c = remote(
                prod.at[lax.rem(mp + k, nmp), sl], prod_in.at[k - 1, sl],
                mp_s.at[stage, k - 1], mp_r.at[stage, k - 1], mp_dev(k),
            )
            c.start()
            mp_copies.append(c)

    def forward_rows(turn):
        copies = []
        for i, f in enumerate(from_chip):
            ag_far[turn][i].wait()
            block = att.at[order[turn], 2 * f + core]
            c = remote(block, block, fw_s.at[turn, i], fw_r.at[turn, i], sibling)
            c.start()
            copies.append(c)
        return copies

    finish(order[0])

    for i in range(3):
        kv_far[i].wait()
        kv_near[i + 1].start()

    load_w.wait()
    ag_near[0].wait()
    products(0, [(order[0], chip)])
    send_products(0, 0, 1)
    for c in kv_near:
        c.wait()

    q_copy.wait()
    s0 = []
    for b in range(BLOCKS):
        scores = dot_nt(q0[...], prompt_keys(b))
        s0.append(jnp.where(iota(scores.shape, 1) + b * n < ctx_s[0], scores, NEG))
    m = functools.reduce(jnp.maximum, [jnp.max(x, axis=1, keepdims=True) for x in s0])
    p0 = [jnp.exp2((x - m) * SCALE) for x in s0]
    l = sum(jnp.sum(p, axis=1, keepdims=True) for p in p0)
    r0_out[0:hs, :] = sum(dot_nn(p.astype(BF16), prompt_values(b)) for b, p in enumerate(p0))
    r0_out[hs:2 * hs, :] = jnp.where(lane == 0, m, l)
    r0_copy = remote(r0_out, r0_in, z_s.at[2], z_r.at[2], partner)
    r0_copy.start()

    finish(order[1])
    load_pq.wait()
    ag_near[1].wait()
    products(1, [(order[1], chip)])
    send_products(1, 1, 1)
    forward = forward_rows(0)
    prompt_pieces(0, 0, 1)
    for c in forward:
        c.wait()
    products(2, [(order[0], f) for f in from_chip])
    send_products(2, 2, 3)
    forward = forward_rows(1)
    for c in forward:
        c.wait()
    products(5, [(order[1], f) for f in from_chip])
    send_products(3, 5, 3)
    prompt_pieces(0, 1, pairs)

    r0_copy.wait()
    prompt_m, prompt_l = r0_in[hs:2 * hs, 0:1], r0_in[hs:2 * hs, 1:2]
    peak = jnp.maximum(row0_m, prompt_m)
    keep = jnp.exp2((row0_m - peak) * SCALE)
    more = jnp.exp2((prompt_m - peak) * SCALE)
    row0 = (row0_acc * keep + r0_in[0:hs, :] * more) / (row0_l * keep + prompt_l * more)
    row0 = jnp.concatenate([row0[h * steps:(h + 1) * steps] for h in range(heads)], axis=1)
    row0 = jnp.concatenate([row0, jnp.zeros((16 - steps, row0.shape[1]), F32)], axis=0)
    row0 = dot_nn(row0.astype(BF16), w_v[...])[0:8]
    row0 = jnp.concatenate([row0[:, :half_cols], row0[:, half_cols:]], axis=0)
    r0_mix[...] = row0.astype(BF16)

    def row0_copy(k):
        return remote(r0_mix, r0_mix_in.at[k - 1], r0_s.at[k - 1], r0_r.at[k - 1], {"mp": 0})

    for k in range(1, nmp):
        @pl.when(mp == k)
        def _(k=k):
            row0_copy(k).start()

    prompt_pieces(1, 0, pairs)
    pre_copy = pltpu.make_async_copy(pre_v, pre_h, out_sem)
    pre_copy.start()

    for k in range(1, nmp):
        @pl.when(mp == k)
        def _(k=k):
            row0_copy(k).wait_send()
            r0_mix_in[...] = jnp.zeros(r0_mix_in.shape, BF16)

    @pl.when(mp == 0)
    def _():
        for k in range(1, nmp):
            row0_copy(k).wait_recv()

    for k in range(nmp - 1):
        row0 = row0 + r0_mix_in[k].astype(F32)

    units = [(t, chip) for t in order]
    units = units + [(t, f) for t in order for f in from_chip]
    for stage, (lo, hi) in enumerate(((0, 1), (1, 2), (2, 5), (5, 8))):
        for c in mp_copies[stage * (nmp - 1):(stage + 1) * (nmp - 1)]:
            c.wait()
        for unit in range(lo, hi):
            t, source = units[unit]
            value = prod[mp, unit].astype(F32)
            for k in range(nmp - 1):
                value = value + prod_in[k, unit].astype(F32)
            if t == 0:
                here = (mp == 0) & (source == 0) & (iota(value.shape, 0) % 8 < steps)
                value = jnp.where(here, row0, value)
            for c in range(2):
                for k in range(heads):
                    at = (2 * c + t) * hs + k * steps
                    row = k // (heads // 2) * 8 + c * steps
                    col = k % (heads // 2) * 128
                    mix_v[source, at:at + steps] = value[row:row + steps, col:col + 128]
    mix_o[...] = mix_v[...].reshape(mix_o.shape).astype(BF16)
    pre_copy.wait()


def hand_over(pre_i, mix_i, pre_o, mix_o, sems):
    copies = [
        pltpu.make_async_copy(pre_i, pre_o, sems.at[0]),
        pltpu.make_async_copy(mix_i, mix_o, sems.at[1]),
    ]
    for c in copies:
        c.start()
    for c in copies:
        c.wait()


def body(
    prompt_queries, prompt_pairs, decode_queries, decode_pairs, cache_pool, out_weight,
    slot_pages, placement, context_len,
):
    nsec, nseq, nmp = (lax.axis_size(a) for a in ("section", "seq", "mp"))
    _, blocks, btok, qwidth = prompt_queries.shape
    _, rows, steps, _ = decode_queries.shape
    slots = cache_pool.shape[1]
    width = out_weight.shape[2]
    heads = qwidth // HEAD
    hs = heads * steps
    own = rows // nseq
    pq = prompt_queries[0]
    pp = prompt_pairs.reshape(blocks * btok * 2, HEAD)
    dq = decode_queries.reshape(rows, steps, heads, HEAD).transpose(0, 2, 1, 3).reshape(rows, hs, HEAD)
    dp = decode_pairs.reshape(rows * steps * 2, HEAD)
    pool = cache_pool.reshape(slots * PAGE * 2, HEAD)
    w = out_weight[0]
    count = slots + own
    any_spec = pl.BlockSpec(memory_space=pl.ANY)
    smem_spec = pl.BlockSpec(memory_space=pltpu.SMEM)
    dma = pltpu.SemaphoreType.DMA
    prefill, mixed = pl.pallas_call(
        functools.partial(kernel, nsec, nseq, nmp, slots, rows, heads, steps),
        out_shape=(
            jax.ShapeDtypeStruct(pq.shape, BF16),
            jax.ShapeDtypeStruct((own * hs, HEAD), BF16),
        ),
        in_specs=[any_spec] * 6 + [smem_spec] * 2,
        out_specs=(any_spec, pl.BlockSpec(memory_space=pltpu.VMEM)),
        scratch_shapes=[
            pltpu.VMEM(pq.shape, BF16),
            pltpu.VMEM(pp.shape, BF16),
            pltpu.VMEM(dq.shape, BF16),
            pltpu.VMEM(dp.shape, BF16),
            pltpu.VMEM(pool.shape, BF16),
            pltpu.VMEM(w.shape, BF16),
            pltpu.VMEM((nseq,) + pp.shape, BF16),
            pltpu.VMEM((hs, HEAD), BF16),
            pltpu.VMEM((2 * hs, HEAD), F32),
            pltpu.VMEM((2 * hs, HEAD), F32),
            pltpu.VMEM((16, width // 2), BF16),
            pltpu.VMEM((nmp - 1, 16, width // 2), BF16),
            pltpu.VMEM((hs, 128), F32),
            pltpu.VMEM((hs, 128), F32),
            pltpu.VMEM((128, 128), F32),
            pltpu.VMEM((3, own, 128), F32),
            pltpu.VMEM((count * hs, HEAD), F32),
            pltpu.VMEM((2, 2, nseq // 2, hs // 2, own, HEAD), BF16),
            pltpu.VMEM((2, nseq // 2, hs // 2, own, HEAD), BF16),
            pltpu.VMEM((2, 3, hs // 2, own, HEAD), BF16),
            pltpu.VMEM((2, nseq, own * hs // 2, HEAD), BF16),
            pltpu.VMEM((width // 128, 48 * steps, 128), F32),
            pltpu.VMEM((nmp, 8, 16, width // 2), BF16),
            pltpu.VMEM((nmp - 1, 8, 16, width // 2), BF16),
            pltpu.VMEM((4, 4 * hs, HEAD), F32),
            pltpu.VMEM(pq.shape, BF16),
            dma((16,)),
            dma,
            dma((7,)), dma((7,)),
            dma((3,)), dma((3,)),
            dma((nmp - 1,)), dma((nmp - 1,)),
            dma((2,)), dma((2,)),
            dma((2, 3)), dma((2, 3)),
            dma((3,)), dma((3,)),
            dma((2, 4)), dma((2, 4)),
            dma((2, 3)), dma((2, 3)),
            dma((4, nmp - 1)), dma((4, nmp - 1)),
        ],
        compiler_params=pltpu.CompilerParams(
            collective_id=0, has_side_effects=True, vmem_limit_bytes=56 * 1024 * 1024
        ),
    )(pq, pp, dq, dp, pool, w, slot_pages, context_len)
    prefill, mixed = pl.pallas_call(
        hand_over,
        out_shape=(
            jax.ShapeDtypeStruct(prefill.shape, BF16), jax.ShapeDtypeStruct(mixed.shape, BF16)
        ),
        in_specs=[pl.BlockSpec(memory_space=pltpu.VMEM)] * 2,
        out_specs=(any_spec,) * 2,
        scratch_shapes=[dma((2,))],
    )(prefill, mixed)
    mixed = mixed.reshape(own, width // HEAD, steps, HEAD).transpose(0, 2, 1, 3)
    mixed = mixed.reshape(own, steps, width)
    return prefill[None], mixed[None]


def solution(mesh):
    return jax.shard_map(
        body,
        mesh=mesh,
        in_specs=(
            P("section", None, "seq", "mp"),
            P("section", None, "seq", None, "mp"),
            P("section", None, None, "mp"),
            P("section", None, None, None, "mp"),
            P("section", "seq", None, None, "mp"),
            P("section", "mp", "seq"),
            P("seq"),
            P(),
            P(),
        ),
        out_specs=(P("section", None, "seq", "mp"), P("section", "mp", None, "seq")),
        check_vma=False,
    )
```

```python
import functools
import math

import jax
import jax.numpy as jnp
from jax import lax
from jax.experimental import pallas as pl
from jax.experimental.pallas import tpu as pltpu
from jax.sharding import PartitionSpec as P

HEAD = 128
PAGE = 128
MAXP = 1024
BLOCKS = 2
NEG = -1e30
F32 = jnp.float32
BF16 = jnp.bfloat16
MESH = pl.DeviceIdType.MESH
SCALE = 1.0 / (math.sqrt(HEAD) * math.log(2.0))


def dot_nt(a, b):
    return lax.dot_general(a, b, (((1,), (1,)), ((), ())), preferred_element_type=F32)


def dot_nn(a, b, precision=None):
    return lax.dot_general(
        a, b, (((1,), (0,)), ((), ())), preferred_element_type=F32, precision=precision
    )


def iota(shape, dim):
    return lax.broadcasted_iota(jnp.int32, shape, dim)


def kernel(
    nsec, nseq, nmp, slots, rows, heads, steps,
    pq_h, pp_h, dq_h, dp_h, pool_h, w_h, slot_s, ctx_s,
    pre_h, mix_o,
    pq_v, pp_v, dq_v, dp_v, pool_v, w_v, kv, q0, r0_out, r0_in, r0_mix, r0_mix_in,
    lse_out, lse_in, lse_t, lse_t_in,
    accs, part, sib_in, part_in, att, prod_f, prod, prod_in, mix_v, pre_v,
    in_sem, out_sem, kv_s, kv_r, z_s, z_r, r0_s, r0_r, sib_s, sib_r, rs_s, rs_r, st_s, st_r, ag_s, ag_r, fw_s, fw_r, mp_s, mp_r,
):
    hs = heads * steps
    half = hs // 2
    own = rows // nseq
    chips = nseq // 2
    me = lax.axis_index("seq")
    mp = lax.axis_index("mp")
    sec = lax.axis_index("section")
    chip, core = me // 2, me % 2
    partner = {"section": lax.rem(sec + nsec // 2, nsec)}
    sibling = {"seq": 2 * chip + 1 - core}
    away = (1, 3, 2)
    far_chip = [lax.rem(chip + k, 4) for k in away]
    far = [{"seq": 2 * c + core} for c in far_chip]
    from_chip = [lax.rem(chip + 4 - k, 4) for k in away]

    def mp_dev(k):
        return {"mp": lax.rem(mp + k, nmp)}

    def remote(src, dst, send, recv, device):
        return pltpu.make_async_remote_copy(
            src_ref=src, dst_ref=dst, send_sem=send, recv_sem=recv,
            device_id=device, device_id_type=MESH,
        )

    barrier = pltpu.get_barrier_semaphore()
    greeted = [partner, *(mp_dev(k) for k in range(1, nmp)), *far, sibling]
    for device in greeted:
        pl.semaphore_signal(barrier, inc=1, device_id=device, device_id_type=MESH)

    width = 12
    groups = slots // width
    group_lines = width * 2 * PAGE

    def pool_load(g):
        sl = slice(g * group_lines, (g + 1) * group_lines)
        return pltpu.make_async_copy(pool_h.at[sl], pool_v.at[sl], in_sem.at[5 + g])

    load_dq = pltpu.make_async_copy(dq_h, dq_v, in_sem.at[0])
    load_dp = pltpu.make_async_copy(dp_h, dp_v, in_sem.at[1])
    load_pp = pltpu.make_async_copy(pp_h, pp_v, in_sem.at[2])
    load_pq = pltpu.make_async_copy(pq_h, pq_v, in_sem.at[3])
    load_w = pltpu.make_async_copy(w_h, w_v, in_sem.at[4])
    load_pool = [pool_load(g) for g in range(groups)]
    for c in [load_dq, *load_pool, load_dp, load_pp, load_pq, load_w]:
        c.start()

    lane = iota((hs, 128), 1)
    lane1 = iota((8, 128), 1)
    key_lane = iota((hs, 2 * PAGE), 1)
    key_id = jnp.where(key_lane % 2 == 0, key_lane // 2, PAGE)

    def place_of(row):
        return (row % 16) // 2 * 16 + row % 2 * 8 + row // 16

    def merge(state, index, place, m, l):
        top, total, slot_top, slot_place = state
        hit = lane == place
        fresh = jnp.where(hit, jnp.maximum(top, m), top)
        total = total * jnp.exp2((top - fresh) * SCALE) + jnp.where(
            hit, l * jnp.exp2((m - fresh) * SCALE), 0.0
        )
        slot_top = jnp.where(lane == index, m, slot_top)
        slot_place = jnp.where(lane1 == index, place, slot_place)
        return fresh, total, slot_top, slot_place

    def slot_group(g, state, width):
        done = []
        for i in range(width):
            j = g * width + i
            entry = slot_s[j]
            live = entry >= 0
            row = jnp.where(live, entry // MAXP, 0)
            count = jnp.where(live, jnp.clip(ctx_s[row] - (entry % MAXP) * PAGE, 0, PAGE), 0)
            page = pool_v[pl.ds(pl.multiple_of(j * 2 * PAGE, 2 * PAGE), 2 * PAGE), :]
            place = jnp.where(live, place_of(row), -1)
            done.append((j, place, count, page, dot_nt(dq_v[row], page)))
        for j, place, count, page, scores in done:
            allowed = key_id < count
            scores = jnp.where(allowed, scores, NEG)
            m = jnp.max(scores, axis=1, keepdims=True)
            p = jnp.where(allowed, jnp.exp2((scores - m) * SCALE), 0.0)
            l = jnp.sum(p, axis=1, keepdims=True)
            acc = dot_nn(pltpu.roll(p, 1, 1).astype(BF16), page)
            accs[pl.ds(pl.multiple_of(j * hs, hs), hs), :] = acc
            state = merge(state, j, place, m, l)
        return state

    state = (
        jnp.full((hs, 128), NEG, F32), jnp.zeros((hs, 128), F32),
        jnp.full((hs, 128), NEG, F32), jnp.full((8, 128), -1, jnp.int32),
    )
    load_dq.wait()
    for g in range(groups):
        load_pool[g].wait()
        state = slot_group(g, state, width)

    load_pp.wait()
    ri = iota((2 * PAGE, 2 * PAGE), 0)
    ci = iota((2 * PAGE, 2 * PAGE), 1)
    pick = jnp.where(ci == jnp.where(ri < PAGE, 2 * ri, 2 * (ri - PAGE) + 1), 1.0, 0.0).astype(BF16)
    for b in range(BLOCKS):
        both = dot_nn(pick, pp_v[b * 2 * PAGE:(b + 1) * 2 * PAGE, :]).astype(BF16)
        kv[me, b * PAGE:(b + 1) * PAGE, :] = both[:PAGE]
        kv[me, (BLOCKS + b) * PAGE:(BLOCKS + b + 1) * PAGE, :] = both[PAGE:]

    load_dp.wait()
    mine = [16 * m + 2 * me for m in range(nmp)]
    line = 2 * steps
    recent = jnp.concatenate(
        [dp_v[pl.ds(pl.multiple_of(r * line, 2 * line), 2 * line), :] for r in mine], axis=0
    )
    rq = jnp.concatenate([dq_v[pl.ds(r, 2)].reshape(2 * hs, HEAD) for r in mine], axis=0)
    scores = dot_nt(rq, recent)
    ri = iota(scores.shape, 0)
    ci = iota(scores.shape, 1)
    allowed = (
        (ci % 2 == 0) & (ci // line == ri // hs) & ((ci % line) // 2 <= ri % steps)
    )
    scores = jnp.where(allowed, scores, NEG)
    m = jnp.max(scores, axis=1, keepdims=True)
    p = jnp.where(allowed, jnp.exp2((scores - m) * SCALE), 0.0)
    l = jnp.sum(p, axis=1, keepdims=True)
    accs[slots * hs:(slots + own) * hs, :] = dot_nn(pltpu.roll(p, 1, 1).astype(BF16), recent)
    for r in range(own):
        state = merge(
            state, slots + r, me * own + r % 2 * 8 + r // 2,
            m[r * hs:(r + 1) * hs], l[r * hs:(r + 1) * hs],
        )
    top, total, slot_top, slot_place = state
    lse_mine = jnp.where(
        total > 0.0, top * SCALE + jnp.log2(jnp.maximum(total, 1e-30)), NEG
    )
    lse_out[...] = lse_mine
    pl.semaphore_wait(barrier, len(greeted))
    lse_copy = remote(lse_out, lse_in, z_s.at[0], z_r.at[0], sibling)
    lse_copy.start()
    q_copy = remote(dq_v.at[0], q0, z_s.at[1], z_r.at[1], partner)
    q_copy.start()
    kv_far = [remote(kv.at[me], kv.at[me], kv_s.at[i], kv_r.at[i], far[i]) for i in range(3)]
    for c in kv_far:
        c.start()
    kv_near = [remote(kv.at[me], kv.at[me], kv_s.at[3], kv_r.at[3], sibling)] + [
        remote(kv.at[2 * f + core], kv.at[2 * f + core], kv_s.at[4 + i], kv_r.at[4 + i], sibling)
        for i, f in enumerate(from_chip)
    ]
    kv_near[0].start()
    place_pick = jnp.where(
        iota((128, 128), 0) == jnp.broadcast_to(slot_place[0:1], (128, 128)), 1.0, 0.0
    )
    scores = dot_nt(dq_v[0], dp_v[0:2 * line, :])
    ci = iota(scores.shape, 1)
    allowed = (ci % 2 == 0) & (ci < line) & (ci // 2 <= iota(scores.shape, 0) % steps)
    scores = jnp.where(allowed, scores, NEG)
    row0_m = jnp.max(scores, axis=1, keepdims=True)
    p = jnp.where(allowed, jnp.exp2((scores - row0_m) * SCALE), 0.0)
    row0_l = jnp.sum(p, axis=1, keepdims=True)
    p = jnp.concatenate([jnp.zeros((hs, 1), F32), p[:, :2 * line - 1]], axis=1)
    row0_acc = dot_nn(p.astype(BF16), dp_v[0:2 * line, :])

    lse_copy.wait()
    peak = jnp.maximum(lse_mine, lse_in[...])
    lse_chip = peak + jnp.log2(jnp.exp2(lse_mine - peak) + jnp.exp2(lse_in[...] - peak))
    whole_slot = dot_nn(lse_chip, place_pick, lax.Precision.HIGHEST)
    factor = jnp.exp2(slot_top * SCALE - whole_slot)
    lse_t[...] = jnp.concatenate([lse_chip, jnp.zeros((128 - hs, 128), F32)], axis=0).T

    count = accs.shape[0] // hs

    def row_sums(j):
        weights = (place_pick * jnp.broadcast_to(factor[j:j + 1], (128, 128)))[:rows, :count]
        return dot_nn(weights.astype(BF16), accs[pl.ds(j, count, stride=hs), :].astype(BF16))

    order = (1, 0)
    sib_copies = [[], []]
    for part_no in range(2):
        lo, hi = part_no * half // 2, (part_no + 1) * half // 2
        for i in range(lo, hi):
            even, odd = row_sums(2 * i), row_sums(2 * i + 1)
            for s in range(nseq):
                for t in range(2):
                    sl = slice(s * own + 8 * t, s * own + 8 * t + 8)
                    part[t, s % 2, s // 2, i] = jnp.concatenate(
                        [even[sl], odd[sl]], axis=0
                    ).astype(BF16)
        for t in order:
            c = remote(
                part.at[t, 1 - core, :, lo:hi], sib_in.at[t, :, lo:hi],
                sib_s.at[t, part_no], sib_r.at[t, part_no], sibling,
            )
            c.start()
            sib_copies[t].append(c)

    st_copies = [
        remote(
            lse_t.at[pl.ds(pl.multiple_of((2 * f + core) * own, own), own)], lse_t_in.at[i],
            st_s.at[i], st_r.at[i], far[i],
        )
        for i, f in enumerate(far_chip)
    ]
    rs_copies = [
        [
            remote(part.at[t, core, f], part_in.at[t, i], rs_s.at[t, i], rs_r.at[t, i], far[i])
            for i, f in enumerate(far_chip)
        ]
        for t in range(2)
    ]
    for t in order:
        for c in sib_copies[t]:
            c.wait()
        for i, f in enumerate(far_chip + [chip]):
            for at in range(0, half, 4):
                sl = slice(at, at + 4)
                part[t, core, f, sl] = (
                    part[t, core, f, sl].astype(F32) + sib_in[t, f, sl].astype(F32)
                ).astype(BF16)
            if i < 3:
                rs_copies[t][i].start()
        if t == order[0]:
            for c in st_copies:
                c.start()


    n = nseq * PAGE

    def prompt_keys(b):
        return kv[:, b * PAGE:(b + 1) * PAGE, :].reshape(n, HEAD)

    def prompt_values(b):
        return kv[:, (BLOCKS + b) * PAGE:(BLOCKS + b + 1) * PAGE, :].reshape(n, HEAD)

    def prompt_piece(b, pair):
        two = pq_v[b, :, pl.ds(pl.multiple_of(pair * 2 * HEAD, 2 * HEAD), 2 * HEAD)]
        q = jnp.concatenate([two[:, :HEAD], two[:, HEAD:]], axis=0)
        s_own = dot_nt(q, prompt_keys(b))
        limit = me * PAGE + iota((2 * PAGE, n), 0) % PAGE
        s_own = jnp.where(iota((2 * PAGE, n), 1) <= limit, s_own, NEG)
        m = jnp.max(s_own, axis=1, keepdims=True)
        if b:
            s_old = dot_nt(q, prompt_keys(0))
            m = jnp.maximum(m, jnp.max(s_old, axis=1, keepdims=True))
        p = jnp.exp2((s_own - m) * SCALE)
        l = jnp.sum(p, axis=1, keepdims=True)
        o = dot_nn(p.astype(BF16), prompt_values(b))
        if b:
            p = jnp.exp2((s_old - m) * SCALE)
            l = l + jnp.sum(p, axis=1, keepdims=True)
            o = o + dot_nn(p.astype(BF16), prompt_values(0))
        o = (o / l).astype(BF16)
        pre_v[b, :, pl.ds(pl.multiple_of(pair * 2 * HEAD, 2 * HEAD), 2 * HEAD)] = jnp.concatenate(
            [o[:PAGE], o[PAGE:]], axis=1
        )

    def prompt_pieces(b, lo, hi):
        def step(i, carry):
            prompt_piece(b, i)
            return carry

        lax.fori_loop(lo, hi, step, 0)

    pairs = heads // 2

    for c in st_copies:
        c.wait()
    ag_far = []
    ag_near = []
    lines = 8 * steps

    def shares_of(terms):
        peak = functools.reduce(jnp.maximum, terms)
        whole = peak + jnp.log2(sum(jnp.exp2(t - peak) for t in terms))
        return [jnp.exp2(t - whole) for t in terms]

    def finish(t):
        sl = slice(8 * t, 8 * t + 8)
        mine_t = lse_t[pl.ds(pl.multiple_of(me * own + 8 * t, 8), 8), :]
        terms = [mine_t] + [lse_t_in[i, sl] for i in range(3)]
        shares = shares_of(terms)
        for c in rs_copies[t]:
            c.wait()
        for i in range(half):
            blocks = [part[t, core, chip, i]] + [part_in[t, k, i] for k in range(3)]
            blocks = [b.astype(F32) for b in blocks]
            two = []
            for j in range(2):
                at = 2 * i + j
                tot = sum(
                    b[8 * j:8 * j + 8] * share[:, at:at + 1] for b, share in zip(blocks, shares)
                )
                two.append(tot)
            att[t, me, 16 * i:16 * i + 16] = jnp.concatenate(two, axis=0).astype(BF16)
        block = att.at[t, me]
        c = remote(block, block, ag_s.at[t, 3], ag_r.at[t, 3], sibling)
        c.start()
        ag_near.append(c)
        group = [remote(block, block, ag_s.at[t, i], ag_r.at[t, i], far[i]) for i in range(3)]
        for c in group:
            c.start()
        ag_far.append(group)

    half_cols = w_v.shape[1] // 2

    def products(first_unit, sources):
        left = jnp.concatenate(
            [
                jnp.concatenate(
                    [att[t, 2 * f + c, h * lines:(h + 1) * lines] for h in range(heads)], axis=1
                )
                for t, f in sources for c in range(2)
            ],
            axis=0,
        )
        out = dot_nn(left, w_v[...])
        for k in range(heads):
            prod_f[k, 0:2 * lines * len(sources), :] = out[:, 128 * k:128 * (k + 1)]
        for i in range(len(sources)):
            for m in range(nmp):
                value = jnp.concatenate(
                    [
                        prod_f[k, pl.ds(2 * lines * i + m, 8, stride=8), :]
                        for k in range(heads)
                    ],
                    axis=1,
                )
                prod[m, first_unit + i] = jnp.concatenate(
                    [value[:, :half_cols], value[:, half_cols:]], axis=0
                ).astype(BF16)

    mp_copies = []

    def send_products(stage, first_unit, units):
        sl = pl.ds(first_unit, units)
        for k in range(1, nmp):
            c = remote(
                prod.at[lax.rem(mp + k, nmp), sl], prod_in.at[k - 1, sl],
                mp_s.at[stage, k - 1], mp_r.at[stage, k - 1], mp_dev(k),
            )
            c.start()
            mp_copies.append(c)

    def forward_rows(turn):
        copies = []
        for i, f in enumerate(from_chip):
            ag_far[turn][i].wait()
            block = att.at[order[turn], 2 * f + core]
            c = remote(block, block, fw_s.at[turn, i], fw_r.at[turn, i], sibling)
            c.start()
            copies.append(c)
        return copies

    finish(order[0])

    for i in range(3):
        kv_far[i].wait()
        kv_near[i + 1].start()

    load_w.wait()
    ag_near[0].wait()
    products(0, [(order[0], chip)])
    send_products(0, 0, 1)
    for c in kv_near:
        c.wait()

    q_copy.wait()
    s0 = []
    for b in range(BLOCKS):
        scores = dot_nt(q0[...], prompt_keys(b))
        s0.append(jnp.where(iota(scores.shape, 1) + b * n < ctx_s[0], scores, NEG))
    m = functools.reduce(jnp.maximum, [jnp.max(x, axis=1, keepdims=True) for x in s0])
    p0 = [jnp.exp2((x - m) * SCALE) for x in s0]
    l = sum(jnp.sum(p, axis=1, keepdims=True) for p in p0)
    r0_out[0:hs, :] = sum(dot_nn(p.astype(BF16), prompt_values(b)) for b, p in enumerate(p0))
    r0_out[hs:2 * hs, :] = jnp.where(lane == 0, m, l)
    r0_copy = remote(r0_out, r0_in, z_s.at[2], z_r.at[2], partner)
    r0_copy.start()

    finish(order[1])
    load_pq.wait()
    ag_near[1].wait()
    products(1, [(order[1], chip)])
    send_products(1, 1, 1)
    forward = forward_rows(0)
    prompt_pieces(0, 0, 1)
    for c in forward:
        c.wait()
    products(2, [(order[0], f) for f in from_chip])
    send_products(2, 2, 3)
    forward = forward_rows(1)
    for c in forward:
        c.wait()
    products(5, [(order[1], f) for f in from_chip])
    send_products(3, 5, 3)
    prompt_pieces(0, 1, pairs)

    r0_copy.wait()
    prompt_m, prompt_l = r0_in[hs:2 * hs, 0:1], r0_in[hs:2 * hs, 1:2]
    peak = jnp.maximum(row0_m, prompt_m)
    keep = jnp.exp2((row0_m - peak) * SCALE)
    more = jnp.exp2((prompt_m - peak) * SCALE)
    row0 = (row0_acc * keep + r0_in[0:hs, :] * more) / (row0_l * keep + prompt_l * more)
    row0 = jnp.concatenate([row0[h * steps:(h + 1) * steps] for h in range(heads)], axis=1)
    row0 = jnp.concatenate([row0, jnp.zeros((16 - steps, row0.shape[1]), F32)], axis=0)
    row0 = dot_nn(row0.astype(BF16), w_v[...])[0:8]
    row0 = jnp.concatenate([row0[:, :half_cols], row0[:, half_cols:]], axis=0)
    r0_mix[...] = row0.astype(BF16)

    def row0_copy(k):
        return remote(r0_mix, r0_mix_in.at[k - 1], r0_s.at[k - 1], r0_r.at[k - 1], {"mp": 0})

    for k in range(1, nmp):
        @pl.when(mp == k)
        def _(k=k):
            row0_copy(k).start()

    prompt_pieces(1, 0, pairs)
    pre_copy = pltpu.make_async_copy(pre_v, pre_h, out_sem)
    pre_copy.start()

    for k in range(1, nmp):
        @pl.when(mp == k)
        def _(k=k):
            row0_copy(k).wait_send()
            r0_mix_in[...] = jnp.zeros(r0_mix_in.shape, BF16)

    @pl.when(mp == 0)
    def _():
        for k in range(1, nmp):
            row0_copy(k).wait_recv()

    for k in range(nmp - 1):
        row0 = row0 + r0_mix_in[k].astype(F32)

    units = [(t, chip) for t in order]
    units = units + [(t, f) for t in order for f in from_chip]
    for stage, (lo, hi) in enumerate(((0, 1), (1, 2), (2, 5), (5, 8))):
        for c in mp_copies[stage * (nmp - 1):(stage + 1) * (nmp - 1)]:
            c.wait()
        for unit in range(lo, hi):
            t, source = units[unit]
            value = prod[mp, unit].astype(F32)
            for k in range(nmp - 1):
                value = value + prod_in[k, unit].astype(F32)
            if t == 0:
                here = (mp == 0) & (source == 0) & (iota(value.shape, 0) % 8 < steps)
                value = jnp.where(here, row0, value)
            for c in range(2):
                for k in range(heads):
                    at = (2 * c + t) * hs + k * steps
                    row = k // (heads // 2) * 8 + c * steps
                    col = k % (heads // 2) * 128
                    mix_v[source, at:at + steps] = value[row:row + steps, col:col + 128]
    mix_o[...] = mix_v[...].reshape(mix_o.shape).astype(BF16)
    pre_copy.wait()


def hand_over(pre_i, mix_i, pre_o, mix_o, sems):
    copies = [
        pltpu.make_async_copy(pre_i, pre_o, sems.at[0]),
        pltpu.make_async_copy(mix_i, mix_o, sems.at[1]),
    ]
    for c in copies:
        c.start()
    for c in copies:
        c.wait()


def body(
    prompt_queries, prompt_pairs, decode_queries, decode_pairs, cache_pool, out_weight,
    slot_pages, placement, context_len,
):
    nsec, nseq, nmp = (lax.axis_size(a) for a in ("section", "seq", "mp"))
    _, blocks, btok, qwidth = prompt_queries.shape
    _, rows, steps, _ = decode_queries.shape
    slots = cache_pool.shape[1]
    width = out_weight.shape[2]
    heads = qwidth // HEAD
    hs = heads * steps
    own = rows // nseq
    pq = prompt_queries[0]
    pp = prompt_pairs.reshape(blocks * btok * 2, HEAD)
    dq = decode_queries.reshape(rows, steps, heads, HEAD).transpose(0, 2, 1, 3).reshape(rows, hs, HEAD)
    dp = decode_pairs.reshape(rows * steps * 2, HEAD)
    pool = cache_pool.reshape(slots * PAGE * 2, HEAD)
    w = out_weight[0]
    count = slots + own
    any_spec = pl.BlockSpec(memory_space=pl.ANY)
    smem_spec = pl.BlockSpec(memory_space=pltpu.SMEM)
    dma = pltpu.SemaphoreType.DMA
    prefill, mixed = pl.pallas_call(
        functools.partial(kernel, nsec, nseq, nmp, slots, rows, heads, steps),
        out_shape=(
            jax.ShapeDtypeStruct(pq.shape, BF16),
            jax.ShapeDtypeStruct((own * hs, HEAD), BF16),
        ),
        in_specs=[any_spec] * 6 + [smem_spec] * 2,
        out_specs=(any_spec, pl.BlockSpec(memory_space=pltpu.VMEM)),
        scratch_shapes=[
            pltpu.VMEM(pq.shape, BF16),
            pltpu.VMEM(pp.shape, BF16),
            pltpu.VMEM(dq.shape, BF16),
            pltpu.VMEM(dp.shape, BF16),
            pltpu.VMEM(pool.shape, BF16),
            pltpu.VMEM(w.shape, BF16),
            pltpu.VMEM((nseq,) + pp.shape, BF16),
            pltpu.VMEM((hs, HEAD), BF16),
            pltpu.VMEM((2 * hs, HEAD), F32),
            pltpu.VMEM((2 * hs, HEAD), F32),
            pltpu.VMEM((16, width // 2), BF16),
            pltpu.VMEM((nmp - 1, 16, width // 2), BF16),
            pltpu.VMEM((hs, 128), F32),
            pltpu.VMEM((hs, 128), F32),
            pltpu.VMEM((128, 128), F32),
            pltpu.VMEM((3, own, 128), F32),
            pltpu.VMEM((count * hs, HEAD), F32),
            pltpu.VMEM((2, 2, nseq // 2, hs // 2, own, HEAD), BF16),
            pltpu.VMEM((2, nseq // 2, hs // 2, own, HEAD), BF16),
            pltpu.VMEM((2, 3, hs // 2, own, HEAD), BF16),
            pltpu.VMEM((2, nseq, own * hs // 2, HEAD), BF16),
            pltpu.VMEM((width // 128, 48 * steps, 128), F32),
            pltpu.VMEM((nmp, 8, 16, width // 2), BF16),
            pltpu.VMEM((nmp - 1, 8, 16, width // 2), BF16),
            pltpu.VMEM((4, 4 * hs, HEAD), F32),
            pltpu.VMEM(pq.shape, BF16),
            dma((16,)),
            dma,
            dma((7,)), dma((7,)),
            dma((3,)), dma((3,)),
            dma((nmp - 1,)), dma((nmp - 1,)),
            dma((2, 2)), dma((2, 2)),
            dma((2, 3)), dma((2, 3)),
            dma((3,)), dma((3,)),
            dma((2, 4)), dma((2, 4)),
            dma((2, 3)), dma((2, 3)),
            dma((4, nmp - 1)), dma((4, nmp - 1)),
        ],
        compiler_params=pltpu.CompilerParams(
            collective_id=0, has_side_effects=True, vmem_limit_bytes=56 * 1024 * 1024
        ),
    )(pq, pp, dq, dp, pool, w, slot_pages, context_len)
    prefill, mixed = pl.pallas_call(
        hand_over,
        out_shape=(
            jax.ShapeDtypeStruct(prefill.shape, BF16), jax.ShapeDtypeStruct(mixed.shape, BF16)
        ),
        in_specs=[pl.BlockSpec(memory_space=pltpu.VMEM)] * 2,
        out_specs=(any_spec,) * 2,
        scratch_shapes=[dma((2,))],
    )(prefill, mixed)
    mixed = mixed.reshape(own, width // HEAD, steps, HEAD).transpose(0, 2, 1, 3)
    mixed = mixed.reshape(own, steps, width)
    return prefill[None], mixed[None]


def solution(mesh):
    return jax.shard_map(
        body,
        mesh=mesh,
        in_specs=(
            P("section", None, "seq", "mp"),
            P("section", None, "seq", None, "mp"),
            P("section", None, None, "mp"),
            P("section", None, None, None, "mp"),
            P("section", "seq", None, None, "mp"),
            P("section", "mp", "seq"),
            P("seq"),
            P(),
            P(),
        ),
        out_specs=(P("section", None, "seq", "mp"), P("section", "mp", None, "seq")),
        check_vma=False,
    )
```
